32 devices in a mesh: groups: 2 (over x), ind: 16 (over z, y, core).
Axes of the slice: x: 2, y: 2, z: 4, core: 2. Of those that a mesh axis runs over, the one named last changes fastest.
Arguments:
- genotype: bfloat16 [12288, 16384], P(('groups', 'ind')), parts along dimension 0, may hold values from -4 to 4
- residual: bfloat16 [12288, 256], P(('groups', 'ind')), parts along dimension 0, may hold values from -4 to 4
- labels: int32 [12288, 256], P(('groups', 'ind')), parts along dimension 0, may hold values 0 or 1
- incl_old: float32 [32768, 256], P(('groups', 'ind')), parts along dimension 0, may hold values from 0.02 to 0.98
- mean_old: float32 [32768, 256], P(('groups', 'ind')), parts along dimension 0, may hold values from -0.078125 to 0.078125
- prior_logit: float32 [256], replicated, may hold values from -4 to 0
- slab_scale: float32 [256], replicated, may hold values from 0.25 to 8
- offset: float32 [256], replicated, may hold values from -2 to 1
Outputs:
- incl_new: float32 [32768, 256], P(('groups', 'ind')), parts along dimension 0
- mean_new: float32 [32768, 256], P(('groups', 'ind')), parts along dimension 0
- resid_new: float32 [12288, 256], P(('groups', 'ind')), parts along dimension 0
The draws below stay inside these ranges and needn't reach their ends.
There are 2 independent parts, one for each index of `groups`. The reference program is written for one: setup_inputs(seed, part) draws one part's arguments, and reference() takes and returns one part's arrays. A program takes and returns all parts, laid end to end along the dimension named above; an argument that names none is the same for every part. Nothing has to cross between parts.
All inputs are finite; a program needn't handle non-finite values. No bound on the sum of `labels` on one device may be relied on, other than what follows from the above.
Results may differ from the reference program's by a relative error of at most 0.00062.
Values may be sent and summed in bfloat16 or wider, within the bound.
No kernel may reach another device: no remote copies, remote signals or barrier semaphores. Data moves between devices by JAX's collectives and lax.ppermute only.
A program may use at most 128 MiB of HBM per device.

```python
import math
import jax
import jax.numpy as jnp

NVAR = 16384
COLS = 256
NIND = 6144


def with_ends(entries, own_key, least, top_value):
    shape = entries.shape
    index_at = [jax.random.randint(jax.random.fold_in(own_key, axis), (), 0, shape[axis]) for axis in range(len(shape))]
    entries = entries.at[tuple(index_at)].set(least)
    longest = shape.index(max(shape))
    index_at[longest] = (index_at[longest] + 1) % shape[longest]
    return entries.at[tuple(index_at)].set(top_value)


def spiked(result, own_key, source, target, blocks, factor):
    def block_of(axis_at):
        return (jnp.arange(result.shape[axis_at]) // (result.shape[axis_at] // blocks)).reshape((-1,) + (1,) * (result.ndim - 1 - axis_at))

    one_side = jax.random.permutation(own_key, blocks)[block_of(target)]
    other_side = (block_of(target) + blocks // 2) % blocks
    return jnp.where((block_of(source) == one_side) | (block_of(source) == other_side), factor * result, result)


def shard_levels(key, dims, cuts, low, largest):
    level, own = 1.0, jax.random.fold_in(key, 6)
    for axis_at, shards_of in cuts:
        draws = jnp.exp(jax.random.uniform(jax.random.fold_in(own, axis_at), (shards_of,), jnp.float32, low / len(cuts), largest / len(cuts)))
        level = level * jnp.repeat(draws, dims[axis_at] // shards_of).reshape([-1 if axis == axis_at else 1 for axis in range(len(dims))])
    return level


def centred(own_key, shape, spread, bound, split=(), held_as=jnp.bfloat16):
    values = spread * jax.random.normal(own_key, shape, jnp.float32)
    if split:
        values = values * shard_levels(own_key, shape, split, -0.22, 0.18)
    return jnp.clip(values, -bound, bound).astype(held_as)


def heavy_noise(key, shape, scale, reach, cuts, heavy, dtype=jnp.bfloat16):
    drawn = scale * jax.random.normal(key, shape, jnp.float32)
    if cuts:
        drawn = drawn * shard_levels(key, shape, cuts, -0.22, 0.18)
    return jnp.clip(spiked(drawn, jax.random.fold_in(key, 3), *heavy), -reach, reach).astype(dtype)


def setup_inputs(seed: int = 0, part: int = 0) -> dict:
    arg_keys = jax.random.split(jax.random.key(seed), 9)
    part_splits = jax.random.split(jax.random.fold_in(arg_keys[8], part), 9)
    genotype = heavy_noise(part_splits[0], (NIND, NVAR), 1.0, 4.0, ((0, 16),), (0, 1, 16, 2.0))
    residual = centred(part_splits[1], (NIND, COLS), 1.5, 4.0, ((0, 16),))
    labels = with_ends((jax.random.randint(part_splits[2], (NIND, COLS), 0, 2) < 1).astype(jnp.int32), jax.random.fold_in(part_splits[2], 1), 0, 1)
    incl_old = jnp.clip(0.02 + 0.96000002 * jax.random.uniform(part_splits[3], (NVAR, COLS), jnp.float32) ** shard_levels(part_splits[3], (NVAR, COLS), ((0, 16),), -0.2, 0.2), 0.02, 0.98)
    mean_old = centred(part_splits[4], (NVAR, COLS), NIND ** -0.5, 0.078125, ((0, 16),), jnp.float32)
    prior_logit = jnp.clip(jax.random.uniform(arg_keys[5], (COLS,), jnp.float32, -4.0, 0.0), -4.0, 0.0)
    slab_scale = jnp.clip(jnp.exp(jax.random.uniform(arg_keys[6], (COLS,), jnp.float32, math.log(0.25), math.log(8.0))), 0.25, 8.0)
    offset = jnp.clip(jax.random.uniform(arg_keys[7], (COLS,), jnp.float32, -2.0, 1.0), -2.0, 1.0)
    return dict(genotype=genotype, residual=residual, labels=labels, incl_old=incl_old, mean_old=mean_old, prior_logit=prior_logit, slab_scale=slab_scale, offset=offset)


def reference(genotype, residual, labels, incl_old, mean_old, prior_logit, slab_scale, offset):
    corr = jnp.dot(genotype.T, residual, preferred_element_type=jnp.float32)
    stat = corr / NIND + incl_old * mean_old
    shrink = slab_scale / (1.0 + slab_scale)
    mean_new = stat * shrink
    logit = prior_logit - 0.5 * jnp.log1p(slab_scale) + 0.5 * NIND * shrink * stat * stat
    incl_new = 0.5 * incl_old + 0.5 * jax.nn.sigmoid(logit)
    effect = (incl_new * mean_new).astype(jnp.bfloat16)
    eta = jnp.dot(genotype, effect, preferred_element_type=jnp.float32) + offset
    resid_new = 4.0 * (labels.astype(jnp.float32) - jax.nn.sigmoid(eta))
    return incl_new, mean_new, resid_new
```

```python
import functools

import jax
import jax.numpy as jnp
import numpy as np
from jax import lax
from jax.experimental import pallas as pl
from jax.experimental.pallas import tpu as pltpu
from jax.sharding import PartitionSpec as P

STEPS = 256.0
TOP = 32700.0
PAD = 16
VMEM = 48 * 1024 * 1024


def ring_of(devices):
    chips = devices[0, ::2]
    where = [getattr(d, "coords", None) for d in chips]
    count = len(where)
    plain = list(range(count))
    if any(w is None for w in where):
        where = [(0, k % 2, k // 2) for k in plain]
    varying = [k for k in range(3) if len({w[k] for w in where}) > 1]
    if len(varying) != 2:
        return sorted(plain, key=lambda k: tuple(where[k]))
    short, long = sorted(varying, key=lambda k: len({w[k] for w in where}))
    low = min(w[short] for w in where)
    if len({w[short] for w in where}) != 2:
        return plain
    up = sorted((k for k in plain if where[k][short] == low), key=lambda k: where[k][long])
    down = sorted((k for k in plain if where[k][short] != low), key=lambda k: -where[k][long])
    return up + down


def decode(message):
    rows = message.shape[0] - PAD
    code = message[rows : rows + 1, :].astype(jnp.float32)
    return message[:rows, :].astype(jnp.float32) * (jnp.exp2(code * (1.0 / STEPS)) * (1.0 / TOP))


def local_sum(own_ref, other_ref, res_ref, res_other_ref):
    dims = (((0,), (0,)), ((), ()))
    return lax.dot_general(
        own_ref[...], res_ref[...], dims, preferred_element_type=jnp.float32
    ) + lax.dot_general(
        other_ref[...], res_other_ref[...], dims, preferred_element_type=jnp.float32
    )


def encode_to(out_ref, total):
    rows = total.shape[0]
    top = jnp.maximum(jnp.max(jnp.abs(total), axis=0, keepdims=True), 1e-30)
    code = jnp.ceil(jnp.log2(top) * STEPS)
    scaled = jnp.round(total * (TOP * jnp.exp2(code * (-1.0 / STEPS))))
    out_ref[:rows, :] = scaled.astype(jnp.int32).astype(jnp.int16)
    out_ref[rows:, :] = jnp.broadcast_to(code, (PAD, code.shape[1])).astype(jnp.int32).astype(jnp.int16)


def start_kernel(at_ref, own_ref, other_ref, res_ref, res_other_ref, out_ref):
    encode_to(out_ref, local_sum(own_ref, other_ref, res_ref, res_other_ref))


def add_kernel(at_ref, own_ref, other_ref, res_ref, res_other_ref, got_ref, out_ref):
    encode_to(
        out_ref, local_sum(own_ref, other_ref, res_ref, res_other_ref) + decode(got_ref[...])
    )


def update_kernel(
    total, at_ref, own_ref, other_ref, res_ref, res_other_ref, right_ref, left_ref, incl_ref,
    mean_ref, prior_ref, scale_ref, *rest
):
    incl_new_ref, mean_new_ref, effect_ref = rest[-3:]
    corr = local_sum(own_ref, other_ref, res_ref, res_other_ref)
    corr = corr + decode(right_ref[...]) + decode(left_ref[...])
    incl = incl_ref[...]
    scale = scale_ref[...]
    stat = corr / total + incl * mean_ref[...]
    shrink = scale / (1.0 + scale)
    mean_new = stat * shrink
    logit = prior_ref[...] - 0.5 * jnp.log1p(scale) + 0.5 * total * shrink * stat * stat
    incl_new = 0.5 * incl + 0.5 * jax.nn.sigmoid(logit)
    incl_new_ref[...] = incl_new
    mean_new_ref[...] = mean_new
    effect_ref[...] = (incl_new * mean_new).astype(jnp.bfloat16)


def eta_kernel(pieces, first, at_ref, *refs):
    out_ref, out_other_ref = refs[-2:]
    mine = other = None
    for k in range(pieces):
        own_ref, peer_ref, effect_ref = refs[3 * k : 3 * k + 3]
        a = jnp.dot(own_ref[...], effect_ref[...], preferred_element_type=jnp.float32)
        b = jnp.dot(peer_ref[...], effect_ref[...], preferred_element_type=jnp.float32)
        mine = a if mine is None else mine + a
        other = b if other is None else other + b
    if not first:
        mine = mine + refs[3 * pieces][...]
        other = other + refs[3 * pieces + 1][...]
    out_ref[...] = mine
    out_other_ref[...] = other


def end_kernel(eta_ref, got_ref, labels_ref, offset_ref, out_ref):
    eta = eta_ref[...] + got_ref[...] + offset_ref[...]
    out_ref[...] = 4.0 * (labels_ref[...].astype(jnp.float32) - jax.nn.sigmoid(eta))


def on_device(ring, genotype, residual, labels, incl_old, mean_old, prior_logit, slab_scale, offset):
    n = lax.axis_size("ind")
    people, cols = residual.shape
    total = float(people * n)
    block = incl_old.shape[0]
    part = block // 2
    size = len(ring)
    reach = size // 2
    spot = {chip: k for k, chip in enumerate(ring)}

    me = lax.axis_index("ind")
    core = lax.rem(me, 2)
    table = np.zeros((n, size), np.int32)
    for dev in range(n):
        for d in range(size):
            table[dev, d] = 2 * ring[(spot[dev // 2] + d) % size] + dev % 2
    owners = lax.dynamic_slice(jnp.asarray(table), (me, 0), (1, size)).reshape(size)

    swap = [(k, k ^ 1) for k in range(n)]
    right, left = [], []
    for k, chip in enumerate(ring):
        for c in range(2):
            right.append((2 * chip + c, 2 * ring[(k + 1) % size] + c))
            left.append((2 * chip + c, 2 * ring[(k - 1) % size] + c))

    residual_other = lax.ppermute(residual, "ind", swap)
    order = [reach]
    for d in range(reach - 1, 0, -1):
        order += [d, size - d]
    order += [0]
    peer = {}
    for d in order:
        if d in peer:
            continue
        wanted = owners[d] + 1 - 2 * core
        slab = lax.dynamic_slice(genotype, (0, wanted * block), (people, block))
        peer[d] = lax.ppermute(slab, "ind", swap)

    params = pltpu.CompilerParams(vmem_limit_bytes=VMEM)

    def specs(d, half):
        return [
            pl.BlockSpec((people, part), lambda i, at, d=d, half=half: (0, 2 * at[d] + half)),
            pl.BlockSpec((people, part), lambda i, at, half=half: (0, half)),
        ]

    def whole(shape):
        return pl.BlockSpec(shape, lambda i, at: (0,) * len(shape))

    res_spec = whole((people, cols))
    message = jax.ShapeDtypeStruct((part + PAD, cols), jnp.int16)
    message_spec = whole(message.shape)
    dot_cost = pl.CostEstimate(
        flops=4 * people * part * cols,
        bytes_accessed=4 * people * part + 4 * people * cols + 4 * part * cols,
        transcendentals=0,
    )

    def outgoing(d, half, got):
        kernel = start_kernel if got is None else add_kernel
        extra = [] if got is None else [got]
        return pl.pallas_call(
            kernel,
            grid_spec=pltpu.PrefetchScalarGridSpec(
                num_scalar_prefetch=1,
                grid=(1,),
                in_specs=specs(d, half) + [res_spec] * 2 + [message_spec] * len(extra),
                out_specs=message_spec,
            ),
            out_shape=message,
            compiler_params=params,
            cost_estimate=dot_cost,
            name="sum_block",
        )(owners, genotype, peer[d], residual, residual_other, *extra)

    got = {}
    for d in range(reach, 0, -1):
        for way, half in ((0, 0), (1, 1), (0, 1), (1, 0)):
            if d == reach and way != half:
                continue
            at = d if way == 0 else (size - d) % size
            sent = outgoing(at, half, got.get((way, half)))
            got[way, half] = lax.ppermute(sent, "ind", right if way == 0 else left)

    prior = prior_logit.reshape(1, cols)
    scale = slab_scale.reshape(1, cols)
    row = whole((1, cols))
    state = pl.BlockSpec((part, cols), lambda i, at: (0, 0))
    outs = None
    effects = {}
    for half in range(2):
        at_half = pl.BlockSpec((part, cols), lambda i, at, half=half: (half, 0))
        extra = [] if outs is None else list(outs)
        incl_new, mean_new, effects[half] = pl.pallas_call(
            functools.partial(update_kernel, total),
            grid_spec=pltpu.PrefetchScalarGridSpec(
                num_scalar_prefetch=1,
                grid=(1,),
                in_specs=specs(0, half)
                + [res_spec] * 2
                + [message_spec] * 2
                + [at_half] * 2
                + [row] * 2
                + [pl.BlockSpec(memory_space=pl.ANY)] * len(extra),
                out_specs=[at_half, at_half, state],
            ),
            out_shape=[
                jax.ShapeDtypeStruct((block, cols), jnp.float32),
                jax.ShapeDtypeStruct((block, cols), jnp.float32),
                jax.ShapeDtypeStruct((part, cols), jnp.bfloat16),
            ],
            input_output_aliases={} if outs is None else {11: 0, 12: 1},
            compiler_params=params,
            name="update",
        )(
            owners, genotype, peer[0], residual, residual_other, got[0, half], got[1, half],
            incl_old, mean_old, prior, scale, *extra
        )
        outs = (incl_new, mean_new)

    eta_spec = whole((people, cols))
    eta_shape = jax.ShapeDtypeStruct((people, cols), jnp.float32)

    def product(pieces, before):
        in_specs, args = [], []
        for d, half, effect in pieces:
            in_specs += specs(d, half) + [state]
            args += [genotype, peer[d], effect]
        return pl.pallas_call(
            functools.partial(eta_kernel, len(pieces), before is None),
            grid_spec=pltpu.PrefetchScalarGridSpec(
                num_scalar_prefetch=1,
                grid=(1,),
                in_specs=in_specs + [eta_spec] * (0 if before is None else 2),
                out_specs=[eta_spec] * 2,
            ),
            out_shape=[eta_shape] * 2,
            compiler_params=params,
            cost_estimate=pl.CostEstimate(
                flops=4 * people * part * cols * len(pieces),
                bytes_accessed=len(pieces) * (4 * people * part + 2 * part * cols)
                + 16 * people * cols,
                transcendentals=0,
            ),
            name="add_eta",
        )(owners, *args, *(() if before is None else before))

    held = {(way, half): effects[half] for way in range(2) for half in range(2)}
    eta = None
    pending = [(0, 0, effects[0]), (0, 1, effects[1])]
    for hop in range(1, reach + 1):
        fresh = []
        for way, half in ((0, 0), (1, 1), (0, 1), (1, 0)):
            if hop == reach and way != half:
                continue
            held[way, half] = lax.ppermute(
                held[way, half], "ind", right if way == 0 else left
            )
            fresh.append(((size - hop) % size if way == 0 else hop, half, held[way, half]))
        eta = product(pending, eta)
        pending = fresh
    eta = product(pending, eta)

    eta_got = lax.ppermute(eta[1], "ind", swap)
    resid_new = pl.pallas_call(
        end_kernel,
        out_shape=eta_shape,
        compiler_params=params,
        name="new_residual",
    )(eta[0], eta_got, labels, offset.reshape(1, cols))
    return (outs[0], outs[1], resid_new)


def solution(mesh):
    split = P(("groups", "ind"), None)
    return jax.shard_map(
        functools.partial(on_device, ring_of(mesh.devices)),
        mesh=mesh,
        in_specs=(split, split, split, split, split, P(), P(), P()),
        out_specs=(split, split, split),
        check_vma=False,
    )
```

```python
import functools

import jax
import jax.numpy as jnp
from jax import lax
from jax.experimental import pallas as pl
from jax.experimental.pallas import tpu as pltpu
from jax.sharding import PartitionSpec as P

STEPS = 256.0
TOP = 32700.0
PAD = 16
LANES = 128
VMEM = 24 * 1024 * 1024


def ring_of(devices):
    chips = devices[0, ::2]
    where = [getattr(d, "coords", None) for d in chips]
    count = len(where)
    plain = list(range(count))
    if any(w is None for w in where):
        where = [(0, k % 2, k // 2) for k in plain]
    varying = [k for k in range(3) if len({w[k] for w in where}) > 1]
    if len(varying) != 2:
        return sorted(plain, key=lambda k: tuple(where[k]))
    short, long = sorted(varying, key=lambda k: len({w[k] for w in where}))
    low = min(w[short] for w in where)
    if len({w[short] for w in where}) != 2:
        return plain
    up = sorted((k for k in plain if where[k][short] == low), key=lambda k: where[k][long])
    down = sorted((k for k in plain if where[k][short] != low), key=lambda k: -where[k][long])
    return up + down


def owners_of(ring, distances):
    chip = lax.div(lax.axis_index("ind"), 2)
    spot = jnp.int32(0)
    for k, c in enumerate(ring):
        spot = jnp.where(chip == c, k, spot)
    found = []
    for d in distances:
        at = lax.rem(spot + d, len(ring))
        owner = jnp.int32(ring[0])
        for k, c in enumerate(ring):
            owner = jnp.where(at == k, c, owner)
        found.append(owner)
    return found


def pick_kernel(ring, wanted, block, genotype_ref, before_ref, *refs):
    outs, sems = refs[:-1], refs[-1]
    core = lax.rem(lax.axis_index("ind"), 2)
    owners = dict(zip([d for d, _ in wanted], owners_of(ring, [d for d, _ in wanted])))
    copies = []
    for k, (d, swapped) in enumerate(wanted):
        parity = 1 - core if swapped else core
        at = pl.multiple_of((2 * owners[d] + parity) * block, LANES)
        copies.append(
            pltpu.make_async_copy(genotype_ref.at[:, pl.ds(at, block)], outs[k], sems.at[k])
        )
        copies[-1].start()
    for copy in copies:
        copy.wait()


def flip_kernel(before_ref, mine_ref, other_ref, out_ref):
    people = mine_ref.shape[0]
    out_ref[:, :people] = mine_ref[...].T
    out_ref[:, people:] = other_ref[...].T


def local_sum(res_ref, own_ref, peer_ref, low, high):
    people = own_ref.shape[0]
    return jnp.dot(
        res_ref[:, :people], own_ref[:, low:high], preferred_element_type=jnp.float32
    ) + jnp.dot(
        res_ref[:, people:], peer_ref[:, low:high], preferred_element_type=jnp.float32
    )


def decode(ref):
    rows = ref.shape[0] - PAD
    code = ref[rows:, :].astype(jnp.float32)[:1, :]
    return ref[:rows, :].astype(jnp.float32) * (jnp.exp2(code * (1.0 / STEPS)) * (1.0 / TOP))


def encode(ref, tiles):
    height = tiles[0].shape[0]
    top = functools.reduce(jnp.maximum, [jnp.abs(t) for t in tiles])
    top = jnp.maximum(jnp.max(top, axis=0, keepdims=True), 1e-30)
    code = jnp.ceil(jnp.log2(top) * STEPS)
    scale = TOP * jnp.exp2(code * (-1.0 / STEPS))
    for k, t in enumerate(tiles):
        ref[k * height : (k + 1) * height, :] = (
            jnp.round(t * scale).astype(jnp.int32).astype(jnp.int16)
        )
    ref[len(tiles) * height :, :] = (
        jnp.broadcast_to(code, (PAD, LANES)).astype(jnp.int32).astype(jnp.int16)
    )


def tiles_of(total):
    return [total[:, k : k + LANES] for k in range(0, total.shape[1], LANES)]


def far_kernel(low, high, before_ref, res_ref, own_ref, peer_ref, right_ref, left_ref):
    tiles = tiles_of(local_sum(res_ref, own_ref, peer_ref, low, high))
    half = len(tiles) // 2
    encode(right_ref, tiles[:half])
    encode(left_ref, tiles[half:])


def hop_kernel(
    low, high, before_ref, res_ref, own_ref, peer_ref, own_left_ref, peer_left_ref, got_right_ref,
    got_left_ref, right_ref, left_ref
):
    for way, own, peer, got_ref, out_ref in (
        (0, own_ref, peer_ref, got_right_ref, right_ref),
        (1, own_left_ref, peer_left_ref, got_left_ref, left_ref),
    ):
        tiles = tiles_of(local_sum(res_ref, own, peer, low, high))
        got = decode(got_ref)
        height = tiles[0].shape[0]
        count = got.shape[0] // height
        first = 0 if way == 0 else len(tiles) - count
        for k in range(count):
            tiles[first + k] = tiles[first + k] + got[k * height : (k + 1) * height, :]
        encode(out_ref, tiles)


def near_kernel(before_ref, res_ref, own_ref, peer_ref, out_ref):
    out_ref[...] = local_sum(res_ref, own_ref, peer_ref, 0, own_ref.shape[1])


def update_kernel(total, low, before_ref, corr_ref, right_ref, left_ref, incl_ref, mean_ref, prior_ref,
                  scale_ref, *rest):
    incl_new_ref, mean_new_ref, effect_ref = rest[-3:]
    height = corr_ref.shape[0]
    right, left = decode(right_ref), decode(left_ref)
    scale = scale_ref[...]
    shrink = scale / (1.0 + scale)
    start = prior_ref[...] - 0.5 * jnp.log1p(scale)
    steep = 0.5 * total * shrink
    halves = [(right, 0), (left, 1)]
    tiles = effect_ref.shape[0] // LANES
    for k in range(tiles):
        corr = corr_ref[:, low + k * LANES : low + (k + 1) * LANES]
        for got, way in halves:
            count = got.shape[0] // height
            first = 0 if way == 0 else tiles - count
            if first <= k < first + count:
                corr = corr + got[(k - first) * height : (k - first + 1) * height, :]
        rows = slice(k * LANES, (k + 1) * LANES)
        incl = incl_ref[rows, :]
        stat = corr.T / total + incl * mean_ref[rows, :]
        mean_new = stat * shrink
        incl_new = 0.5 * incl + 0.5 * jax.nn.sigmoid(start + steep * stat * stat)
        incl_new_ref[rows, :] = incl_new
        mean_new_ref[rows, :] = mean_new
        effect_ref[rows, :] = (incl_new * mean_new).astype(jnp.bfloat16)


def eta_kernel(ring, low, part, first, before_ref, gathered_ref, *refs):
    size = len(ring)
    own, peer = refs[:size], refs[size : 2 * size]
    out_ref, out_other_ref = refs[-2:]
    mine = other = None
    for d, owner in enumerate(owners_of(ring, range(size))):
        effect = gathered_ref[pl.ds(pl.multiple_of(owner * part, part), part), :]
        a = jnp.dot(own[d][:, low : low + part], effect, preferred_element_type=jnp.float32)
        b = jnp.dot(peer[d][:, low : low + part], effect, preferred_element_type=jnp.float32)
        mine = a if mine is None else mine + a
        other = b if other is None else other + b
    if not first:
        mine = mine + refs[2 * size][...]
        other = other + refs[2 * size + 1][...]
    out_ref[...] = mine
    out_other_ref[...] = other


def end_kernel(eta_ref, got_ref, labels_ref, offset_ref, out_ref):
    eta = eta_ref[...] + got_ref[...] + offset_ref[...]
    out_ref[...] = 4.0 * (labels_ref[...].astype(jnp.float32) - jax.nn.sigmoid(eta))


def on_device(ring, genotype, residual, labels, incl_old, mean_old, prior_logit, slab_scale, offset):
    n = lax.axis_size("ind")
    people, cols = residual.shape
    total = float(people * n)
    block = incl_old.shape[0]
    size = len(ring)
    reach = size // 2
    pieces = 2 if block % (4 * LANES) == 0 else 1
    part = block // pieces
    f32, bf16 = jnp.float32, jnp.bfloat16
    params = pltpu.CompilerParams(vmem_limit_bytes=VMEM)

    swap = [(k, k ^ 1) for k in range(n)]
    right, left = [], []
    for k, chip in enumerate(ring):
        for c in range(2):
            right.append((2 * chip + c, 2 * ring[(k + 1) % size] + c))
            left.append((2 * chip + c, 2 * ring[(k - 1) % size] + c))

    anywhere = pl.BlockSpec(memory_space=pl.ANY)

    def after(before, args):
        return [anywhere] + [pl.BlockSpec()] * len(args)

    peer, own = {}, {}

    def pick(distances, before):
        wanted = [(d, True) for d in distances] + [(d, False) for d in distances]
        found = pl.pallas_call(
            functools.partial(pick_kernel, ring, wanted, block),
            in_specs=[pl.BlockSpec(memory_space=pltpu.HBM), anywhere],
            out_specs=[anywhere] * len(wanted),
            out_shape=[jax.ShapeDtypeStruct((people, block), bf16)] * len(wanted),
            scratch_shapes=[pltpu.SemaphoreType.DMA((len(wanted),))],
            compiler_params=params,
            name="pick_blocks",
        )(pltpu.with_memory_space_constraint(genotype, pltpu.HBM), before)
        for k, d in enumerate(distances):
            peer[d] = lax.ppermute(found[k], "ind", swap)
            own[d] = found[len(distances) + k]
        return found[0]

    def around(d):
        return [0] if d == 0 else [d, size - d] if 2 * d != size else [d]

    residual_other = lax.ppermute(residual, "ind", swap)
    last = pick(around(reach), residual)
    if reach > 1:
        last = pick(around(reach - 1), last)
    res = last = pl.pallas_call(
        flip_kernel,
        in_specs=after(last, (residual, residual_other)),
        out_shape=jax.ShapeDtypeStruct((cols, 2 * people), bf16),
        compiler_params=params,
        name="flip",
    )(last, residual, residual_other)

    def message(width):
        return jax.ShapeDtypeStruct((width // LANES * cols + PAD, LANES), jnp.int16)

    def dot_cost(width):
        return pl.CostEstimate(
            flops=4 * people * width * cols,
            bytes_accessed=4 * people * width + 4 * people * cols + 4 * width * cols,
            transcendentals=0,
        )

    got = {}
    for d in range(reach, 0, -1):
        for piece in range(pieces):
            low, high = piece * part, (piece + 1) * part
            if d == reach:
                kernel, width, name = far_kernel, part // 2, "sum_far"
                args = (res, own[d], peer[d])
            else:
                kernel, width, name = hop_kernel, part, "sum_hop"
                args = (res, own[d], peer[d], own[size - d], peer[size - d], *got[piece])
            sent = pl.pallas_call(
                functools.partial(kernel, low, high),
                in_specs=after(last, args),
                out_shape=[message(width)] * 2,
                compiler_params=params,
                cost_estimate=dot_cost(2 * width),
                name=name,
            )(last, *args)
            last = sent[0]
            got[piece] = (lax.ppermute(sent[0], "ind", right), lax.ppermute(sent[1], "ind", left))
        if d > 1:
            last = pick(around(d - 2), last)
    if reach == 1:
        last = pick([0], last)

    near = last = pl.pallas_call(
        near_kernel,
        in_specs=after(last, (res, own[0], peer[0])),
        out_shape=jax.ShapeDtypeStruct((cols, block), f32),
        compiler_params=params,
        cost_estimate=dot_cost(block),
        name="sum_near",
    )(last, res, own[0], peer[0])

    prior = prior_logit.reshape(1, cols)
    scale = slab_scale.reshape(1, cols)

    def full(shape):
        return pl.BlockSpec(shape, lambda i: (0,) * len(shape))

    outs = ()
    gathered = []
    groups = [[2 * chip + c for chip in range(size)] for c in range(2)]
    for piece in range(pieces):
        rows = pl.BlockSpec((part, cols), lambda i, piece=piece: (piece, 0))
        incl_new, mean_new, effect = pl.pallas_call(
            functools.partial(update_kernel, total, piece * part),
            grid=(1,),
            in_specs=[anywhere, full((cols, block))]
            + [full(m.shape) for m in got[piece]]
            + [rows] * 2
            + [full((1, cols))] * 2
            + [anywhere] * len(outs),
            out_specs=[rows, rows, full((part, cols))],
            out_shape=[
                jax.ShapeDtypeStruct((block, cols), f32),
                jax.ShapeDtypeStruct((block, cols), f32),
                jax.ShapeDtypeStruct((part, cols), bf16),
            ],
            input_output_aliases={8: 0, 9: 1} if outs else {},
            compiler_params=params,
            name="update",
        )(last, near, *got[piece], incl_old, mean_old, prior, scale, *outs)
        outs = (incl_new, mean_new)
        last = effect
        gathered.append(
            lax.all_gather(effect, "ind", axis=0, tiled=True, axis_index_groups=groups)
        )

    eta_shape = jax.ShapeDtypeStruct((people, cols), f32)
    eta = ()
    for piece in range(pieces):
        args = (
            gathered[piece], *[own[d] for d in range(size)], *[peer[d] for d in range(size)], *eta
        )
        eta = pl.pallas_call(
            functools.partial(eta_kernel, ring, piece * part, part, not eta),
            in_specs=after(last, args),
            out_shape=[eta_shape] * 2,
            compiler_params=params,
            cost_estimate=pl.CostEstimate(
                flops=4 * people * part * size * cols,
                bytes_accessed=size * (4 * people * part + 2 * part * cols),
                transcendentals=0,
            ),
            name="add_eta",
        )(last, *args)
        last = eta[0]

    eta_got = lax.ppermute(eta[1], "ind", swap)
    resid_new = pl.pallas_call(
        end_kernel,
        out_shape=eta_shape,
        compiler_params=params,
        name="new_residual",
    )(eta[0], eta_got, labels, offset.reshape(1, cols))
    return (outs[0], outs[1], resid_new)


def solution(mesh):
    split = P(("groups", "ind"), None)
    return jax.shard_map(
        functools.partial(on_device, ring_of(mesh.devices)),
        mesh=mesh,
        in_specs=(split, split, split, split, split, P(), P(), P()),
        out_specs=(split, split, split),
        check_vma=False,
    )
```

```python
import functools

import jax
import jax.numpy as jnp
from jax import lax
from jax.experimental import pallas as pl
from jax.experimental.pallas import tpu as pltpu
from jax.sharding import PartitionSpec as P

STEPS = 256.0
TOP = 32700.0
PAD = 16
LANES = 128
VMEM = 14 * 1024 * 1024


def ring_of(devices):
    chips = devices[0, ::2]
    where = [getattr(d, "coords", None) for d in chips]
    count = len(where)
    plain = list(range(count))
    if any(w is None for w in where):
        where = [(0, k % 2, k // 2) for k in plain]
    varying = [k for k in range(3) if len({w[k] for w in where}) > 1]
    if len(varying) != 2:
        return sorted(plain, key=lambda k: tuple(where[k]))
    short, long = sorted(varying, key=lambda k: len({w[k] for w in where}))
    low = min(w[short] for w in where)
    if len({w[short] for w in where}) != 2:
        return plain
    up = sorted((k for k in plain if where[k][short] == low), key=lambda k: where[k][long])
    down = sorted((k for k in plain if where[k][short] != low), key=lambda k: -where[k][long])
    return up + down


def owners_of(ring, distances):
    chip = lax.div(lax.axis_index("ind"), 2)
    spot = jnp.int32(0)
    for k, c in enumerate(ring):
        spot = jnp.where(chip == c, k, spot)
    found = []
    for d in distances:
        at = lax.rem(spot + d, len(ring))
        owner = jnp.int32(ring[0])
        for k, c in enumerate(ring):
            owner = jnp.where(at == k, c, owner)
        found.append(owner)
    return found


def pick_kernel(ring, wanted, block, genotype_ref, *refs):
    outs, sems = refs[-1 - len(wanted) : -1], refs[-1]
    core = lax.rem(lax.axis_index("ind"), 2)
    needed = sorted({d for distances, _ in wanted for d in distances})
    owners = dict(zip(needed, owners_of(ring, needed)))
    copies = []
    for out_ref, (distances, swapped) in zip(outs, wanted):
        parity = 1 - core if swapped else core
        for k, d in enumerate(distances):
            at = pl.multiple_of((2 * owners[d] + parity) * block, LANES)
            copies.append(
                pltpu.make_async_copy(
                    genotype_ref.at[:, pl.ds(at, block)], out_ref.at[k], sems.at[len(copies)]
                )
            )
            copies[-1].start()
    for copy in copies:
        copy.wait()


def flip_kernel(before_ref, mine_ref, other_ref, out_ref):
    people = mine_ref.shape[0]
    out_ref[:, :people] = mine_ref[...].T
    out_ref[:, people:] = other_ref[...].T


def local_sum(res_ref, own_ref, peer_ref, at, low, high):
    people = own_ref.shape[1]
    return jnp.dot(
        res_ref[:, :people], own_ref[at[0], :, low:high], preferred_element_type=jnp.float32
    ) + jnp.dot(
        res_ref[:, people:], peer_ref[at[1], :, low:high], preferred_element_type=jnp.float32
    )


def decode(ref):
    rows = ref.shape[0] - PAD
    code = ref[rows:, :].astype(jnp.float32)[:1, :]
    return ref[:rows, :].astype(jnp.float32) * (jnp.exp2(code * (1.0 / STEPS)) * (1.0 / TOP))


def encode(ref, tiles):
    height = tiles[0].shape[0]
    top = functools.reduce(jnp.maximum, [jnp.abs(t) for t in tiles])
    top = jnp.maximum(jnp.max(top, axis=0, keepdims=True), 1e-30)
    code = jnp.ceil(jnp.log2(top) * STEPS)
    scale = TOP * jnp.exp2(code * (-1.0 / STEPS))
    for k, t in enumerate(tiles):
        ref[k * height : (k + 1) * height, :] = (
            jnp.round(t * scale).astype(jnp.int32).astype(jnp.int16)
        )
    ref[len(tiles) * height :, :] = (
        jnp.broadcast_to(code, (PAD, LANES)).astype(jnp.int32).astype(jnp.int16)
    )


def tiles_of(total):
    return [total[:, k : k + LANES] for k in range(0, total.shape[1], LANES)]


def far_kernel(at, low, high, before_ref, res_ref, own_ref, peer_ref, right_ref, left_ref):
    tiles = tiles_of(local_sum(res_ref, own_ref, peer_ref, at[0], low, high))
    half = len(tiles) // 2
    encode(right_ref, tiles[:half])
    encode(left_ref, tiles[half:])


def hop_kernel(
    at, low, high, before_ref, res_ref, own_ref, peer_ref, own_left_ref, peer_left_ref, got_right_ref,
    got_left_ref, right_ref, left_ref
):
    for way, own, peer, got_ref, out_ref in (
        (0, own_ref, peer_ref, got_right_ref, right_ref),
        (1, own_left_ref, peer_left_ref, got_left_ref, left_ref),
    ):
        tiles = tiles_of(local_sum(res_ref, own, peer, at[way], low, high))
        got = decode(got_ref)
        height = tiles[0].shape[0]
        count = got.shape[0] // height
        first = 0 if way == 0 else len(tiles) - count
        for k in range(count):
            tiles[first + k] = tiles[first + k] + got[k * height : (k + 1) * height, :]
        encode(out_ref, tiles)


def near_kernel(at, before_ref, res_ref, own_ref, peer_ref, out_ref):
    out_ref[...] = local_sum(res_ref, own_ref, peer_ref, at, 0, own_ref.shape[2])


def update_kernel(total, low, before_ref, corr_ref, right_ref, left_ref, incl_ref, mean_ref, prior_ref,
                  scale_ref, *rest):
    incl_new_ref, mean_new_ref, effect_ref = rest[-3:]
    height = corr_ref.shape[0]
    right, left = decode(right_ref), decode(left_ref)
    scale = scale_ref[...]
    shrink = scale / (1.0 + scale)
    start = prior_ref[...] - 0.5 * jnp.log1p(scale)
    steep = 0.5 * total * shrink
    halves = [(right, 0), (left, 1)]
    tiles = effect_ref.shape[0] // LANES
    for k in range(tiles):
        corr = corr_ref[:, low + k * LANES : low + (k + 1) * LANES]
        for got, way in halves:
            count = got.shape[0] // height
            first = 0 if way == 0 else tiles - count
            if first <= k < first + count:
                corr = corr + got[(k - first) * height : (k - first + 1) * height, :]
        rows = slice(k * LANES, (k + 1) * LANES)
        incl = incl_ref[rows, :]
        stat = corr.T / total + incl * mean_ref[rows, :]
        mean_new = stat * shrink
        incl_new = 0.5 * incl + 0.5 * jax.nn.sigmoid(start + steep * stat * stat)
        incl_new_ref[rows, :] = incl_new
        mean_new_ref[rows, :] = mean_new
        effect_ref[rows, :] = (incl_new * mean_new).astype(jnp.bfloat16)


def eta_kernel(places, first, before_ref, *refs):
    out_ref, out_other_ref = refs[-2:]
    mine = other = None
    for k, (at, low) in enumerate(places):
        effect_ref, own_ref, peer_ref = refs[3 * k : 3 * k + 3]
        effect = effect_ref[...]
        high = low + effect.shape[0]
        a = jnp.dot(own_ref[at[0], :, low:high], effect, preferred_element_type=jnp.float32)
        b = jnp.dot(peer_ref[at[1], :, low:high], effect, preferred_element_type=jnp.float32)
        mine = a if mine is None else mine + a
        other = b if other is None else other + b
    if not first:
        mine = mine + refs[3 * len(places)][...]
        other = other + refs[3 * len(places) + 1][...]
    out_ref[...] = mine
    out_other_ref[...] = other


def end_kernel(eta_ref, got_ref, labels_ref, offset_ref, out_ref):
    eta = eta_ref[...] + got_ref[...] + offset_ref[...]
    out_ref[...] = 4.0 * (labels_ref[...].astype(jnp.float32) - jax.nn.sigmoid(eta))


def on_device(ring, genotype, residual, labels, incl_old, mean_old, prior_logit, slab_scale, offset):
    n = lax.axis_size("ind")
    people, cols = residual.shape
    total = float(people * n)
    block = incl_old.shape[0]
    size = len(ring)
    reach = size // 2
    pieces = 2 if block % (4 * LANES) == 0 else 1
    part = block // pieces
    f32, bf16 = jnp.float32, jnp.bfloat16
    params = pltpu.CompilerParams(vmem_limit_bytes=VMEM)
    heavy = pl.CostEstimate(flops=10**10, bytes_accessed=10**6, transcendentals=0)
    light = pl.CostEstimate(flops=2 * 10**9, bytes_accessed=10**6, transcendentals=0)

    swap = [(k, k ^ 1) for k in range(n)]
    right, left = [], []
    for k, chip in enumerate(ring):
        for c in range(2):
            right.append((2 * chip + c, 2 * ring[(k + 1) % size] + c))
            left.append((2 * chip + c, 2 * ring[(k - 1) % size] + c))

    anywhere = pl.BlockSpec(memory_space=pl.ANY)

    def after(before, args):
        return [anywhere] + [pl.BlockSpec()] * len(args)

    def pick(wanted, *before):
        return pl.pallas_call(
            functools.partial(pick_kernel, ring, wanted, block),
            in_specs=[pl.BlockSpec(memory_space=pltpu.HBM)] + [anywhere] * len(before),
            out_specs=[anywhere] * len(wanted),
            out_shape=[
                jax.ShapeDtypeStruct((len(distances), people, block), bf16)
                for distances, _ in wanted
            ],
            scratch_shapes=[pltpu.SemaphoreType.DMA((sum(len(d) for d, _ in wanted),))],
            compiler_params=params,
            cost_estimate=heavy,
            name="pick_blocks",
        )(pltpu.with_memory_space_constraint(genotype, pltpu.HBM), *before)

    order = [reach]
    for d in range(reach - 1, 0, -1):
        order += [d, size - d]
    order += [0]
    batches = [b for b in (order[:1], order[1:3], order[3:]) if b]
    own, peer = {}, {}
    residual_other = lax.ppermute(residual, "ind", swap)
    last = None
    for k, batch in enumerate(batches):
        if k == 0:
            last, mine = pick([(batch, True), (batch, False)])
            own[reach] = (mine, 0)
        else:
            last = pick([(batch, True)], last)[0]
        sent = lax.ppermute(last, "ind", swap)
        peer.update({d: (sent, j) for j, d in enumerate(batch)})
    res = last = pl.pallas_call(
        flip_kernel,
        in_specs=after(last, (residual, residual_other)),
        out_shape=jax.ShapeDtypeStruct((cols, 2 * people), bf16),
        compiler_params=params,
        cost_estimate=heavy,
        name="flip",
    )(last, residual, residual_other)

    def shape_of(width):
        return jax.ShapeDtypeStruct((width // LANES * cols + PAD, LANES), jnp.int16)

    got = {}
    for d in range(reach, 0, -1):
        for piece in range(pieces):
            low, high = piece * part, (piece + 1) * part
            if d == reach > 1 and piece:
                last, _ = lax.optimization_barrier((last, peer[d - 1][0]))
            if d == reach:
                kernel, width, name, where = far_kernel, part // 2, "sum_far", (d,)
            else:
                kernel, width, name, where = hop_kernel, part, "sum_hop", (d, size - d)
            args = [res]
            for w in where:
                args += [own[w][0], peer[w][0]]
            if d < reach:
                args += got[piece]
            sent = pl.pallas_call(
                functools.partial(kernel, [(own[w][1], peer[w][1]) for w in where], low, high),
                in_specs=after(last, args),
                out_shape=[shape_of(width)] * 2,
                compiler_params=params,
                cost_estimate=heavy,
                name=name,
            )(last, *args)
            last = sent[0]
            got[piece] = (lax.ppermute(sent[0], "ind", right), lax.ppermute(sent[1], "ind", left))
        if d == reach:
            last = pick([(order[1:], False)], last)[0]
            own.update({w: (last, j) for j, w in enumerate(order[1:])})

    near = last = pl.pallas_call(
        functools.partial(near_kernel, (own[0][1], peer[0][1])),
        in_specs=after(last, (res, own[0], peer[0])),
        out_shape=jax.ShapeDtypeStruct((cols, block), f32),
        compiler_params=params,
        cost_estimate=light,
        name="sum_near",
    )(last, res, own[0][0], peer[0][0])

    prior = prior_logit.reshape(1, cols)
    scale = slab_scale.reshape(1, cols)

    def full(shape):
        return pl.BlockSpec(shape, lambda i: (0,) * len(shape))

    outs = ()
    effects = []
    for piece in range(pieces):
        rows = pl.BlockSpec((part, cols), lambda i, piece=piece: (piece, 0))
        incl_new, mean_new, effect = pl.pallas_call(
            functools.partial(update_kernel, total, piece * part),
            grid=(1,),
            in_specs=[anywhere, full((cols, block))]
            + [full(m.shape) for m in got[piece]]
            + [rows] * 2
            + [full((1, cols))] * 2
            + [anywhere] * len(outs),
            out_specs=[rows, rows, full((part, cols))],
            out_shape=[
                jax.ShapeDtypeStruct((block, cols), f32),
                jax.ShapeDtypeStruct((block, cols), f32),
                jax.ShapeDtypeStruct((part, cols), bf16),
            ],
            input_output_aliases={8: 0, 9: 1} if outs else {},
            compiler_params=params,
            cost_estimate=light,
            name="update",
        )(last, near, *got[piece], incl_old, mean_old, prior, scale, *outs)
        outs = (incl_new, mean_new)
        last = effect
        effects.append(effect)

    eta_shape = jax.ShapeDtypeStruct((people, cols), f32)
    def product(found, eta, before):
        args = [v for d, _, effect in found for v in (effect, own[d][0], peer[d][0])] + list(eta)
        places = [((own[d][1], peer[d][1]), piece * part) for d, piece, _ in found]
        return pl.pallas_call(
            functools.partial(eta_kernel, places, not eta),
            in_specs=after(before, args),
            out_shape=[eta_shape] * 2,
            compiler_params=params,
            cost_estimate=heavy if eta else light,
            name="add_eta",
        )(before, *args)

    eta = product([(0, piece, effects[piece]) for piece in range(pieces)], (), last)
    held = {(way, piece): effects[piece] for way in range(2) for piece in range(pieces)}
    etas = [eta[0]]
    for hop in range(1, reach + 1):
        for piece in range(pieces):
            found = []
            for way in range(2):
                if hop == reach and way != piece % 2:
                    continue
                message = held[way, piece]
                if hop > 1:
                    message, _ = lax.optimization_barrier((message, etas[-1 - pieces]))
                held[way, piece] = lax.ppermute(message, "ind", left if way else right)
                found.append((hop if way else size - hop, piece, held[way, piece]))
            if hop == reach and pieces == 2:
                tail = found if piece == 0 else tail + found
                if piece == 0:
                    continue
                found = tail
            if found:
                eta = product(found, eta, eta[0])
                etas.append(eta[0])

    eta_got = lax.ppermute(eta[1], "ind", swap)
    resid_new = pl.pallas_call(
        end_kernel,
        out_shape=eta_shape,
        compiler_params=params,
        cost_estimate=light,
        name="new_residual",
    )(eta[0], eta_got, labels, offset.reshape(1, cols))
    return (outs[0], outs[1], resid_new)


def solution(mesh):
    split = P(("groups", "ind"), None)
    return jax.shard_map(
        functools.partial(on_device, ring_of(mesh.devices)),
        mesh=mesh,
        in_specs=(split, split, split, split, split, P(), P(), P()),
        out_specs=(split, split, split),
        check_vma=False,
    )
```

```python
import functools

import jax
import jax.numpy as jnp
from jax import lax
from jax.experimental import pallas as pl
from jax.experimental.pallas import tpu as pltpu
from jax.sharding import PartitionSpec as P

STEPS = 256.0
TOP = 32700.0
PAD = 16
LANES = 128
VMEM = 14 * 1024 * 1024


def ring_of(devices):
    chips = devices[0, ::2]
    where = [getattr(d, "coords", None) for d in chips]
    count = len(where)
    plain = list(range(count))
    if any(w is None for w in where):
        where = [(0, k % 2, k // 2) for k in plain]
    varying = [k for k in range(3) if len({w[k] for w in where}) > 1]
    if len(varying) != 2:
        return sorted(plain, key=lambda k: tuple(where[k]))
    short, long = sorted(varying, key=lambda k: len({w[k] for w in where}))
    low = min(w[short] for w in where)
    if len({w[short] for w in where}) != 2:
        return plain
    up = sorted((k for k in plain if where[k][short] == low), key=lambda k: where[k][long])
    down = sorted((k for k in plain if where[k][short] != low), key=lambda k: -where[k][long])
    return up + down


def owners_of(ring, distances):
    chip = lax.div(lax.axis_index("ind"), 2)
    spot = jnp.int32(0)
    for k, c in enumerate(ring):
        spot = jnp.where(chip == c, k, spot)
    found = []
    for d in distances:
        at = lax.rem(spot + d, len(ring))
        owner = jnp.int32(ring[0])
        for k, c in enumerate(ring):
            owner = jnp.where(at == k, c, owner)
        found.append(owner)
    return found


def pick_kernel(ring, wanted, block, genotype_ref, *refs):
    outs, sems = refs[-1 - len(wanted) : -1], refs[-1]
    core = lax.rem(lax.axis_index("ind"), 2)
    needed = sorted({d for distances, _ in wanted for d in distances})
    owners = dict(zip(needed, owners_of(ring, needed)))
    copies = []
    for out_ref, (distances, swapped) in zip(outs, wanted):
        parity = 1 - core if swapped else core
        for k, d in enumerate(distances):
            at = pl.multiple_of((2 * owners[d] + parity) * block, LANES)
            copies.append(
                pltpu.make_async_copy(
                    genotype_ref.at[:, pl.ds(at, block)], out_ref.at[k], sems.at[len(copies)]
                )
            )
            copies[-1].start()
    for copy in copies:
        copy.wait()


def flip_kernel(before_ref, mine_ref, other_ref, out_ref):
    people = mine_ref.shape[0]
    out_ref[:, :people] = mine_ref[...].T
    out_ref[:, people:] = other_ref[...].T


def local_sum(res_ref, own_ref, peer_ref, at, low, high):
    people = own_ref.shape[1]
    return jnp.dot(
        res_ref[:, :people], own_ref[at[0], :, low:high], preferred_element_type=jnp.float32
    ) + jnp.dot(
        res_ref[:, people:], peer_ref[at[1], :, low:high], preferred_element_type=jnp.float32
    )


def decode(ref):
    rows = ref.shape[0] - PAD
    code = ref[rows:, :].astype(jnp.float32)[:1, :]
    return ref[:rows, :].astype(jnp.float32) * (jnp.exp2(code * (1.0 / STEPS)) * (1.0 / TOP))


def encode(ref, tiles):
    height = tiles[0].shape[0]
    top = functools.reduce(jnp.maximum, [jnp.abs(t) for t in tiles])
    top = jnp.maximum(jnp.max(top, axis=0, keepdims=True), 1e-30)
    code = jnp.ceil(jnp.log2(top) * STEPS)
    scale = TOP * jnp.exp2(code * (-1.0 / STEPS))
    for k, t in enumerate(tiles):
        ref[k * height : (k + 1) * height, :] = (
            jnp.round(t * scale).astype(jnp.int32).astype(jnp.int16)
        )
    ref[len(tiles) * height :, :] = (
        jnp.broadcast_to(code, (PAD, LANES)).astype(jnp.int32).astype(jnp.int16)
    )


def tiles_of(total):
    return [total[:, k : k + LANES] for k in range(0, total.shape[1], LANES)]


def far_kernel(at, low, high, before_ref, res_ref, own_ref, peer_ref, right_ref, left_ref):
    tiles = tiles_of(local_sum(res_ref, own_ref, peer_ref, at[0], low, high))
    half = len(tiles) // 2
    encode(right_ref, tiles[:half])
    encode(left_ref, tiles[half:])


def hop_kernel(
    at, low, high, before_ref, res_ref, own_ref, peer_ref, own_left_ref, peer_left_ref, got_right_ref,
    got_left_ref, right_ref, left_ref
):
    for way, own, peer, got_ref, out_ref in (
        (0, own_ref, peer_ref, got_right_ref, right_ref),
        (1, own_left_ref, peer_left_ref, got_left_ref, left_ref),
    ):
        tiles = tiles_of(local_sum(res_ref, own, peer, at[way], low, high))
        got = decode(got_ref)
        height = tiles[0].shape[0]
        count = got.shape[0] // height
        first = 0 if way == 0 else len(tiles) - count
        for k in range(count):
            tiles[first + k] = tiles[first + k] + got[k * height : (k + 1) * height, :]
        encode(out_ref, tiles)


def near_kernel(at, before_ref, res_ref, own_ref, peer_ref, out_ref):
    out_ref[...] = local_sum(res_ref, own_ref, peer_ref, at, 0, own_ref.shape[2])


def update_kernel(total, low, before_ref, corr_ref, right_ref, left_ref, incl_ref, mean_ref, prior_ref,
                  scale_ref, *rest):
    incl_new_ref, mean_new_ref, effect_ref = rest[-3:]
    height = corr_ref.shape[0]
    right, left = decode(right_ref), decode(left_ref)
    scale = scale_ref[...]
    shrink = scale / (1.0 + scale)
    start = prior_ref[...] - 0.5 * jnp.log1p(scale)
    steep = 0.5 * total * shrink
    halves = [(right, 0), (left, 1)]
    tiles = effect_ref.shape[0] // LANES
    for k in range(tiles):
        corr = corr_ref[:, low + k * LANES : low + (k + 1) * LANES]
        for got, way in halves:
            count = got.shape[0] // height
            first = 0 if way == 0 else tiles - count
            if first <= k < first + count:
                corr = corr + got[(k - first) * height : (k - first + 1) * height, :]
        rows = slice(k * LANES, (k + 1) * LANES)
        incl = incl_ref[rows, :]
        stat = corr.T / total + incl * mean_ref[rows, :]
        mean_new = stat * shrink
        incl_new = 0.5 * incl + 0.5 * jax.nn.sigmoid(start + steep * stat * stat)
        incl_new_ref[rows, :] = incl_new
        mean_new_ref[rows, :] = mean_new
        effect_ref[rows, :] = (incl_new * mean_new).astype(jnp.bfloat16)


def eta_kernel(places, first, before_ref, *refs):
    out_ref, out_other_ref = refs[-2:]
    mine = other = None
    for k, (at, low) in enumerate(places):
        effect_ref, own_ref, peer_ref = refs[3 * k : 3 * k + 3]
        effect = effect_ref[...]
        high = low + effect.shape[0]
        a = jnp.dot(own_ref[at[0], :, low:high], effect, preferred_element_type=jnp.float32)
        b = jnp.dot(peer_ref[at[1], :, low:high], effect, preferred_element_type=jnp.float32)
        mine = a if mine is None else mine + a
        other = b if other is None else other + b
    if not first:
        mine = mine + refs[3 * len(places)][...]
        other = other + refs[3 * len(places) + 1][...]
    out_ref[...] = mine
    out_other_ref[...] = other


def end_kernel(eta_ref, got_ref, labels_ref, offset_ref, out_ref):
    eta = eta_ref[...] + got_ref[...] + offset_ref[...]
    out_ref[...] = 4.0 * (labels_ref[...].astype(jnp.float32) - jax.nn.sigmoid(eta))


def on_device(ring, genotype, residual, labels, incl_old, mean_old, prior_logit, slab_scale, offset):
    n = lax.axis_size("ind")
    people, cols = residual.shape
    total = float(people * n)
    block = incl_old.shape[0]
    size = len(ring)
    reach = size // 2
    pieces = 2 if block % (4 * LANES) == 0 else 1
    part = block // pieces
    f32, bf16 = jnp.float32, jnp.bfloat16
    params = pltpu.CompilerParams(vmem_limit_bytes=VMEM)
    heavy = pl.CostEstimate(flops=10**10, bytes_accessed=10**6, transcendentals=0)
    longest = pl.CostEstimate(flops=10**11, bytes_accessed=10**6, transcendentals=0)
    light = pl.CostEstimate(flops=2 * 10**9, bytes_accessed=10**6, transcendentals=0)

    swap = [(k, k ^ 1) for k in range(n)]
    right, left = [], []
    for k, chip in enumerate(ring):
        for c in range(2):
            right.append((2 * chip + c, 2 * ring[(k + 1) % size] + c))
            left.append((2 * chip + c, 2 * ring[(k - 1) % size] + c))

    anywhere = pl.BlockSpec(memory_space=pl.ANY)

    def after(before, args):
        return [anywhere] + [pl.BlockSpec()] * len(args)

    def pick(wanted, cost, *before):
        return pl.pallas_call(
            functools.partial(pick_kernel, ring, wanted, block),
            in_specs=[pl.BlockSpec(memory_space=pltpu.HBM)] + [anywhere] * len(before),
            out_specs=[anywhere] * len(wanted),
            out_shape=[
                jax.ShapeDtypeStruct((len(distances), people, block), bf16)
                for distances, _ in wanted
            ],
            scratch_shapes=[pltpu.SemaphoreType.DMA((sum(len(d) for d, _ in wanted),))],
            compiler_params=params,
            cost_estimate=cost,
            name="pick_blocks",
        )(pltpu.with_memory_space_constraint(genotype, pltpu.HBM), *before)

    order = [reach]
    for d in range(reach - 1, 0, -1):
        order += [d, size - d]
    order += [0]
    own, peer = {}, {}

    def swapped(distances, sent):
        got = lax.ppermute(sent, "ind", swap)
        peer.update({d: (got, k) for k, d in enumerate(distances)})

    residual_other = lax.ppermute(residual, "ind", swap)
    (last,) = pick([(order[:1], True)], heavy)
    swapped(order[:1], last)
    next_two, others = order[1:3], order[3:]
    mine, last = pick([(order[:3], False), (next_two, True)], heavy, last)
    own.update({d: (mine, k) for k, d in enumerate(order[:3])})
    swapped(next_two, last)
    res = last = pl.pallas_call(
        flip_kernel,
        in_specs=after(last, (residual, residual_other)),
        out_shape=jax.ShapeDtypeStruct((cols, 2 * people), bf16),
        compiler_params=params,
        cost_estimate=heavy,
        name="flip",
    )(last, residual, residual_other)

    def shape_of(width):
        return jax.ShapeDtypeStruct((width // LANES * cols + PAD, LANES), jnp.int16)

    got = {}
    for d in range(reach, 0, -1):
        for piece in range(pieces):
            low, high = piece * part, (piece + 1) * part
            if d == reach > 1 and piece:
                last, _ = lax.optimization_barrier((last, peer[d - 1][0]))
            if d == reach:
                kernel, width, name, where = far_kernel, part // 2, "sum_far", (d,)
            else:
                kernel, width, name, where = hop_kernel, part, "sum_hop", (d, size - d)
            args = [res]
            for w in where:
                args += [own[w][0], peer[w][0]]
            if d < reach:
                args += got[piece]
            sent = pl.pallas_call(
                functools.partial(kernel, [(own[w][1], peer[w][1]) for w in where], low, high),
                in_specs=after(last, args),
                out_shape=[shape_of(width)] * 2,
                compiler_params=params,
                cost_estimate=longest,
                name=name,
            )(last, *args)
            last = sent[0]
            got[piece] = (lax.ppermute(sent[0], "ind", right), lax.ppermute(sent[1], "ind", left))
            if others and d == max(reach - 1, 1):
                if piece == 0:
                    (last,) = pick([(others, True)], light, last)
                    swapped(others, last)
                if piece == pieces - 1:
                    (last,) = pick([(others, False)], light, last)
                    own.update({w: (last, k) for k, w in enumerate(others)})

    near = last = pl.pallas_call(
        functools.partial(near_kernel, (own[0][1], peer[0][1])),
        in_specs=after(last, (res, own[0], peer[0])),
        out_shape=jax.ShapeDtypeStruct((cols, block), f32),
        compiler_params=params,
        cost_estimate=light,
        name="sum_near",
    )(last, res, own[0][0], peer[0][0])

    prior = prior_logit.reshape(1, cols)
    scale = slab_scale.reshape(1, cols)

    def full(shape):
        return pl.BlockSpec(shape, lambda i: (0,) * len(shape))

    outs = ()
    effects = []
    for piece in range(pieces):
        rows = pl.BlockSpec((part, cols), lambda i, piece=piece: (piece, 0))
        incl_new, mean_new, effect = pl.pallas_call(
            functools.partial(update_kernel, total, piece * part),
            grid=(1,),
            in_specs=[anywhere, full((cols, block))]
            + [full(m.shape) for m in got[piece]]
            + [rows] * 2
            + [full((1, cols))] * 2
            + [anywhere] * len(outs),
            out_specs=[rows, rows, full((part, cols))],
            out_shape=[
                jax.ShapeDtypeStruct((block, cols), f32),
                jax.ShapeDtypeStruct((block, cols), f32),
                jax.ShapeDtypeStruct((part, cols), bf16),
            ],
            input_output_aliases={8: 0, 9: 1} if outs else {},
            compiler_params=params,
            cost_estimate=light,
            name="update",
        )(last, near, *got[piece], incl_old, mean_old, prior, scale, *outs)
        outs = (incl_new, mean_new)
        last = effect
        effects.append(effect)

    eta_shape = jax.ShapeDtypeStruct((people, cols), f32)
    def product(found, eta, before):
        args = [v for d, _, effect in found for v in (effect, own[d][0], peer[d][0])] + list(eta)
        places = [((own[d][1], peer[d][1]), low) for d, low, _ in found]
        return pl.pallas_call(
            functools.partial(eta_kernel, places, not eta),
            in_specs=after(before, args),
            out_shape=[eta_shape] * 2,
            compiler_params=params,
            cost_estimate=heavy if eta else light,
            name="add_eta",
        )(before, *args)

    eta = product([(0, piece * part, effects[piece]) for piece in range(pieces)], (), last)
    held = {(way, piece): effects[piece] for way in range(2) for piece in range(pieces)}
    etas = [eta[0]]
    for hop in range(1, reach + 1):
        for piece in range(pieces):
            found = []
            for way in range(2):
                message = held[way, piece]
                if hop > 1:
                    message, _ = lax.optimization_barrier((message, etas[-1 - pieces]))
                low = 0
                if hop == reach:
                    low = way * (part // 2)
                    message = message[low : low + part // 2]
                held[way, piece] = lax.ppermute(message, "ind", left if way else right)
                found.append((hop if way else size - hop, piece * part + low, held[way, piece]))
            eta = product(found, eta, eta[0])
            etas.append(eta[0])

    eta_got = lax.ppermute(eta[1], "ind", swap)
    resid_new = pl.pallas_call(
        end_kernel,
        out_shape=eta_shape,
        compiler_params=params,
        cost_estimate=light,
        name="new_residual",
    )(eta[0], eta_got, labels, offset.reshape(1, cols))
    return (outs[0], outs[1], resid_new)


def solution(mesh):
    split = P(("groups", "ind"), None)
    return jax.shard_map(
        functools.partial(on_device, ring_of(mesh.devices)),
        mesh=mesh,
        in_specs=(split, split, split, split, split, P(), P(), P()),
        out_specs=(split, split, split),
        check_vma=False,
    )
```

```python
import functools

import jax
import jax.numpy as jnp
from jax import lax
from jax.experimental import pallas as pl
from jax.experimental.pallas import tpu as pltpu
from jax.sharding import PartitionSpec as P

STEPS = 256.0
TOP = 32700.0
PAD = 16
LANES = 128
VMEM = 14 * 1024 * 1024


def ring_of(devices):
    chips = devices[0, ::2]
    where = [getattr(d, "coords", None) for d in chips]
    count = len(where)
    plain = list(range(count))
    if any(w is None for w in where):
        where = [(0, k % 2, k // 2) for k in plain]
    varying = [k for k in range(3) if len({w[k] for w in where}) > 1]
    if len(varying) != 2:
        return sorted(plain, key=lambda k: tuple(where[k]))
    short, long = sorted(varying, key=lambda k: len({w[k] for w in where}))
    low = min(w[short] for w in where)
    if len({w[short] for w in where}) != 2:
        return plain
    up = sorted((k for k in plain if where[k][short] == low), key=lambda k: where[k][long])
    down = sorted((k for k in plain if where[k][short] != low), key=lambda k: -where[k][long])
    return up + down


def owners_of(ring, distances):
    chip = lax.div(lax.axis_index("ind"), 2)
    spot = jnp.int32(0)
    for k, c in enumerate(ring):
        spot = jnp.where(chip == c, k, spot)
    found = []
    for d in distances:
        at = lax.rem(spot + d, len(ring))
        owner = jnp.int32(ring[0])
        for k, c in enumerate(ring):
            owner = jnp.where(at == k, c, owner)
        found.append(owner)
    return found


def pick_kernel(ring, wanted, block, genotype_ref, *refs):
    outs, sems = refs[-1 - len(wanted) : -1], refs[-1]
    core = lax.rem(lax.axis_index("ind"), 2)
    needed = sorted({d for distances, _ in wanted for d in distances})
    owners = dict(zip(needed, owners_of(ring, needed)))
    copies = []
    for out_ref, (distances, swapped) in zip(outs, wanted):
        parity = 1 - core if swapped else core
        for k, d in enumerate(distances):
            at = pl.multiple_of((2 * owners[d] + parity) * block, LANES)
            copies.append(
                pltpu.make_async_copy(
                    genotype_ref.at[:, pl.ds(at, block)], out_ref.at[k], sems.at[len(copies)]
                )
            )
            copies[-1].start()
    for copy in copies:
        copy.wait()


def flip_kernel(before_ref, mine_ref, other_ref, out_ref):
    people = mine_ref.shape[0]
    out_ref[:, :people] = mine_ref[...].T
    out_ref[:, people:] = other_ref[...].T


def local_sum(res_ref, own_ref, peer_ref, at, low, high):
    people = own_ref.shape[1]
    return jnp.dot(
        res_ref[:, :people], own_ref[at[0], :, low:high], preferred_element_type=jnp.float32
    ) + jnp.dot(
        res_ref[:, people:], peer_ref[at[1], :, low:high], preferred_element_type=jnp.float32
    )


def decode(ref):
    rows = ref.shape[0] - PAD
    code = ref[rows:, :].astype(jnp.float32)[:1, :]
    return ref[:rows, :].astype(jnp.float32) * (jnp.exp2(code * (1.0 / STEPS)) * (1.0 / TOP))


def encode(ref, tiles):
    height = tiles[0].shape[0]
    top = functools.reduce(jnp.maximum, [jnp.abs(t) for t in tiles])
    top = jnp.maximum(jnp.max(top, axis=0, keepdims=True), 1e-30)
    code = jnp.ceil(jnp.log2(top) * STEPS)
    scale = TOP * jnp.exp2(code * (-1.0 / STEPS))
    for k, t in enumerate(tiles):
        ref[k * height : (k + 1) * height, :] = (
            jnp.round(t * scale).astype(jnp.int32).astype(jnp.int16)
        )
    ref[len(tiles) * height :, :] = (
        jnp.broadcast_to(code, (PAD, LANES)).astype(jnp.int32).astype(jnp.int16)
    )


def tiles_of(total):
    return [total[:, k : k + LANES] for k in range(0, total.shape[1], LANES)]


def far_kernel(at, low, high, before_ref, res_ref, own_ref, peer_ref, right_ref, left_ref):
    tiles = tiles_of(local_sum(res_ref, own_ref, peer_ref, at, low, high))
    half = len(tiles) // 2
    encode(right_ref, tiles[:half])
    encode(left_ref, tiles[half:])


def hop_kernel(at, low, high, way, before_ref, res_ref, own_ref, peer_ref, got_ref, out_ref):
    tiles = tiles_of(local_sum(res_ref, own_ref, peer_ref, at, low, high))
    got = decode(got_ref)
    height = tiles[0].shape[0]
    count = got.shape[0] // height
    first = 0 if way == 0 else len(tiles) - count
    for k in range(count):
        tiles[first + k] = tiles[first + k] + got[k * height : (k + 1) * height, :]
    encode(out_ref, tiles)


def near_kernel(at, before_ref, res_ref, own_ref, peer_ref, out_ref):
    out_ref[...] = local_sum(res_ref, own_ref, peer_ref, at, 0, own_ref.shape[2])


def update_kernel(total, low, before_ref, corr_ref, right_ref, left_ref, incl_ref, mean_ref, prior_ref,
                  scale_ref, *rest):
    incl_new_ref, mean_new_ref, effect_ref = rest[-3:]
    height = corr_ref.shape[0]
    right, left = decode(right_ref), decode(left_ref)
    scale = scale_ref[...]
    shrink = scale / (1.0 + scale)
    start = prior_ref[...] - 0.5 * jnp.log1p(scale)
    steep = 0.5 * total * shrink
    halves = [(right, 0), (left, 1)]
    tiles = effect_ref.shape[0] // LANES
    for k in range(tiles):
        corr = corr_ref[:, low + k * LANES : low + (k + 1) * LANES]
        for got, way in halves:
            count = got.shape[0] // height
            first = 0 if way == 0 else tiles - count
            if first <= k < first + count:
                corr = corr + got[(k - first) * height : (k - first + 1) * height, :]
        rows = slice(k * LANES, (k + 1) * LANES)
        incl = incl_ref[rows, :]
        stat = corr.T / total + incl * mean_ref[rows, :]
        mean_new = stat * shrink
        incl_new = 0.5 * incl + 0.5 * jax.nn.sigmoid(start + steep * stat * stat)
        incl_new_ref[rows, :] = incl_new
        mean_new_ref[rows, :] = mean_new
        effect_ref[rows, :] = (incl_new * mean_new).astype(jnp.bfloat16)


def eta_kernel(places, first, before_ref, *refs):
    out_ref, out_other_ref = refs[-2:]
    mine = other = None
    for k, (at, low) in enumerate(places):
        effect_ref, own_ref, peer_ref = refs[3 * k : 3 * k + 3]
        effect = effect_ref[...]
        high = low + effect.shape[0]
        a = jnp.dot(own_ref[at[0], :, low:high], effect, preferred_element_type=jnp.float32)
        b = jnp.dot(peer_ref[at[1], :, low:high], effect, preferred_element_type=jnp.float32)
        mine = a if mine is None else mine + a
        other = b if other is None else other + b
    if not first:
        mine = mine + refs[3 * len(places)][...]
        other = other + refs[3 * len(places) + 1][...]
    out_ref[...] = mine
    out_other_ref[...] = other


def end_kernel(eta_ref, got_ref, labels_ref, offset_ref, out_ref):
    eta = eta_ref[...] + got_ref[...] + offset_ref[...]
    out_ref[...] = 4.0 * (labels_ref[...].astype(jnp.float32) - jax.nn.sigmoid(eta))


def on_device(ring, genotype, residual, labels, incl_old, mean_old, prior_logit, slab_scale, offset):
    n = lax.axis_size("ind")
    people, cols = residual.shape
    total = float(people * n)
    block = incl_old.shape[0]
    size = len(ring)
    reach = size // 2
    pieces = 2 if block % (4 * LANES) == 0 else 1
    part = block // pieces
    f32, bf16 = jnp.float32, jnp.bfloat16
    params = pltpu.CompilerParams(vmem_limit_bytes=VMEM)
    small = pl.CostEstimate(flops=1, bytes_accessed=1, transcendentals=0)
    heavy = pl.CostEstimate(flops=10**10, bytes_accessed=10**6, transcendentals=0)
    longest = pl.CostEstimate(flops=10**11, bytes_accessed=10**6, transcendentals=0)
    light = pl.CostEstimate(flops=2 * 10**9, bytes_accessed=10**6, transcendentals=0)

    swap = [(k, k ^ 1) for k in range(n)]
    right, left = [], []
    for k, chip in enumerate(ring):
        for c in range(2):
            right.append((2 * chip + c, 2 * ring[(k + 1) % size] + c))
            left.append((2 * chip + c, 2 * ring[(k - 1) % size] + c))

    anywhere = pl.BlockSpec(memory_space=pl.ANY)

    def after(before, args):
        return [anywhere] + [pl.BlockSpec()] * len(args)

    def pick(wanted, cost, *before):
        return pl.pallas_call(
            functools.partial(pick_kernel, ring, wanted, block),
            in_specs=[pl.BlockSpec(memory_space=pltpu.HBM)] + [anywhere] * len(before),
            out_specs=[anywhere] * len(wanted),
            out_shape=[
                jax.ShapeDtypeStruct((len(distances), people, block), bf16)
                for distances, _ in wanted
            ],
            scratch_shapes=[pltpu.SemaphoreType.DMA((sum(len(d) for d, _ in wanted),))],
            compiler_params=params,
            cost_estimate=cost,
            name="pick_blocks",
        )(pltpu.with_memory_space_constraint(genotype, pltpu.HBM), *before)

    order = [reach]
    for d in range(reach - 1, 0, -1):
        order += [d, size - d]
    order += [0]
    own, peer = {}, {}

    def swapped(distances, sent):
        got = lax.ppermute(sent, "ind", swap)
        peer.update({d: (got, k) for k, d in enumerate(distances)})

    residual_other = lax.ppermute(residual, "ind", swap)
    (last,) = pick([(order[:1], True)], heavy)
    swapped(order[:1], last)
    next_two, others = order[1:3], order[3:]
    mine, last = pick([(order[:3], False), (next_two, True)], heavy, last)
    own.update({d: (mine, k) for k, d in enumerate(order[:3])})
    swapped(next_two, last)
    res = last = pl.pallas_call(
        flip_kernel,
        in_specs=after(last, (residual, residual_other)),
        out_shape=jax.ShapeDtypeStruct((cols, 2 * people), bf16),
        compiler_params=params,
        cost_estimate=heavy,
        name="flip",
    )(last, residual, residual_other)

    def shape_of(width):
        return jax.ShapeDtypeStruct((width // LANES * cols + PAD, LANES), jnp.int16)

    got = {}
    for d in range(reach, 0, -1):
        for piece in range(pieces):
            low, high = piece * part, (piece + 1) * part
            if d == reach > 1 and piece:
                last, _ = lax.optimization_barrier((last, peer[d - 1][0]))
            if d == reach:
                sent = last = pl.pallas_call(
                    functools.partial(far_kernel, (own[d][1], peer[d][1]), low, high),
                    in_specs=after(last, (res, own[d][0], peer[d][0])),
                    out_shape=[shape_of(part // 2)] * 2,
                    compiler_params=params,
                    cost_estimate=longest,
                    name="sum_far",
                )(last, res, own[d][0], peer[d][0])
                last = sent[0]
                got[0, piece] = lax.ppermute(sent[0], "ind", right)
                got[1, piece] = lax.ppermute(sent[1], "ind", left)
            else:
                for way in (1, 0):
                    w = size - d if way else d
                    args = (res, own[w][0], peer[w][0], got[way, piece])
                    last = pl.pallas_call(
                        functools.partial(
                            hop_kernel, (own[w][1], peer[w][1]), low, high, way
                        ),
                        in_specs=after(last, args),
                        out_shape=shape_of(part),
                        compiler_params=params,
                        cost_estimate=longest,
                        name="sum_hop",
                    )(last, *args)
                    got[way, piece] = lax.ppermute(last, "ind", left if way else right)
            if others and d == max(reach - 1, 1):
                if piece == 0:
                    (last,) = pick([(others, True)], light, last)
                    swapped(others, last)
                if piece == pieces - 1:
                    (last,) = pick([(others, False)], light, last)
                    own.update({w: (last, k) for k, w in enumerate(others)})

    near = last = pl.pallas_call(
        functools.partial(near_kernel, (own[0][1], peer[0][1])),
        in_specs=after(last, (res, own[0], peer[0])),
        out_shape=jax.ShapeDtypeStruct((cols, block), f32),
        compiler_params=params,
        cost_estimate=light,
        name="sum_near",
    )(last, res, own[0][0], peer[0][0])

    prior = prior_logit.reshape(1, cols)
    scale = slab_scale.reshape(1, cols)

    def full(shape):
        return pl.BlockSpec(shape, lambda i: (0,) * len(shape))

    outs = ()
    effects = []
    for piece in range(pieces):
        rows = pl.BlockSpec((part, cols), lambda i, piece=piece: (piece, 0))
        incl_new, mean_new, effect = pl.pallas_call(
            functools.partial(update_kernel, total, piece * part),
            grid=(1,),
            in_specs=[anywhere, full((cols, block))]
            + [full(got[way, piece].shape) for way in range(2)]
            + [rows] * 2
            + [full((1, cols))] * 2
            + [anywhere] * len(outs),
            out_specs=[rows, rows, full((part, cols))],
            out_shape=[
                jax.ShapeDtypeStruct((block, cols), f32),
                jax.ShapeDtypeStruct((block, cols), f32),
                jax.ShapeDtypeStruct((part, cols), bf16),
            ],
            input_output_aliases={8: 0, 9: 1} if outs else {},
            compiler_params=params,
            cost_estimate=light,
            name="update",
        )(last, near, got[0, piece], got[1, piece], incl_old, mean_old, prior, scale, *outs)
        outs = (incl_new, mean_new)
        last = effect
        effects.append(effect)

    eta_shape = jax.ShapeDtypeStruct((people, cols), f32)
    def product(found, eta, before, cost):
        args = [v for d, _, effect in found for v in (effect, own[d][0], peer[d][0])] + list(eta)
        places = [((own[d][1], peer[d][1]), low) for d, low, _ in found]
        return pl.pallas_call(
            functools.partial(eta_kernel, places, not eta),
            in_specs=after(before, args),
            out_shape=[eta_shape] * 2,
            compiler_params=params,
            cost_estimate=cost,
            name="add_eta",
        )(before, *args)

    eta = product([(0, piece * part, effects[piece]) for piece in range(pieces)], (), last, small)
    held = {(way, piece): effects[piece] for way in range(2) for piece in range(pieces)}
    etas = [eta[0]]
    for hop in range(1, reach + 1):
        for piece in range(pieces):
            for way in (1, 0):
                message = held[way, piece]
                if hop > 1:
                    message, _ = lax.optimization_barrier((message, etas[-2 * pieces - 1]))
                low = 0
                if hop == reach:
                    low = way * (part // 2)
                    message = message[low : low + part // 2]
                held[way, piece] = lax.ppermute(message, "ind", left if way else right)
                found = [(hop if way else size - hop, piece * part + low, held[way, piece])]
                eta = product(found, eta, eta[0], small if len(etas) == 1 else light)
                etas.append(eta[0])

    eta_got = lax.ppermute(eta[1], "ind", swap)
    resid_new = pl.pallas_call(
        end_kernel,
        out_shape=eta_shape,
        compiler_params=params,
        cost_estimate=light,
        name="new_residual",
    )(eta[0], eta_got, labels, offset.reshape(1, cols))
    return (outs[0], outs[1], resid_new)


def solution(mesh):
    split = P(("groups", "ind"), None)
    return jax.shard_map(
        functools.partial(on_device, ring_of(mesh.devices)),
        mesh=mesh,
        in_specs=(split, split, split, split, split, P(), P(), P()),
        out_specs=(split, split, split),
        check_vma=False,
    )
```

```python
import functools

import jax
import jax.numpy as jnp
from jax import lax
from jax.experimental import pallas as pl
from jax.experimental.pallas import tpu as pltpu
from jax.sharding import PartitionSpec as P

STEPS = 256.0
TOP = 32700.0
PAD = 16
LANES = 128
VMEM = 14 * 1024 * 1024


def ring_of(devices):
    chips = devices[0, ::2]
    where = [getattr(d, "coords", None) for d in chips]
    count = len(where)
    plain = list(range(count))
    if any(w is None for w in where):
        where = [(0, k % 2, k // 2) for k in plain]
    varying = [k for k in range(3) if len({w[k] for w in where}) > 1]
    if len(varying) != 2:
        return sorted(plain, key=lambda k: tuple(where[k]))
    short, long = sorted(varying, key=lambda k: len({w[k] for w in where}))
    low = min(w[short] for w in where)
    if len({w[short] for w in where}) != 2:
        return plain
    up = sorted((k for k in plain if where[k][short] == low), key=lambda k: where[k][long])
    down = sorted((k for k in plain if where[k][short] != low), key=lambda k: -where[k][long])
    return up + down


def owners_of(ring, distances):
    chip = lax.div(lax.axis_index("ind"), 2)
    spot = jnp.int32(0)
    for k, c in enumerate(ring):
        spot = jnp.where(chip == c, k, spot)
    found = []
    for d in distances:
        at = lax.rem(spot + d, len(ring))
        owner = jnp.int32(ring[0])
        for k, c in enumerate(ring):
            owner = jnp.where(at == k, c, owner)
        found.append(owner)
    return found


def pick_kernel(ring, wanted, block, genotype_ref, *refs):
    outs, sems = refs[-1 - len(wanted) : -1], refs[-1]
    core = lax.rem(lax.axis_index("ind"), 2)
    needed = sorted({d for distances, _ in wanted for d in distances})
    owners = dict(zip(needed, owners_of(ring, needed)))
    copies = []
    for out_ref, (distances, swapped) in zip(outs, wanted):
        parity = 1 - core if swapped else core
        for k, d in enumerate(distances):
            at = pl.multiple_of((2 * owners[d] + parity) * block, LANES)
            copies.append(
                pltpu.make_async_copy(
                    genotype_ref.at[:, pl.ds(at, block)], out_ref.at[k], sems.at[len(copies)]
                )
            )
            copies[-1].start()
    for copy in copies:
        copy.wait()


def flip_kernel(before_ref, mine_ref, other_ref, out_ref):
    people = mine_ref.shape[0]
    out_ref[:, :people] = mine_ref[...].T
    out_ref[:, people:] = other_ref[...].T


def local_sum(res_ref, own_ref, peer_ref, at, low, high):
    people = own_ref.shape[1]
    return jnp.dot(
        res_ref[:, :people], own_ref[at[0], :, low:high], preferred_element_type=jnp.float32
    ) + jnp.dot(
        res_ref[:, people:], peer_ref[at[1], :, low:high], preferred_element_type=jnp.float32
    )


def decode(ref):
    rows = ref.shape[0] - PAD
    code = ref[rows:, :].astype(jnp.float32)[:1, :]
    return ref[:rows, :].astype(jnp.float32) * (jnp.exp2(code * (1.0 / STEPS)) * (1.0 / TOP))


def encode(ref, tiles):
    height = tiles[0].shape[0]
    top = functools.reduce(jnp.maximum, [jnp.abs(t) for t in tiles])
    top = jnp.maximum(jnp.max(top, axis=0, keepdims=True), 1e-30)
    code = jnp.ceil(jnp.log2(top) * STEPS)
    scale = TOP * jnp.exp2(code * (-1.0 / STEPS))
    for k, t in enumerate(tiles):
        ref[k * height : (k + 1) * height, :] = (
            jnp.round(t * scale).astype(jnp.int32).astype(jnp.int16)
        )
    ref[len(tiles) * height :, :] = (
        jnp.broadcast_to(code, (PAD, LANES)).astype(jnp.int32).astype(jnp.int16)
    )


def tiles_of(total):
    return [total[:, k : k + LANES] for k in range(0, total.shape[1], LANES)]


def far_kernel(at, low, high, before_ref, res_ref, own_ref, peer_ref, right_ref, left_ref):
    tiles = tiles_of(local_sum(res_ref, own_ref, peer_ref, at, low, high))
    half = len(tiles) // 2
    encode(right_ref, tiles[:half])
    encode(left_ref, tiles[half:])


def hop_kernel(at, low, high, way, before_ref, res_ref, own_ref, peer_ref, got_ref, out_ref):
    tiles = tiles_of(local_sum(res_ref, own_ref, peer_ref, at, low, high))
    got = decode(got_ref)
    height = tiles[0].shape[0]
    count = got.shape[0] // height
    first = 0 if way == 0 else len(tiles) - count
    for k in range(count):
        tiles[first + k] = tiles[first + k] + got[k * height : (k + 1) * height, :]
    encode(out_ref, tiles)


def near_kernel(at, before_ref, res_ref, own_ref, peer_ref, out_ref):
    out_ref[...] = local_sum(res_ref, own_ref, peer_ref, at, 0, own_ref.shape[2])


def update_kernel(total, low, before_ref, corr_ref, right_ref, left_ref, incl_ref, mean_ref, prior_ref,
                  scale_ref, *rest):
    incl_new_ref, mean_new_ref, effect_ref = rest[-3:]
    height = corr_ref.shape[0]
    right, left = decode(right_ref), decode(left_ref)
    scale = scale_ref[...]
    shrink = scale / (1.0 + scale)
    start = prior_ref[...] - 0.5 * jnp.log1p(scale)
    steep = 0.5 * total * shrink
    halves = [(right, 0), (left, 1)]
    tiles = effect_ref.shape[0] // LANES
    for k in range(tiles):
        corr = corr_ref[:, low + k * LANES : low + (k + 1) * LANES]
        for got, way in halves:
            count = got.shape[0] // height
            first = 0 if way == 0 else tiles - count
            if first <= k < first + count:
                corr = corr + got[(k - first) * height : (k - first + 1) * height, :]
        rows = slice(k * LANES, (k + 1) * LANES)
        incl = incl_ref[rows, :]
        stat = corr.T / total + incl * mean_ref[rows, :]
        mean_new = stat * shrink
        incl_new = 0.5 * incl + 0.5 * jax.nn.sigmoid(start + steep * stat * stat)
        incl_new_ref[rows, :] = incl_new
        mean_new_ref[rows, :] = mean_new
        effect_ref[rows, :] = (incl_new * mean_new).astype(jnp.bfloat16)


def eta_kernel(places, first, before_ref, *refs):
    out_ref, out_other_ref = refs[-2:]
    mine = other = None
    for k, (at, low) in enumerate(places):
        effect_ref, own_ref, peer_ref = refs[3 * k : 3 * k + 3]
        effect = effect_ref[...]
        high = low + effect.shape[0]
        a = jnp.dot(own_ref[at[0], :, low:high], effect, preferred_element_type=jnp.float32)
        b = jnp.dot(peer_ref[at[1], :, low:high], effect, preferred_element_type=jnp.float32)
        mine = a if mine is None else mine + a
        other = b if other is None else other + b
    if not first:
        mine = mine + refs[3 * len(places)][...]
        other = other + refs[3 * len(places) + 1][...]
    out_ref[...] = mine
    out_other_ref[...] = other


def end_kernel(eta_ref, got_ref, labels_ref, offset_ref, out_ref):
    eta = eta_ref[...] + got_ref[...] + offset_ref[...]
    out_ref[...] = 4.0 * (labels_ref[...].astype(jnp.float32) - jax.nn.sigmoid(eta))


def on_device(ring, genotype, residual, labels, incl_old, mean_old, prior_logit, slab_scale, offset):
    n = lax.axis_size("ind")
    people, cols = residual.shape
    total = float(people * n)
    block = incl_old.shape[0]
    size = len(ring)
    reach = size // 2
    pieces = 2 if block % (4 * LANES) == 0 else 1
    part = block // pieces
    f32, bf16 = jnp.float32, jnp.bfloat16
    params = pltpu.CompilerParams(vmem_limit_bytes=VMEM)
    small = pl.CostEstimate(flops=1, bytes_accessed=1, transcendentals=0)
    heavy = pl.CostEstimate(flops=10**10, bytes_accessed=10**6, transcendentals=0)
    longest = pl.CostEstimate(flops=2 * 10**10, bytes_accessed=10**6, transcendentals=0)
    middle = pl.CostEstimate(flops=4 * 10**9, bytes_accessed=10**6, transcendentals=0)
    light = pl.CostEstimate(flops=2 * 10**9, bytes_accessed=10**6, transcendentals=0)

    swap = [(k, k ^ 1) for k in range(n)]
    right, left = [], []
    for k, chip in enumerate(ring):
        for c in range(2):
            right.append((2 * chip + c, 2 * ring[(k + 1) % size] + c))
            left.append((2 * chip + c, 2 * ring[(k - 1) % size] + c))

    anywhere = pl.BlockSpec(memory_space=pl.ANY)

    def after(before, args):
        return [anywhere] + [pl.BlockSpec()] * len(args)

    def pick(wanted, cost, *before):
        return pl.pallas_call(
            functools.partial(pick_kernel, ring, wanted, block),
            in_specs=[pl.BlockSpec(memory_space=pltpu.HBM)] + [anywhere] * len(before),
            out_specs=[anywhere] * len(wanted),
            out_shape=[
                jax.ShapeDtypeStruct((len(distances), people, block), bf16)
                for distances, _ in wanted
            ],
            scratch_shapes=[pltpu.SemaphoreType.DMA((sum(len(d) for d, _ in wanted),))],
            compiler_params=params,
            cost_estimate=cost,
            name="pick_blocks",
        )(pltpu.with_memory_space_constraint(genotype, pltpu.HBM), *before)

    order = [reach]
    for d in range(reach - 1, 0, -1):
        order += [d, size - d]
    order += [0]
    own, peer = {}, {}

    def swapped(distances, sent):
        got = lax.ppermute(sent, "ind", swap)
        peer.update({d: (got, k) for k, d in enumerate(distances)})

    residual_other = lax.ppermute(residual, "ind", swap)
    (last,) = pick([(order[:1], True)], heavy)
    swapped(order[:1], last)
    next_two, others = order[1:3], order[3:]
    mine, last = pick([(order[:3], False), (next_two, True)], heavy, last)
    own.update({d: (mine, k) for k, d in enumerate(order[:3])})
    swapped(next_two, last)
    res = last = pl.pallas_call(
        flip_kernel,
        in_specs=after(last, (residual, residual_other)),
        out_shape=jax.ShapeDtypeStruct((cols, 2 * people), bf16),
        compiler_params=params,
        cost_estimate=heavy,
        name="flip",
    )(last, residual, residual_other)

    def shape_of(width):
        return jax.ShapeDtypeStruct((width // LANES * cols + PAD, LANES), jnp.int16)

    got = {}
    for d in range(reach, 0, -1):
        for piece in range(pieces):
            low, high = piece * part, (piece + 1) * part
            if d == reach > 1 and piece:
                last, _ = lax.optimization_barrier((last, peer[d - 1][0]))
            if d == reach:
                sent = last = pl.pallas_call(
                    functools.partial(far_kernel, (own[d][1], peer[d][1]), low, high),
                    in_specs=after(last, (res, own[d][0], peer[d][0])),
                    out_shape=[shape_of(part // 2)] * 2,
                    compiler_params=params,
                    cost_estimate=longest,
                    name="sum_far",
                )(last, res, own[d][0], peer[d][0])
                last = sent[0]
                got[0, piece] = lax.ppermute(sent[0], "ind", right)
                got[1, piece] = lax.ppermute(sent[1], "ind", left)
            else:
                for way in (1, 0):
                    w = size - d if way else d
                    args = (res, own[w][0], peer[w][0], got[way, piece])
                    last = pl.pallas_call(
                        functools.partial(
                            hop_kernel, (own[w][1], peer[w][1]), low, high, way
                        ),
                        in_specs=after(last, args),
                        out_shape=shape_of(part),
                        compiler_params=params,
                        cost_estimate=longest if d == reach - 1 else middle,
                        name="sum_hop",
                    )(last, *args)
                    got[way, piece] = lax.ppermute(last, "ind", left if way else right)
            if others and d == max(reach - 1, 1):
                if piece == 0:
                    (last,) = pick([(others, True)], light, last)
                    swapped(others, last)
                if piece == pieces - 1:
                    (last,) = pick([(others, False)], light, last)
                    own.update({w: (last, k) for k, w in enumerate(others)})

    near = last = pl.pallas_call(
        functools.partial(near_kernel, (own[0][1], peer[0][1])),
        in_specs=after(last, (res, own[0], peer[0])),
        out_shape=jax.ShapeDtypeStruct((cols, block), f32),
        compiler_params=params,
        cost_estimate=light,
        name="sum_near",
    )(last, res, own[0][0], peer[0][0])

    prior = prior_logit.reshape(1, cols)
    scale = slab_scale.reshape(1, cols)

    def full(shape):
        return pl.BlockSpec(shape, lambda i: (0,) * len(shape))

    outs = ()
    effects = []
    for piece in range(pieces):
        rows = pl.BlockSpec((part, cols), lambda i, piece=piece: (piece, 0))
        incl_new, mean_new, effect = pl.pallas_call(
            functools.partial(update_kernel, total, piece * part),
            grid=(1,),
            in_specs=[anywhere, full((cols, block))]
            + [full(got[way, piece].shape) for way in range(2)]
            + [rows] * 2
            + [full((1, cols))] * 2
            + [anywhere] * len(outs),
            out_specs=[rows, rows, full((part, cols))],
            out_shape=[
                jax.ShapeDtypeStruct((block, cols), f32),
                jax.ShapeDtypeStruct((block, cols), f32),
                jax.ShapeDtypeStruct((part, cols), bf16),
            ],
            input_output_aliases={8: 0, 9: 1} if outs else {},
            compiler_params=params,
            cost_estimate=light,
            name="update",
        )(last, near, got[0, piece], got[1, piece], incl_old, mean_old, prior, scale, *outs)
        outs = (incl_new, mean_new)
        last = effect
        effects.append(effect)

    eta_shape = jax.ShapeDtypeStruct((people, cols), f32)
    def product(found, eta, before, cost):
        args = [v for d, _, effect in found for v in (effect, own[d][0], peer[d][0])] + list(eta)
        places = [((own[d][1], peer[d][1]), low) for d, low, _ in found]
        return pl.pallas_call(
            functools.partial(eta_kernel, places, not eta),
            in_specs=after(before, args),
            out_shape=[eta_shape] * 2,
            compiler_params=params,
            cost_estimate=cost,
            name="add_eta",
        )(before, *args)

    eta = product([(0, piece * part, effects[piece]) for piece in range(pieces)], (), last, small)
    held = {(way, piece): effects[piece] for way in range(2) for piece in range(pieces)}
    etas = [eta[0]]
    for hop in range(1, reach + 1):
        for piece in range(pieces):
            for way in (1, 0):
                message = held[way, piece]
                if hop > 1:
                    message, _ = lax.optimization_barrier((message, etas[-2 * pieces - 1]))
                low = 0
                if hop == reach:
                    low = way * (part // 2)
                    message = message[low : low + part // 2]
                held[way, piece] = lax.ppermute(message, "ind", left if way else right)
                found = [(hop if way else size - hop, piece * part + low, held[way, piece])]
                eta = product(found, eta, eta[0], small if len(etas) == 1 else light)
                etas.append(eta[0])

    eta_got = lax.ppermute(eta[1], "ind", swap)
    resid_new = pl.pallas_call(
        end_kernel,
        out_shape=eta_shape,
        compiler_params=params,
        cost_estimate=light,
        name="new_residual",
    )(eta[0], eta_got, labels, offset.reshape(1, cols))
    return (outs[0], outs[1], resid_new)


def solution(mesh):
    split = P(("groups", "ind"), None)
    return jax.shard_map(
        functools.partial(on_device, ring_of(mesh.devices)),
        mesh=mesh,
        in_specs=(split, split, split, split, split, P(), P(), P()),
        out_specs=(split, split, split),
        check_vma=False,
    )
```

```python
import functools

import jax
import jax.numpy as jnp
from jax import lax
from jax.experimental import pallas as pl
from jax.experimental.pallas import tpu as pltpu
from jax.sharding import PartitionSpec as P

STEPS = 256.0
TOP = 32700.0
PAD = 16
LANES = 128
VMEM = 14 * 1024 * 1024


def ring_of(devices):
    chips = devices[0, ::2]
    where = [getattr(d, "coords", None) for d in chips]
    count = len(where)
    plain = list(range(count))
    if any(w is None for w in where):
        where = [(0, k % 2, k // 2) for k in plain]
    varying = [k for k in range(3) if len({w[k] for w in where}) > 1]
    if len(varying) != 2:
        return sorted(plain, key=lambda k: tuple(where[k]))
    short, long = sorted(varying, key=lambda k: len({w[k] for w in where}))
    low = min(w[short] for w in where)
    if len({w[short] for w in where}) != 2:
        return plain
    up = sorted((k for k in plain if where[k][short] == low), key=lambda k: where[k][long])
    down = sorted((k for k in plain if where[k][short] != low), key=lambda k: -where[k][long])
    return up + down


def owners_of(ring, distances):
    chip = lax.div(lax.axis_index("ind"), 2)
    spot = jnp.int32(0)
    for k, c in enumerate(ring):
        spot = jnp.where(chip == c, k, spot)
    found = []
    for d in distances:
        at = lax.rem(spot + d, len(ring))
        owner = jnp.int32(ring[0])
        for k, c in enumerate(ring):
            owner = jnp.where(at == k, c, owner)
        found.append(owner)
    return found


def pick_kernel(ring, wanted, block, genotype_ref, *refs):
    outs, sems = refs[-1 - len(wanted) : -1], refs[-1]
    other = 1 - lax.rem(lax.axis_index("ind"), 2)
    copies = []
    for out_ref, distances in zip(outs, wanted):
        for k, owner in enumerate(owners_of(ring, distances)):
            at = pl.multiple_of((2 * owner + other) * block, LANES)
            copies.append(
                pltpu.make_async_copy(
                    genotype_ref.at[:, pl.ds(at, block)], out_ref.at[k], sems.at[len(copies)]
                )
            )
            copies[-1].start()
    for copy in copies:
        copy.wait()


def flip_kernel(before_ref, mine_ref, other_ref, out_ref):
    people = mine_ref.shape[0]
    out_ref[:, :people] = mine_ref[...].T
    out_ref[:, people:] = other_ref[...].T


def own_columns(ring, own_ref, peer_ref, d, low, high):
    (owner,) = owners_of(ring, [d])
    block = peer_ref.shape[2]
    at = (2 * owner + lax.rem(lax.axis_index("ind"), 2)) * block + low
    return own_ref[:, pl.ds(pl.multiple_of(at, LANES), high - low)]


def local_sum(ring, res_ref, own_ref, peer_ref, at, low, high):
    people = own_ref.shape[0]
    own = own_columns(ring, own_ref, peer_ref, at[0], low, high)
    return jnp.dot(
        res_ref[:, :people], own, preferred_element_type=jnp.float32
    ) + jnp.dot(
        res_ref[:, people:], peer_ref[at[1], :, low:high], preferred_element_type=jnp.float32
    )


def decode(ref):
    rows = ref.shape[0] - PAD
    code = ref[rows:, :].astype(jnp.float32)[:1, :]
    return ref[:rows, :].astype(jnp.float32) * (jnp.exp2(code * (1.0 / STEPS)) * (1.0 / TOP))


def encode(ref, tiles):
    height = tiles[0].shape[0]
    top = functools.reduce(jnp.maximum, [jnp.abs(t) for t in tiles])
    top = jnp.maximum(jnp.max(top, axis=0, keepdims=True), 1e-30)
    code = jnp.ceil(jnp.log2(top) * STEPS)
    scale = TOP * jnp.exp2(code * (-1.0 / STEPS))
    for k, t in enumerate(tiles):
        ref[k * height : (k + 1) * height, :] = (
            jnp.round(t * scale).astype(jnp.int32).astype(jnp.int16)
        )
    ref[len(tiles) * height :, :] = (
        jnp.broadcast_to(code, (PAD, LANES)).astype(jnp.int32).astype(jnp.int16)
    )


def tiles_of(total):
    return [total[:, k : k + LANES] for k in range(0, total.shape[1], LANES)]


def far_kernel(ring, at, low, high, before_ref, res_ref, own_ref, peer_ref, right_ref, left_ref):
    tiles = tiles_of(local_sum(ring, res_ref, own_ref, peer_ref, at, low, high))
    half = len(tiles) // 2
    encode(right_ref, tiles[:half])
    encode(left_ref, tiles[half:])


def hop_kernel(
    ring, at, low, high, way, before_ref, res_ref, own_ref, peer_ref, got_ref, out_ref
):
    tiles = tiles_of(local_sum(ring, res_ref, own_ref, peer_ref, at, low, high))
    got = decode(got_ref)
    height = tiles[0].shape[0]
    count = got.shape[0] // height
    first = 0 if way == 0 else len(tiles) - count
    for k in range(count):
        tiles[first + k] = tiles[first + k] + got[k * height : (k + 1) * height, :]
    encode(out_ref, tiles)


def near_kernel(ring, at, before_ref, res_ref, own_ref, peer_ref, out_ref):
    out_ref[...] = local_sum(ring, res_ref, own_ref, peer_ref, at, 0, peer_ref.shape[2])


def update_kernel(total, low, before_ref, corr_ref, right_ref, left_ref, incl_ref, mean_ref, prior_ref,
                  scale_ref, *rest):
    incl_new_ref, mean_new_ref, effect_ref = rest[-3:]
    height = corr_ref.shape[0]
    right, left = decode(right_ref), decode(left_ref)
    scale = scale_ref[...]
    shrink = scale / (1.0 + scale)
    start = prior_ref[...] - 0.5 * jnp.log1p(scale)
    steep = 0.5 * total * shrink
    halves = [(right, 0), (left, 1)]
    tiles = effect_ref.shape[0] // LANES
    for k in range(tiles):
        corr = corr_ref[:, low + k * LANES : low + (k + 1) * LANES]
        for got, way in halves:
            count = got.shape[0] // height
            first = 0 if way == 0 else tiles - count
            if first <= k < first + count:
                corr = corr + got[(k - first) * height : (k - first + 1) * height, :]
        rows = slice(k * LANES, (k + 1) * LANES)
        incl = incl_ref[rows, :]
        stat = corr.T / total + incl * mean_ref[rows, :]
        mean_new = stat * shrink
        incl_new = 0.5 * incl + 0.5 * jax.nn.sigmoid(start + steep * stat * stat)
        incl_new_ref[rows, :] = incl_new
        mean_new_ref[rows, :] = mean_new
        effect_ref[rows, :] = (incl_new * mean_new).astype(jnp.bfloat16)


def eta_kernel(ring, places, first, before_ref, *refs):
    out_ref, out_other_ref = refs[-2:]
    mine = other = None
    for k, (at, low) in enumerate(places):
        effect_ref, own_ref, peer_ref = refs[3 * k : 3 * k + 3]
        effect = effect_ref[...]
        high = low + effect.shape[0]
        own = own_columns(ring, own_ref, peer_ref, at[0], low, high)
        a = jnp.dot(own, effect, preferred_element_type=jnp.float32)
        b = jnp.dot(peer_ref[at[1], :, low:high], effect, preferred_element_type=jnp.float32)
        mine = a if mine is None else mine + a
        other = b if other is None else other + b
    if not first:
        mine = mine + refs[3 * len(places)][...]
        other = other + refs[3 * len(places) + 1][...]
    out_ref[...] = mine
    out_other_ref[...] = other


def end_kernel(eta_ref, got_ref, labels_ref, offset_ref, out_ref):
    eta = eta_ref[...] + got_ref[...] + offset_ref[...]
    out_ref[...] = 4.0 * (labels_ref[...].astype(jnp.float32) - jax.nn.sigmoid(eta))


def on_device(ring, genotype, residual, labels, incl_old, mean_old, prior_logit, slab_scale, offset):
    n = lax.axis_size("ind")
    people, cols = residual.shape
    total = float(people * n)
    block = incl_old.shape[0]
    size = len(ring)
    reach = size // 2
    pieces = 2 if block % (4 * LANES) == 0 else 1
    part = block // pieces
    f32, bf16 = jnp.float32, jnp.bfloat16
    params = pltpu.CompilerParams(vmem_limit_bytes=VMEM)
    small = pl.CostEstimate(flops=1, bytes_accessed=1, transcendentals=0)
    heavy = pl.CostEstimate(flops=10**10, bytes_accessed=10**6, transcendentals=0)
    middle = pl.CostEstimate(flops=4 * 10**9, bytes_accessed=10**6, transcendentals=0)
    light = pl.CostEstimate(flops=2 * 10**9, bytes_accessed=10**6, transcendentals=0)

    swap = [(k, k ^ 1) for k in range(n)]
    right, left = [], []
    for k, chip in enumerate(ring):
        for c in range(2):
            right.append((2 * chip + c, 2 * ring[(k + 1) % size] + c))
            left.append((2 * chip + c, 2 * ring[(k - 1) % size] + c))

    anywhere = pl.BlockSpec(memory_space=pl.ANY)

    def after(before, args):
        return [anywhere] + [pl.BlockSpec()] * len(args)

    def pick(wanted, source, cost, *before):
        return pl.pallas_call(
            functools.partial(pick_kernel, ring, wanted, block),
            in_specs=[anywhere] * (1 + len(before)),
            out_specs=[anywhere] * len(wanted),
            out_shape=[
                jax.ShapeDtypeStruct((len(distances), people, block), bf16)
                for distances in wanted
            ],
            scratch_shapes=[pltpu.SemaphoreType.DMA((sum(len(d) for d in wanted),))],
            compiler_params=params,
            cost_estimate=cost,
            name="pick_blocks",
        )(pltpu.with_memory_space_constraint(genotype, source), *before)

    order = [reach]
    for d in range(reach - 1, 0, -1):
        order += [d, size - d]
    order += [0]
    peer = {}

    def swapped(distances, sent):
        got = lax.ppermute(sent, "ind", swap)
        peer.update({d: (got, k) for k, d in enumerate(distances)})

    first, later = [b for b in (order[:1], order[1:3]) if b], [b for b in (order[3:5], order[5:]) if b]
    sent = pick(first, pltpu.HBM, light)
    last = sent[0]
    for distances, array in zip(first, sent):
        swapped(distances, array)
    mine, _ = lax.optimization_barrier((residual, last))
    residual_other = lax.ppermute(mine, "ind", swap)
    res = last = pl.pallas_call(
        flip_kernel,
        in_specs=after(last, (residual, residual_other)),
        out_shape=jax.ShapeDtypeStruct((cols, 2 * people), bf16),
        compiler_params=params,
        cost_estimate=light,
        name="flip",
    )(last, residual, residual_other)

    def shape_of(width):
        return jax.ShapeDtypeStruct((width // LANES * cols + PAD, LANES), jnp.int16)

    got = {}
    for d in range(reach, 0, -1):
        for piece in range(pieces):
            low, high = piece * part, (piece + 1) * part
            if d == reach > 1 and piece:
                last, _ = lax.optimization_barrier((last, peer[d - 1][0]))
            if d == reach:
                sent = last = pl.pallas_call(
                    functools.partial(far_kernel, ring, (d, peer[d][1]), low, high),
                    in_specs=after(last, (res, genotype, peer[d][0])),
                    out_shape=[shape_of(part // 2)] * 2,
                    compiler_params=params,
                    cost_estimate=heavy,
                    name="sum_far",
                )(last, res, genotype, peer[d][0])
                last = sent[0]
                got[0, piece] = lax.ppermute(sent[0], "ind", right)
                got[1, piece] = lax.ppermute(sent[1], "ind", left)
            else:
                if d == reach - 1 > 1 and piece == pieces - 1:
                    last, _ = lax.optimization_barrier((last, peer[d - 1][0]))
                for way in (1, 0):
                    w = size - d if way else d
                    args = (res, genotype, peer[w][0], got[way, piece])
                    last = pl.pallas_call(
                        functools.partial(
                            hop_kernel, ring, (w, peer[w][1]), low, high, way
                        ),
                        in_specs=after(last, args),
                        out_shape=shape_of(part),
                        compiler_params=params,
                        cost_estimate=heavy if d == reach - 1 else middle,
                        name="sum_hop",
                    )(last, *args)
                    got[way, piece] = lax.ppermute(last, "ind", left if way else right)
            if later and (d, piece) in ((reach, pieces - 1), (reach - 1, 0)):
                distances = later.pop(0)
                (last,) = pick([distances], pltpu.VMEM, light, last)
                swapped(distances, last)

    near = last = pl.pallas_call(
        functools.partial(near_kernel, ring, (0, peer[0][1])),
        in_specs=after(last, (res, genotype, peer[0][0])),
        out_shape=jax.ShapeDtypeStruct((cols, block), f32),
        compiler_params=params,
        cost_estimate=light,
        name="sum_near",
    )(last, res, genotype, peer[0][0])

    prior = prior_logit.reshape(1, cols)
    scale = slab_scale.reshape(1, cols)

    def full(shape):
        return pl.BlockSpec(shape, lambda i: (0,) * len(shape))

    outs = ()
    effects = []
    for piece in range(pieces):
        rows = pl.BlockSpec((part, cols), lambda i, piece=piece: (piece, 0))
        incl_new, mean_new, effect = pl.pallas_call(
            functools.partial(update_kernel, total, piece * part),
            grid=(1,),
            in_specs=[anywhere, full((cols, block))]
            + [full(got[way, piece].shape) for way in range(2)]
            + [rows] * 2
            + [full((1, cols))] * 2
            + [anywhere] * len(outs),
            out_specs=[rows, rows, full((part, cols))],
            out_shape=[
                jax.ShapeDtypeStruct((block, cols), f32),
                jax.ShapeDtypeStruct((block, cols), f32),
                jax.ShapeDtypeStruct((part, cols), bf16),
            ],
            input_output_aliases={8: 0, 9: 1} if outs else {},
            compiler_params=params,
            cost_estimate=light,
            name="update",
        )(last, near, got[0, piece], got[1, piece], incl_old, mean_old, prior, scale, *outs)
        outs = (incl_new, mean_new)
        last = effect
        effects.append(effect)

    eta_shape = jax.ShapeDtypeStruct((people, cols), f32)
    def product(found, eta, before, cost):
        args = [v for d, _, effect in found for v in (effect, genotype, peer[d][0])] + list(eta)
        places = [((d, peer[d][1]), low) for d, low, _ in found]
        return pl.pallas_call(
            functools.partial(eta_kernel, ring, places, not eta),
            in_specs=after(before, args),
            out_shape=[eta_shape] * 2,
            compiler_params=params,
            cost_estimate=cost,
            name="add_eta",
        )(before, *args)

    eta = product([(0, piece * part, effects[piece]) for piece in range(pieces)], (), last, small)
    held = {(way, piece): effects[piece] for way in range(2) for piece in range(pieces)}
    etas = [eta[0]]
    for hop in range(1, reach + 1):
        for piece in range(pieces):
            for way in (1, 0):
                message = held[way, piece]
                if hop > 1:
                    message, _ = lax.optimization_barrier((message, etas[-2 * pieces - 1]))
                low = 0
                if hop == reach:
                    low = way * (part // 2)
                    message = message[low : low + part // 2]
                held[way, piece] = lax.ppermute(message, "ind", left if way else right)
                found = [(hop if way else size - hop, piece * part + low, held[way, piece])]
                eta = product(found, eta, eta[0], small if len(etas) == 1 else light)
                etas.append(eta[0])

    eta_got = lax.ppermute(eta[1], "ind", swap)
    resid_new = pl.pallas_call(
        end_kernel,
        out_shape=eta_shape,
        compiler_params=params,
        cost_estimate=light,
        name="new_residual",
    )(eta[0], eta_got, labels, offset.reshape(1, cols))
    return (outs[0], outs[1], resid_new)


def solution(mesh):
    split = P(("groups", "ind"), None)
    return jax.shard_map(
        functools.partial(on_device, ring_of(mesh.devices)),
        mesh=mesh,
        in_specs=(split, split, split, split, split, P(), P(), P()),
        out_specs=(split, split, split),
        check_vma=False,
    )
```

```python
import functools

import jax
import jax.numpy as jnp
from jax import lax
from jax.experimental import pallas as pl
from jax.experimental.pallas import tpu as pltpu
from jax.sharding import PartitionSpec as P

STEPS = 256.0
TOP = 32700.0
PAD = 16
LANES = 128
VMEM = 14 * 1024 * 1024


def ring_of(devices):
    chips = devices[0, ::2]
    where = [getattr(d, "coords", None) for d in chips]
    count = len(where)
    plain = list(range(count))
    if any(w is None for w in where):
        where = [(0, k % 2, k // 2) for k in plain]
    varying = [k for k in range(3) if len({w[k] for w in where}) > 1]
    if len(varying) != 2:
        return sorted(plain, key=lambda k: tuple(where[k]))
    short, long = sorted(varying, key=lambda k: len({w[k] for w in where}))
    low = min(w[short] for w in where)
    if len({w[short] for w in where}) != 2:
        return plain
    up = sorted((k for k in plain if where[k][short] == low), key=lambda k: where[k][long])
    down = sorted((k for k in plain if where[k][short] != low), key=lambda k: -where[k][long])
    return up + down


def owners_of(ring, distances):
    chip = lax.div(lax.axis_index("ind"), 2)
    spot = jnp.int32(0)
    for k, c in enumerate(ring):
        spot = jnp.where(chip == c, k, spot)
    found = []
    for d in distances:
        at = lax.rem(spot + d, len(ring))
        owner = jnp.int32(ring[0])
        for k, c in enumerate(ring):
            owner = jnp.where(at == k, c, owner)
        found.append(owner)
    return found


def pick_kernel(ring, wanted, block, genotype_ref, *refs):
    outs, sems = refs[-1 - len(wanted) : -1], refs[-1]
    other = 1 - lax.rem(lax.axis_index("ind"), 2)
    copies = []
    for out_ref, distances in zip(outs, wanted):
        for k, owner in enumerate(owners_of(ring, distances)):
            at = pl.multiple_of((2 * owner + other) * block, LANES)
            copies.append(
                pltpu.make_async_copy(
                    genotype_ref.at[:, pl.ds(at, block)], out_ref.at[k], sems.at[len(copies)]
                )
            )
            copies[-1].start()
    for copy in copies:
        copy.wait()


def flip_kernel(before_ref, mine_ref, other_ref, out_ref):
    people = mine_ref.shape[0]
    out_ref[:, :people] = mine_ref[...].T
    out_ref[:, people:] = other_ref[...].T


def own_columns(ring, own_ref, peer_ref, d, low, high):
    (owner,) = owners_of(ring, [d])
    block = peer_ref.shape[2]
    at = (2 * owner + lax.rem(lax.axis_index("ind"), 2)) * block + low
    return own_ref[:, pl.ds(pl.multiple_of(at, LANES), high - low)]


def local_sum(ring, res_ref, own_ref, peer_ref, at, low, high):
    people = own_ref.shape[0]
    own = own_columns(ring, own_ref, peer_ref, at[0], low, high)
    return jnp.dot(
        res_ref[:, :people], own, preferred_element_type=jnp.float32
    ) + jnp.dot(
        res_ref[:, people:], peer_ref[at[1], :, low:high], preferred_element_type=jnp.float32
    )


def decode(ref):
    rows = ref.shape[0] - PAD
    code = ref[rows:, :].astype(jnp.float32)[:1, :]
    return ref[:rows, :].astype(jnp.float32) * (jnp.exp2(code * (1.0 / STEPS)) * (1.0 / TOP))


def encode(ref, tiles):
    height = tiles[0].shape[0]
    top = functools.reduce(jnp.maximum, [jnp.abs(t) for t in tiles])
    top = jnp.maximum(jnp.max(top, axis=0, keepdims=True), 1e-30)
    code = jnp.ceil(jnp.log2(top) * STEPS)
    scale = TOP * jnp.exp2(code * (-1.0 / STEPS))
    for k, t in enumerate(tiles):
        ref[k * height : (k + 1) * height, :] = (
            jnp.round(t * scale).astype(jnp.int32).astype(jnp.int16)
        )
    ref[len(tiles) * height :, :] = (
        jnp.broadcast_to(code, (PAD, LANES)).astype(jnp.int32).astype(jnp.int16)
    )


def tiles_of(total):
    return [total[:, k : k + LANES] for k in range(0, total.shape[1], LANES)]


def far_kernel(ring, at, low, high, before_ref, res_ref, own_ref, peer_ref, right_ref, left_ref):
    tiles = tiles_of(local_sum(ring, res_ref, own_ref, peer_ref, at, low, high))
    half = len(tiles) // 2
    encode(right_ref, tiles[:half])
    encode(left_ref, tiles[half:])


def hop_kernel(
    ring, at, low, high, way, before_ref, res_ref, own_ref, peer_ref, got_ref, out_ref
):
    tiles = tiles_of(local_sum(ring, res_ref, own_ref, peer_ref, at, low, high))
    got = decode(got_ref)
    height = tiles[0].shape[0]
    count = got.shape[0] // height
    first = 0 if way == 0 else len(tiles) - count
    for k in range(count):
        tiles[first + k] = tiles[first + k] + got[k * height : (k + 1) * height, :]
    encode(out_ref, tiles)


def near_kernel(ring, at, before_ref, res_ref, own_ref, peer_ref, out_ref):
    out_ref[...] = local_sum(ring, res_ref, own_ref, peer_ref, at, 0, peer_ref.shape[2])


def update_kernel(total, low, before_ref, corr_ref, right_ref, left_ref, incl_ref, mean_ref, prior_ref,
                  scale_ref, *rest):
    incl_new_ref, mean_new_ref, effect_ref = rest[-3:]
    height = corr_ref.shape[0]
    right, left = decode(right_ref), decode(left_ref)
    scale = scale_ref[...]
    shrink = scale / (1.0 + scale)
    start = prior_ref[...] - 0.5 * jnp.log1p(scale)
    steep = 0.5 * total * shrink
    halves = [(right, 0), (left, 1)]
    tiles = effect_ref.shape[0] // LANES
    for k in range(tiles):
        corr = corr_ref[:, low + k * LANES : low + (k + 1) * LANES]
        for got, way in halves:
            count = got.shape[0] // height
            first = 0 if way == 0 else tiles - count
            if first <= k < first + count:
                corr = corr + got[(k - first) * height : (k - first + 1) * height, :]
        rows = slice(k * LANES, (k + 1) * LANES)
        incl = incl_ref[rows, :]
        stat = corr.T / total + incl * mean_ref[rows, :]
        mean_new = stat * shrink
        incl_new = 0.5 * incl + 0.5 * jax.nn.sigmoid(start + steep * stat * stat)
        incl_new_ref[rows, :] = incl_new
        mean_new_ref[rows, :] = mean_new
        effect_ref[rows, :] = (incl_new * mean_new).astype(jnp.bfloat16)


def eta_kernel(ring, places, first, before_ref, *refs):
    out_ref, out_other_ref = refs[-2:]
    mine = other = None
    for k, (at, low) in enumerate(places):
        effect_ref, own_ref, peer_ref = refs[3 * k : 3 * k + 3]
        effect = effect_ref[...]
        high = low + effect.shape[0]
        own = own_columns(ring, own_ref, peer_ref, at[0], low, high)
        a = jnp.dot(own, effect, preferred_element_type=jnp.float32)
        b = jnp.dot(peer_ref[at[1], :, low:high], effect, preferred_element_type=jnp.float32)
        mine = a if mine is None else mine + a
        other = b if other is None else other + b
    if not first:
        mine = mine + refs[3 * len(places)][...]
        other = other + refs[3 * len(places) + 1][...]
    out_ref[...] = mine
    out_other_ref[...] = other


def end_kernel(eta_ref, got_ref, labels_ref, offset_ref, out_ref):
    eta = eta_ref[...] + got_ref[...] + offset_ref[...]
    out_ref[...] = 4.0 * (labels_ref[...].astype(jnp.float32) - jax.nn.sigmoid(eta))


def on_device(ring, genotype, residual, labels, incl_old, mean_old, prior_logit, slab_scale, offset):
    n = lax.axis_size("ind")
    people, cols = residual.shape
    total = float(people * n)
    block = incl_old.shape[0]
    size = len(ring)
    reach = size // 2
    pieces = 2 if block % (4 * LANES) == 0 else 1
    part = block // pieces
    f32, bf16 = jnp.float32, jnp.bfloat16
    params = pltpu.CompilerParams(vmem_limit_bytes=VMEM)
    small = pl.CostEstimate(flops=1, bytes_accessed=1, transcendentals=0)
    heavy = pl.CostEstimate(flops=10**10, bytes_accessed=10**6, transcendentals=0)
    middle = pl.CostEstimate(flops=4 * 10**9, bytes_accessed=10**6, transcendentals=0)
    light = pl.CostEstimate(flops=2 * 10**9, bytes_accessed=10**6, transcendentals=0)

    swap = [(k, k ^ 1) for k in range(n)]
    right, left = [], []
    for k, chip in enumerate(ring):
        for c in range(2):
            right.append((2 * chip + c, 2 * ring[(k + 1) % size] + c))
            left.append((2 * chip + c, 2 * ring[(k - 1) % size] + c))

    anywhere = pl.BlockSpec(memory_space=pl.ANY)

    def after(before, args):
        return [anywhere] + [pl.BlockSpec()] * len(args)

    def pick(wanted, source, cost, *before):
        return pl.pallas_call(
            functools.partial(pick_kernel, ring, wanted, block),
            in_specs=[anywhere] * (1 + len(before)),
            out_specs=[anywhere] * len(wanted),
            out_shape=[
                jax.ShapeDtypeStruct((len(distances), people, block), bf16)
                for distances in wanted
            ],
            scratch_shapes=[pltpu.SemaphoreType.DMA((sum(len(d) for d in wanted),))],
            compiler_params=params,
            cost_estimate=cost,
            name="pick_blocks",
        )(pltpu.with_memory_space_constraint(genotype, source), *before)

    order = [reach]
    for d in range(reach - 1, 0, -1):
        order += [d, size - d]
    order += [0]
    peer = {}

    def swapped(distances, sent):
        got = lax.ppermute(sent, "ind", swap)
        peer.update({d: (got, k) for k, d in enumerate(distances)})

    later = [b for b in (order[3:5], order[5:]) if b]
    residual_other = lax.ppermute(residual, "ind", swap)
    (last,) = pick([order[:1]], pltpu.HBM, light)
    swapped(order[:1], last)
    res = last = pl.pallas_call(
        flip_kernel,
        in_specs=after(last, (residual, residual_other)),
        out_shape=jax.ShapeDtypeStruct((cols, 2 * people), bf16),
        compiler_params=params,
        cost_estimate=light,
        name="flip",
    )(last, residual, residual_other)

    if order[1:3]:
        (last,) = pick([order[1:3]], pltpu.VMEM, light, last)
        swapped(order[1:3], last)

    def shape_of(width):
        return jax.ShapeDtypeStruct((width // LANES * cols + PAD, LANES), jnp.int16)

    got = {}
    for d in range(reach, 0, -1):
        for piece in range(pieces):
            low, high = piece * part, (piece + 1) * part
            if d == reach > 1 and piece:
                last, _ = lax.optimization_barrier((last, peer[d - 1][0]))
            if d == reach:
                sent = last = pl.pallas_call(
                    functools.partial(far_kernel, ring, (d, peer[d][1]), low, high),
                    in_specs=after(last, (res, genotype, peer[d][0])),
                    out_shape=[shape_of(part // 2)] * 2,
                    compiler_params=params,
                    cost_estimate=heavy,
                    name="sum_far",
                )(last, res, genotype, peer[d][0])
                last = sent[0]
                got[0, piece] = lax.ppermute(sent[0], "ind", right)
                got[1, piece] = lax.ppermute(sent[1], "ind", left)
            else:
                if d == reach - 1 > 1 and piece == pieces - 1:
                    last, _ = lax.optimization_barrier((last, peer[d - 1][0]))
                for way in (1, 0):
                    w = size - d if way else d
                    args = (res, genotype, peer[w][0], got[way, piece])
                    last = pl.pallas_call(
                        functools.partial(
                            hop_kernel, ring, (w, peer[w][1]), low, high, way
                        ),
                        in_specs=after(last, args),
                        out_shape=shape_of(part),
                        compiler_params=params,
                        cost_estimate=heavy if d == reach - 1 else middle,
                        name="sum_hop",
                    )(last, *args)
                    got[way, piece] = lax.ppermute(last, "ind", left if way else right)
            if later and (d, piece) in ((reach, pieces - 1), (reach - 1, 0)):
                distances = later.pop(0)
                (last,) = pick([distances], pltpu.VMEM, light, last)
                swapped(distances, last)

    near = last = pl.pallas_call(
        functools.partial(near_kernel, ring, (0, peer[0][1])),
        in_specs=after(last, (res, genotype, peer[0][0])),
        out_shape=jax.ShapeDtypeStruct((cols, block), f32),
        compiler_params=params,
        cost_estimate=light,
        name="sum_near",
    )(last, res, genotype, peer[0][0])

    prior = prior_logit.reshape(1, cols)
    scale = slab_scale.reshape(1, cols)

    def full(shape):
        return pl.BlockSpec(shape, lambda i: (0,) * len(shape))

    outs = ()
    effects = []
    for piece in range(pieces):
        rows = pl.BlockSpec((part, cols), lambda i, piece=piece: (piece, 0))
        incl_new, mean_new, effect = pl.pallas_call(
            functools.partial(update_kernel, total, piece * part),
            grid=(1,),
            in_specs=[anywhere, full((cols, block))]
            + [full(got[way, piece].shape) for way in range(2)]
            + [rows] * 2
            + [full((1, cols))] * 2
            + [anywhere] * len(outs),
            out_specs=[rows, rows, full((part, cols))],
            out_shape=[
                jax.ShapeDtypeStruct((block, cols), f32),
                jax.ShapeDtypeStruct((block, cols), f32),
                jax.ShapeDtypeStruct((part, cols), bf16),
            ],
            input_output_aliases={8: 0, 9: 1} if outs else {},
            compiler_params=params,
            cost_estimate=light,
            name="update",
        )(last, near, got[0, piece], got[1, piece], incl_old, mean_old, prior, scale, *outs)
        outs = (incl_new, mean_new)
        last = effect
        effects.append(effect)

    eta_shape = jax.ShapeDtypeStruct((people, cols), f32)
    def product(found, eta, before, cost):
        args = [v for d, _, effect in found for v in (effect, genotype, peer[d][0])] + list(eta)
        places = [((d, peer[d][1]), low) for d, low, _ in found]
        return pl.pallas_call(
            functools.partial(eta_kernel, ring, places, not eta),
            in_specs=after(before, args),
            out_shape=[eta_shape] * 2,
            compiler_params=params,
            cost_estimate=cost,
            name="add_eta",
        )(before, *args)

    eta = product([(0, piece * part, effects[piece]) for piece in range(pieces)], (), last, small)
    held = {(way, piece): effects[piece] for way in range(2) for piece in range(pieces)}
    etas = [eta[0]]
    for hop in range(1, reach + 1):
        for piece in range(pieces):
            for way in (1, 0):
                message = held[way, piece]
                if hop > 1:
                    message, _ = lax.optimization_barrier((message, etas[-2 * pieces - 1]))
                low = 0
                if hop == reach:
                    low = way * (part // 2)
                    message = message[low : low + part // 2]
                held[way, piece] = lax.ppermute(message, "ind", left if way else right)
                found = [(hop if way else size - hop, piece * part + low, held[way, piece])]
                eta = product(found, eta, eta[0], small if len(etas) == 1 else light)
                etas.append(eta[0])

    eta_got = lax.ppermute(eta[1], "ind", swap)
    resid_new = pl.pallas_call(
        end_kernel,
        out_shape=eta_shape,
        compiler_params=params,
        cost_estimate=light,
        name="new_residual",
    )(eta[0], eta_got, labels, offset.reshape(1, cols))
    return (outs[0], outs[1], resid_new)


def solution(mesh):
    split = P(("groups", "ind"), None)
    return jax.shard_map(
        functools.partial(on_device, ring_of(mesh.devices)),
        mesh=mesh,
        in_specs=(split, split, split, split, split, P(), P(), P()),
        out_specs=(split, split, split),
        check_vma=False,
    )
```

```python
import functools

import jax
import jax.numpy as jnp
from jax import lax
from jax.experimental import pallas as pl
from jax.experimental.pallas import tpu as pltpu
from jax.sharding import PartitionSpec as P

STEPS = 256.0
TOP = 32700.0
PAD = 16
LANES = 128
VMEM = 14 * 1024 * 1024


def ring_of(devices):
    chips = devices[0, ::2]
    where = [getattr(d, "coords", None) for d in chips]
    count = len(where)
    plain = list(range(count))
    if any(w is None for w in where):
        where = [(0, k % 2, k // 2) for k in plain]
    varying = [k for k in range(3) if len({w[k] for w in where}) > 1]
    if len(varying) != 2:
        return sorted(plain, key=lambda k: tuple(where[k]))
    short, long = sorted(varying, key=lambda k: len({w[k] for w in where}))
    low = min(w[short] for w in where)
    if len({w[short] for w in where}) != 2:
        return plain
    up = sorted((k for k in plain if where[k][short] == low), key=lambda k: where[k][long])
    down = sorted((k for k in plain if where[k][short] != low), key=lambda k: -where[k][long])
    return up + down


def owners_of(ring, distances):
    chip = lax.div(lax.axis_index("ind"), 2)
    spot = jnp.int32(0)
    for k, c in enumerate(ring):
        spot = jnp.where(chip == c, k, spot)
    found = []
    for d in distances:
        at = lax.rem(spot + d, len(ring))
        owner = jnp.int32(ring[0])
        for k, c in enumerate(ring):
            owner = jnp.where(at == k, c, owner)
        found.append(owner)
    return found


def pick_kernel(ring, wanted, block, genotype_ref, *refs):
    outs, sems = refs[-1 - len(wanted) : -1], refs[-1]
    core = lax.rem(lax.axis_index("ind"), 2)
    copies = []
    for out_ref, (distances, swapped, low, _) in zip(outs, wanted):
        parity = 1 - core if swapped else core
        width = out_ref.shape[2]
        for k, owner in enumerate(owners_of(ring, distances)):
            at = pl.multiple_of((2 * owner + parity) * block + low, LANES)
            copies.append(
                pltpu.make_async_copy(
                    genotype_ref.at[:, pl.ds(at, width)], out_ref.at[k], sems.at[len(copies)]
                )
            )
            copies[-1].start()
    for copy in copies:
        copy.wait()


def flip_kernel(before_ref, mine_ref, other_ref, out_ref):
    people = mine_ref.shape[0]
    out_ref[:, :people] = mine_ref[...].T
    out_ref[:, people:] = other_ref[...].T


def own_columns(ring, own_ref, d, low, high):
    (owner,) = owners_of(ring, [d])
    block = own_ref.shape[1] // (2 * len(ring))
    at = (2 * owner + lax.rem(lax.axis_index("ind"), 2)) * block + low
    return own_ref[:, pl.ds(pl.multiple_of(at, LANES), high - low)]


def local_sum(res_ref, own, other):
    people = own.shape[0]
    return jnp.dot(
        res_ref[:, :people], own, preferred_element_type=jnp.float32
    ) + jnp.dot(res_ref[:, people:], other, preferred_element_type=jnp.float32)


def decode(ref):
    rows = ref.shape[0] - PAD
    code = ref[rows:, :].astype(jnp.float32)[:1, :]
    return ref[:rows, :].astype(jnp.float32) * (jnp.exp2(code * (1.0 / STEPS)) * (1.0 / TOP))


def encode(ref, tiles):
    height = tiles[0].shape[0]
    top = functools.reduce(jnp.maximum, [jnp.abs(t) for t in tiles])
    top = jnp.maximum(jnp.max(top, axis=0, keepdims=True), 1e-30)
    code = jnp.ceil(jnp.log2(top) * STEPS)
    scale = TOP * jnp.exp2(code * (-1.0 / STEPS))
    for k, t in enumerate(tiles):
        ref[k * height : (k + 1) * height, :] = (
            jnp.round(t * scale).astype(jnp.int32).astype(jnp.int16)
        )
    ref[len(tiles) * height :, :] = (
        jnp.broadcast_to(code, (PAD, LANES)).astype(jnp.int32).astype(jnp.int16)
    )


def tiles_of(total):
    return [total[:, k : k + LANES] for k in range(0, total.shape[1], LANES)]


def far_kernel(before_ref, res_ref, own_ref, peer_ref, right_ref, left_ref):
    tiles = tiles_of(local_sum(res_ref, own_ref[0], peer_ref[0]))
    half = len(tiles) // 2
    encode(right_ref, tiles[:half])
    encode(left_ref, tiles[half:])


def hop_kernel(
    ring, at, low, high, way, before_ref, res_ref, own_ref, peer_ref, got_ref, out_ref
):
    own = own_columns(ring, own_ref, at[0], low, high)
    tiles = tiles_of(local_sum(res_ref, own, peer_ref[at[1], :, low:high]))
    got = decode(got_ref)
    height = tiles[0].shape[0]
    count = got.shape[0] // height
    first = 0 if way == 0 else len(tiles) - count
    for k in range(count):
        tiles[first + k] = tiles[first + k] + got[k * height : (k + 1) * height, :]
    encode(out_ref, tiles)


def near_kernel(ring, at, before_ref, res_ref, own_ref, peer_ref, out_ref):
    own = own_columns(ring, own_ref, at[0], 0, peer_ref.shape[2])
    out_ref[...] = local_sum(res_ref, own, peer_ref[at[1]])


def update_kernel(total, low, before_ref, corr_ref, right_ref, left_ref, incl_ref, mean_ref, prior_ref,
                  scale_ref, *rest):
    incl_new_ref, mean_new_ref, effect_ref = rest[-3:]
    height = corr_ref.shape[0]
    right, left = decode(right_ref), decode(left_ref)
    scale = scale_ref[...]
    shrink = scale / (1.0 + scale)
    start = prior_ref[...] - 0.5 * jnp.log1p(scale)
    steep = 0.5 * total * shrink
    halves = [(right, 0), (left, 1)]
    tiles = effect_ref.shape[0] // LANES
    for k in range(tiles):
        corr = corr_ref[:, low + k * LANES : low + (k + 1) * LANES]
        for got, way in halves:
            count = got.shape[0] // height
            first = 0 if way == 0 else tiles - count
            if first <= k < first + count:
                corr = corr + got[(k - first) * height : (k - first + 1) * height, :]
        rows = slice(k * LANES, (k + 1) * LANES)
        incl = incl_ref[rows, :]
        stat = corr.T / total + incl * mean_ref[rows, :]
        mean_new = stat * shrink
        incl_new = 0.5 * incl + 0.5 * jax.nn.sigmoid(start + steep * stat * stat)
        incl_new_ref[rows, :] = incl_new
        mean_new_ref[rows, :] = mean_new
        effect_ref[rows, :] = (incl_new * mean_new).astype(jnp.bfloat16)


def eta_kernel(ring, places, first, before_ref, *refs):
    out_ref, out_other_ref = refs[-2:]
    mine = other = None
    for k, (at, low) in enumerate(places):
        effect_ref, own_ref, peer_ref = refs[3 * k : 3 * k + 3]
        effect = effect_ref[...]
        high = low + effect.shape[0]
        own = own_columns(ring, own_ref, at[0], low, high)
        a = jnp.dot(own, effect, preferred_element_type=jnp.float32)
        b = jnp.dot(peer_ref[at[1], :, low - at[2] : high - at[2]], effect, preferred_element_type=jnp.float32)
        mine = a if mine is None else mine + a
        other = b if other is None else other + b
    if not first:
        mine = mine + refs[3 * len(places)][...]
        other = other + refs[3 * len(places) + 1][...]
    out_ref[...] = mine
    out_other_ref[...] = other


def end_kernel(eta_ref, got_ref, labels_ref, offset_ref, out_ref):
    eta = eta_ref[...] + got_ref[...] + offset_ref[...]
    out_ref[...] = 4.0 * (labels_ref[...].astype(jnp.float32) - jax.nn.sigmoid(eta))


def on_device(ring, genotype, residual, labels, incl_old, mean_old, prior_logit, slab_scale, offset):
    n = lax.axis_size("ind")
    people, cols = residual.shape
    total = float(people * n)
    block = incl_old.shape[0]
    size = len(ring)
    reach = size // 2
    pieces = 2 if block % (4 * LANES) == 0 else 1
    part = block // pieces
    f32, bf16 = jnp.float32, jnp.bfloat16
    params = pltpu.CompilerParams(vmem_limit_bytes=VMEM)
    small = pl.CostEstimate(flops=1, bytes_accessed=1, transcendentals=0)
    longest = pl.CostEstimate(flops=25 * 10**9, bytes_accessed=10**6, transcendentals=0)
    heavy = pl.CostEstimate(flops=10**10, bytes_accessed=10**6, transcendentals=0)
    middle = pl.CostEstimate(flops=4 * 10**9, bytes_accessed=10**6, transcendentals=0)
    light = pl.CostEstimate(flops=2 * 10**9, bytes_accessed=10**6, transcendentals=0)

    swap = [(k, k ^ 1) for k in range(n)]
    right, left = [], []
    for k, chip in enumerate(ring):
        for c in range(2):
            right.append((2 * chip + c, 2 * ring[(k + 1) % size] + c))
            left.append((2 * chip + c, 2 * ring[(k - 1) % size] + c))

    anywhere = pl.BlockSpec(memory_space=pl.ANY)

    def after(before, args):
        return [anywhere] + [pl.BlockSpec()] * len(args)

    def pick(wanted, source, cost, *before):
        return pl.pallas_call(
            functools.partial(pick_kernel, ring, wanted, block),
            in_specs=[anywhere] * (1 + len(before)),
            out_specs=[anywhere] * len(wanted),
            out_shape=[
                jax.ShapeDtypeStruct((len(distances), people, width), bf16)
                for distances, _, _, width in wanted
            ],
            scratch_shapes=[pltpu.SemaphoreType.DMA((sum(len(w[0]) for w in wanted),))],
            compiler_params=params,
            cost_estimate=cost,
            name="pick_blocks",
        )(pltpu.with_memory_space_constraint(genotype, source), *before)

    order = [reach]
    for d in range(reach - 1, 0, -1):
        order += [d, size - d]
    order += [0]
    peer, own_far, peer_far = {}, {}, {}

    def swapped(distances, sent):
        got = lax.ppermute(sent, "ind", swap)
        peer.update({d: (got, k, 0) for k, d in enumerate(distances)})

    def far(piece):
        return [(order[:1], True, piece * part, part), (order[:1], False, piece * part, part)]

    def whole(distances):
        return [(distances, True, 0, block)] if distances else []

    later = [b for b in (order[3:5], order[5:]) if b]
    last, own_far[0] = pick(far(0), pltpu.HBM, small)
    peer_far[0] = lax.ppermute(last, "ind", swap)
    mine, _ = lax.optimization_barrier((residual, last))
    residual_other = lax.ppermute(mine, "ind", swap)
    wanted = (far(1) if pieces > 1 else []) + whole(order[1:3])
    if wanted:
        found = pick(wanted, pltpu.HBM, heavy, last)
        last = found[0]
        if pieces > 1:
            peer_far[1], own_far[1] = lax.ppermute(found[0], "ind", swap), found[1]
        if order[1:3]:
            swapped(order[1:3], found[-1])
    res = last = pl.pallas_call(
        flip_kernel,
        in_specs=after(last, (residual, residual_other)),
        out_shape=jax.ShapeDtypeStruct((cols, 2 * people), bf16),
        compiler_params=params,
        cost_estimate=small,
        name="flip",
    )(last, residual, residual_other)

    def shape_of(width):
        return jax.ShapeDtypeStruct((width // LANES * cols + PAD, LANES), jnp.int16)

    got = {}
    for d in range(reach, 0, -1):
        for piece in range(pieces):
            low, high = piece * part, (piece + 1) * part
            if d == reach > 1 and piece == pieces - 1:
                last, _ = lax.optimization_barrier((last, peer[d - 1][0]))
            if d == reach:
                args = (res, own_far[piece], peer_far[piece])
                sent = pl.pallas_call(
                    far_kernel,
                    in_specs=after(last, args),
                    out_shape=[shape_of(part // 2)] * 2,
                    compiler_params=params,
                    cost_estimate=small if piece else longest,
                    name="sum_far",
                )(last, *args)
                last = sent[0]
                got[0, piece] = lax.ppermute(sent[0], "ind", right)
                got[1, piece] = lax.ppermute(sent[1], "ind", left)
            else:
                if d == reach - 1 > 1 and piece == pieces - 1:
                    last, _ = lax.optimization_barrier((last, peer[d - 1][0]))
                for way in (1, 0):
                    w = size - d if way else d
                    args = (res, genotype, peer[w][0], got[way, piece])
                    last = pl.pallas_call(
                        functools.partial(
                            hop_kernel, ring, (w, peer[w][1]), low, high, way
                        ),
                        in_specs=after(last, args),
                        out_shape=shape_of(part),
                        compiler_params=params,
                        cost_estimate=heavy if d == reach - 1 else middle,
                        name="sum_hop",
                    )(last, *args)
                    got[way, piece] = lax.ppermute(last, "ind", left if way else right)
            if later and (d, piece) in ((reach, pieces - 1), (reach - 1, 0)):
                distances = later.pop(0)
                (last,) = pick(whole(distances), pltpu.VMEM, light, last)
                swapped(distances, last)

    near = last = pl.pallas_call(
        functools.partial(near_kernel, ring, (0, peer[0][1])),
        in_specs=after(last, (res, genotype, peer[0][0])),
        out_shape=jax.ShapeDtypeStruct((cols, block), f32),
        compiler_params=params,
        cost_estimate=light,
        name="sum_near",
    )(last, res, genotype, peer[0][0])

    prior = prior_logit.reshape(1, cols)
    scale = slab_scale.reshape(1, cols)

    def full(shape):
        return pl.BlockSpec(shape, lambda i: (0,) * len(shape))

    outs = ()
    effects = []
    for piece in range(pieces):
        rows = pl.BlockSpec((part, cols), lambda i, piece=piece: (piece, 0))
        incl_new, mean_new, effect = pl.pallas_call(
            functools.partial(update_kernel, total, piece * part),
            grid=(1,),
            in_specs=[anywhere, full((cols, block))]
            + [full(got[way, piece].shape) for way in range(2)]
            + [rows] * 2
            + [full((1, cols))] * 2
            + [anywhere] * len(outs),
            out_specs=[rows, rows, full((part, cols))],
            out_shape=[
                jax.ShapeDtypeStruct((block, cols), f32),
                jax.ShapeDtypeStruct((block, cols), f32),
                jax.ShapeDtypeStruct((part, cols), bf16),
            ],
            input_output_aliases={8: 0, 9: 1} if outs else {},
            compiler_params=params,
            cost_estimate=light,
            name="update",
        )(last, near, got[0, piece], got[1, piece], incl_old, mean_old, prior, scale, *outs)
        outs = (incl_new, mean_new)
        last = effect
        effects.append(effect)

    eta_shape = jax.ShapeDtypeStruct((people, cols), f32)
    def product(found, eta, before, cost):
        args, places = list(eta), []
        for d, low, effect in reversed(found):
            piece = low // part
            there = (peer_far[piece], 0, piece * part) if d == reach else peer[d]
            args = [effect, genotype, there[0]] + args
            places = [((d, *there[1:]), low)] + places
        return pl.pallas_call(
            functools.partial(eta_kernel, ring, places, not eta),
            in_specs=after(before, args),
            out_shape=[eta_shape] * 2,
            compiler_params=params,
            cost_estimate=cost,
            name="add_eta",
        )(before, *args)

    eta = product([(0, piece * part, effects[piece]) for piece in range(pieces)], (), last, small)
    held = {(way, piece): effects[piece] for way in range(2) for piece in range(pieces)}
    etas = [eta[0]]
    for hop in range(1, reach + 1):
        for piece in range(pieces):
            for way in (1, 0):
                message = held[way, piece]
                if hop > 1:
                    message, _ = lax.optimization_barrier((message, etas[-2 * pieces - 1]))
                low = 0
                if hop == reach:
                    low = way * (part // 2)
                    message = message[low : low + part // 2]
                held[way, piece] = lax.ppermute(message, "ind", left if way else right)
                found = [(hop if way else size - hop, piece * part + low, held[way, piece])]
                eta = product(found, eta, eta[0], small if len(etas) == 1 else light)
                etas.append(eta[0])

    eta_got = lax.ppermute(eta[1], "ind", swap)
    resid_new = pl.pallas_call(
        end_kernel,
        out_shape=eta_shape,
        compiler_params=params,
        cost_estimate=light,
        name="new_residual",
    )(eta[0], eta_got, labels, offset.reshape(1, cols))
    return (outs[0], outs[1], resid_new)


def solution(mesh):
    split = P(("groups", "ind"), None)
    return jax.shard_map(
        functools.partial(on_device, ring_of(mesh.devices)),
        mesh=mesh,
        in_specs=(split, split, split, split, split, P(), P(), P()),
        out_specs=(split, split, split),
        check_vma=False,
    )
```

```python
import functools

import jax
import jax.numpy as jnp
from jax import lax
from jax.experimental import pallas as pl
from jax.experimental.pallas import tpu as pltpu
from jax.sharding import PartitionSpec as P

STEPS = 256.0
TOP = 32700.0
PAD = 16
LANES = 128
VMEM = 14 * 1024 * 1024


def ring_of(devices):
    chips = devices[0, ::2]
    where = [getattr(d, "coords", None) for d in chips]
    count = len(where)
    plain = list(range(count))
    if any(w is None for w in where):
        where = [(0, k % 2, k // 2) for k in plain]
    varying = [k for k in range(3) if len({w[k] for w in where}) > 1]
    if len(varying) != 2:
        return sorted(plain, key=lambda k: tuple(where[k]))
    short, long = sorted(varying, key=lambda k: len({w[k] for w in where}))
    low = min(w[short] for w in where)
    if len({w[short] for w in where}) != 2:
        return plain
    up = sorted((k for k in plain if where[k][short] == low), key=lambda k: where[k][long])
    down = sorted((k for k in plain if where[k][short] != low), key=lambda k: -where[k][long])
    return up + down


def owners_of(ring, distances):
    chip = lax.div(lax.axis_index("ind"), 2)
    spot = jnp.int32(0)
    for k, c in enumerate(ring):
        spot = jnp.where(chip == c, k, spot)
    found = []
    for d in distances:
        at = lax.rem(spot + d, len(ring))
        owner = jnp.int32(ring[0])
        for k, c in enumerate(ring):
            owner = jnp.where(at == k, c, owner)
        found.append(owner)
    return found


def pick_kernel(ring, wanted, block, genotype_ref, *refs):
    outs, sems = refs[-1 - len(wanted) : -1], refs[-1]
    core = lax.rem(lax.axis_index("ind"), 2)
    copies = []
    for out_ref, (distances, swapped, low, _) in zip(outs, wanted):
        parity = 1 - core if swapped else core
        width = out_ref.shape[2]
        for k, owner in enumerate(owners_of(ring, distances)):
            at = pl.multiple_of((2 * owner + parity) * block + low, LANES)
            copies.append(
                pltpu.make_async_copy(
                    genotype_ref.at[:, pl.ds(at, width)], out_ref.at[k], sems.at[len(copies)]
                )
            )
            copies[-1].start()
    for copy in copies:
        copy.wait()


def flip_kernel(before_ref, mine_ref, other_ref, out_ref):
    people = mine_ref.shape[0]
    out_ref[:, :people] = mine_ref[...].T
    out_ref[:, people:] = other_ref[...].T


def own_columns(ring, own_ref, d, low, high, swapped=False):
    (owner,) = owners_of(ring, [d])
    block = own_ref.shape[1] // (2 * len(ring))
    core = lax.rem(lax.axis_index("ind"), 2)
    at = (2 * owner + (1 - core if swapped else core)) * block + low
    return own_ref[:, pl.ds(pl.multiple_of(at, LANES), high - low)]


def local_sum(res_ref, own, other):
    people = own.shape[0]
    return jnp.dot(
        res_ref[:, :people], own, preferred_element_type=jnp.float32
    ) + jnp.dot(res_ref[:, people:], other, preferred_element_type=jnp.float32)


def decode(ref):
    rows = ref.shape[0] - PAD
    code = ref[rows:, :].astype(jnp.float32)[:1, :]
    return ref[:rows, :].astype(jnp.float32) * (jnp.exp2(code * (1.0 / STEPS)) * (1.0 / TOP))


def encode(ref, tiles):
    height = tiles[0].shape[0]
    top = functools.reduce(jnp.maximum, [jnp.abs(t) for t in tiles])
    top = jnp.maximum(jnp.max(top, axis=0, keepdims=True), 1e-30)
    code = jnp.ceil(jnp.log2(top) * STEPS)
    scale = TOP * jnp.exp2(code * (-1.0 / STEPS))
    for k, t in enumerate(tiles):
        ref[k * height : (k + 1) * height, :] = (
            jnp.round(t * scale).astype(jnp.int32).astype(jnp.int16)
        )
    ref[len(tiles) * height :, :] = (
        jnp.broadcast_to(code, (PAD, LANES)).astype(jnp.int32).astype(jnp.int16)
    )


def tiles_of(total):
    return [total[:, k : k + LANES] for k in range(0, total.shape[1], LANES)]


def far_kernel(before_ref, res_ref, own_ref, peer_ref, right_ref, left_ref):
    tiles = tiles_of(local_sum(res_ref, own_ref[0], peer_ref[0]))
    half = len(tiles) // 2
    encode(right_ref, tiles[:half])
    encode(left_ref, tiles[half:])


def hop_kernel(
    ring, at, low, high, way, before_ref, res_ref, own_ref, peer_ref, got_ref, out_ref
):
    own = own_columns(ring, own_ref, at[0], low, high)
    tiles = tiles_of(local_sum(res_ref, own, peer_ref[at[1], :, low:high]))
    got = decode(got_ref)
    height = tiles[0].shape[0]
    count = got.shape[0] // height
    first = 0 if way == 0 else len(tiles) - count
    for k in range(count):
        tiles[first + k] = tiles[first + k] + got[k * height : (k + 1) * height, :]
    encode(out_ref, tiles)


def near_kernel(ring, at, before_ref, res_ref, own_ref, peer_ref, out_ref):
    own = own_columns(ring, own_ref, at[0], 0, peer_ref.shape[2])
    out_ref[...] = local_sum(res_ref, own, peer_ref[at[1]])


def new_state(total, low, first, rows, refs):
    corr_ref, right_ref, left_ref, incl_ref, mean_ref, prior_ref, scale_ref = refs
    height = corr_ref.shape[0]
    right, left = decode(right_ref), decode(left_ref)
    scale = scale_ref[...]
    shrink = scale / (1.0 + scale)
    start = prior_ref[...] - 0.5 * jnp.log1p(scale)
    steep = 0.5 * total * shrink
    tiles = rows // LANES
    for k in range(tiles):
        corr = corr_ref[:, low + k * LANES : low + (k + 1) * LANES]
        for got, way in ((right, 0), (left, 1)):
            count = got.shape[0] // height
            skip = 0 if way == 0 else tiles - count
            if skip <= k < skip + count:
                corr = corr + got[(k - skip) * height : (k - skip + 1) * height, :]
        at = slice(first + k * LANES, first + (k + 1) * LANES)
        incl = incl_ref[at, :]
        stat = corr.T * (1.0 / total) + incl * mean_ref[at, :]
        mean_new = stat * shrink
        incl_new = 0.5 * incl + 0.5 * jax.nn.sigmoid(start + steep * stat * stat)
        yield slice(k * LANES, (k + 1) * LANES), incl_new, mean_new


def effect_kernel(total, low, before_ref, *refs):
    out_ref = refs[-1]
    for rows, incl_new, mean_new in new_state(total, low, low, out_ref.shape[0], refs[:7]):
        out_ref[rows, :] = (incl_new * mean_new).astype(jnp.bfloat16)


def update_kernel(total, low, before_ref, *refs):
    incl_new_ref, mean_new_ref = refs[-2:]
    rows_all = incl_new_ref.shape[0]
    for rows, incl_new, mean_new in new_state(total, low, 0, rows_all, refs[:7]):
        incl_new_ref[rows, :] = incl_new
        mean_new_ref[rows, :] = mean_new


def eta_kernel(ring, places, first, before_ref, *refs):
    out_ref, out_other_ref = refs[-2:]
    mine = other = None
    for k, (at, low) in enumerate(places):
        effect_ref, own_ref, peer_ref = refs[3 * k : 3 * k + 3]
        effect = effect_ref[...]
        high = low + effect.shape[0]
        own = own_columns(ring, own_ref, at[0], low, high)
        a = jnp.dot(own, effect, preferred_element_type=jnp.float32)
        b = jnp.dot(peer_ref[at[1], :, low - at[2] : high - at[2]], effect, preferred_element_type=jnp.float32)
        mine = a if mine is None else mine + a
        other = b if other is None else other + b
    if not first:
        mine = mine + refs[3 * len(places)][...]
        other = other + refs[3 * len(places) + 1][...]
    out_ref[...] = mine
    out_other_ref[...] = other


def end_kernel(
    ring, places, genotype_ref, eta_ref, upper_ref, lower_ref, labels_ref, offset_ref, *refs
):
    out_ref = refs[-1]
    got = jnp.concatenate([upper_ref[...], lower_ref[...]], axis=0)
    eta = eta_ref[...] + got + offset_ref[...]
    for effect_ref, (d, low, swapped) in zip(refs, places):
        own = own_columns(ring, genotype_ref, d, low, low + effect_ref.shape[0], swapped)
        eta = eta + jnp.dot(own, effect_ref[...], preferred_element_type=jnp.float32)
    out_ref[...] = 4.0 * (labels_ref[...].astype(jnp.float32) - jax.nn.sigmoid(eta))


def on_device(ring, genotype, residual, labels, incl_old, mean_old, prior_logit, slab_scale, offset):
    n = lax.axis_size("ind")
    people, cols = residual.shape
    total = float(people * n)
    block = incl_old.shape[0]
    size = len(ring)
    reach = size // 2
    pieces = 2 if block % (4 * LANES) == 0 else 1
    part = block // pieces
    f32, bf16 = jnp.float32, jnp.bfloat16
    params = pltpu.CompilerParams(vmem_limit_bytes=VMEM)
    small = pl.CostEstimate(flops=1, bytes_accessed=1, transcendentals=0)
    longest = pl.CostEstimate(flops=25 * 10**9, bytes_accessed=10**6, transcendentals=0)
    heavy = pl.CostEstimate(flops=10**10, bytes_accessed=10**6, transcendentals=0)
    middle = pl.CostEstimate(flops=4 * 10**9, bytes_accessed=10**6, transcendentals=0)
    light = pl.CostEstimate(flops=2 * 10**9, bytes_accessed=10**6, transcendentals=0)

    swap = [(k, k ^ 1) for k in range(n)]
    right, left = [], []
    for k, chip in enumerate(ring):
        for c in range(2):
            right.append((2 * chip + c, 2 * ring[(k + 1) % size] + c))
            left.append((2 * chip + c, 2 * ring[(k - 1) % size] + c))

    anywhere = pl.BlockSpec(memory_space=pl.ANY)

    def after(before, args):
        return [anywhere] + [pl.BlockSpec()] * len(args)

    def pick(wanted, source, cost, *before):
        return pl.pallas_call(
            functools.partial(pick_kernel, ring, wanted, block),
            in_specs=[anywhere] * (1 + len(before)),
            out_specs=[anywhere] * len(wanted),
            out_shape=[
                jax.ShapeDtypeStruct((len(distances), people, width), bf16)
                for distances, _, _, width in wanted
            ],
            scratch_shapes=[pltpu.SemaphoreType.DMA((sum(len(w[0]) for w in wanted),))],
            compiler_params=params,
            cost_estimate=cost,
            name="pick_blocks",
        )(pltpu.with_memory_space_constraint(genotype, source), *before)

    order = [reach]
    for d in range(reach - 1, 0, -1):
        order += [d, size - d]
    order += [0]
    peer, own_far, peer_far = {}, {}, {}

    def swapped(distances, sent):
        got = lax.ppermute(sent, "ind", swap)
        peer.update({d: (got, k, 0) for k, d in enumerate(distances)})

    def far(piece):
        return [(order[:1], True, piece * part, part), (order[:1], False, piece * part, part)]

    def whole(distances):
        return [(distances, True, 0, block)] if distances else []

    later = [b for b in (order[3:5], order[5:]) if b]
    last, own_far[0] = pick(far(0), pltpu.HBM, small)
    peer_far[0] = lax.ppermute(last, "ind", swap)
    mine, _ = lax.optimization_barrier((residual, last))
    residual_other = lax.ppermute(mine, "ind", swap)
    wanted = (far(1) if pieces > 1 else []) + whole(order[1:3])
    if wanted:
        found = pick(wanted, pltpu.HBM, heavy, last)
        last = found[0]
        if pieces > 1:
            peer_far[1], own_far[1] = lax.ppermute(found[0], "ind", swap), found[1]
        if order[1:3]:
            swapped(order[1:3], found[-1])
    res = last = pl.pallas_call(
        flip_kernel,
        in_specs=after(last, (residual, residual_other)),
        out_shape=jax.ShapeDtypeStruct((cols, 2 * people), bf16),
        compiler_params=params,
        cost_estimate=small,
        name="flip",
    )(last, residual, residual_other)

    def shape_of(width):
        return jax.ShapeDtypeStruct((width // LANES * cols + PAD, LANES), jnp.int16)

    got = {}
    for d in range(reach, 0, -1):
        for piece in range(pieces):
            low, high = piece * part, (piece + 1) * part
            if d == reach > 1 and piece == pieces - 1:
                last, _ = lax.optimization_barrier((last, peer[d - 1][0]))
            if d == reach:
                args = (res, own_far[piece], peer_far[piece])
                sent = pl.pallas_call(
                    far_kernel,
                    in_specs=after(last, args),
                    out_shape=[shape_of(part // 2)] * 2,
                    compiler_params=params,
                    cost_estimate=small if piece else longest,
                    name="sum_far",
                )(last, *args)
                last = sent[0]
                got[0, piece] = lax.ppermute(sent[0], "ind", right)
                got[1, piece] = lax.ppermute(sent[1], "ind", left)
            else:
                if d == reach - 1 > 1 and piece == pieces - 1:
                    last, _ = lax.optimization_barrier((last, peer[d - 1][0]))
                for way in (1, 0):
                    w = size - d if way else d
                    args = (res, genotype, peer[w][0], got[way, piece])
                    last = pl.pallas_call(
                        functools.partial(
                            hop_kernel, ring, (w, peer[w][1]), low, high, way
                        ),
                        in_specs=after(last, args),
                        out_shape=shape_of(part),
                        compiler_params=params,
                        cost_estimate=heavy if d == reach - 1 else middle,
                        name="sum_hop",
                    )(last, *args)
                    got[way, piece] = lax.ppermute(last, "ind", left if way else right)
            if later and (d, piece) in ((reach, pieces - 1), (reach - 1, 0)):
                distances = later.pop(0)
                (last,) = pick(whole(distances), pltpu.VMEM, light, last)
                swapped(distances, last)

    near = last = pl.pallas_call(
        functools.partial(near_kernel, ring, (0, peer[0][1])),
        in_specs=after(last, (res, genotype, peer[0][0])),
        out_shape=jax.ShapeDtypeStruct((cols, block), f32),
        compiler_params=params,
        cost_estimate=light,
        name="sum_near",
    )(last, res, genotype, peer[0][0])

    prior = prior_logit.reshape(1, cols)
    scale = slab_scale.reshape(1, cols)

    def full(shape):
        return pl.BlockSpec(shape, lambda i: (0,) * len(shape))

    effects = []
    for piece in range(pieces):
        args = (near, got[0, piece], got[1, piece], incl_old, mean_old, prior, scale)
        last = pl.pallas_call(
            functools.partial(effect_kernel, total, piece * part),
            in_specs=after(last, args),
            out_shape=jax.ShapeDtypeStruct((part, cols), bf16),
            compiler_params=params,
            cost_estimate=light,
            name="effect",
        )(last, *args)
        effects.append(last)

    def update(piece, outs, before):
        rows = pl.BlockSpec((part, cols), lambda i, piece=piece: (piece, 0))
        return pl.pallas_call(
            functools.partial(update_kernel, total, piece * part),
            grid=(1,),
            in_specs=[anywhere, full((cols, block))]
            + [full(got[way, piece].shape) for way in range(2)]
            + [rows] * 2
            + [full((1, cols))] * 2
            + [anywhere] * len(outs),
            out_specs=[rows, rows],
            out_shape=[jax.ShapeDtypeStruct((block, cols), f32)] * 2,
            input_output_aliases={8: 0, 9: 1} if outs else {},
            compiler_params=params,
            cost_estimate=small,
            name="update",
        )(before, near, got[0, piece], got[1, piece], incl_old, mean_old, prior, scale, *outs)

    eta_shape = jax.ShapeDtypeStruct((people, cols), f32)
    def product(found, eta, before, cost):
        args, places = list(eta), []
        for d, low, effect in reversed(found):
            piece = low // part
            there = (peer_far[piece], 0, piece * part) if d == reach else peer[d]
            args = [effect, genotype, there[0]] + args
            places = [((d, *there[1:]), low)] + places
        return pl.pallas_call(
            functools.partial(eta_kernel, ring, places, not eta),
            in_specs=after(before, args),
            out_shape=[eta_shape] * 2,
            compiler_params=params,
            cost_estimate=cost,
            name="add_eta",
        )(before, *args)

    eta = product([(0, piece * part, effects[piece]) for piece in range(pieces)], (), last, small)
    last = eta[0]
    held = {(way, piece): effects[piece] for way in range(2) for piece in range(pieces)}
    etas = [eta[0]]
    outs, updated, final = (), 0, []
    for hop in range(1, reach + 1):
        for piece in range(pieces):
            for way in (1, 0):
                message = held[way, piece]
                if hop > 1:
                    message, _ = lax.optimization_barrier((message, etas[-2 * pieces - 1]))
                low = 0
                if hop == reach:
                    low = way * (part // 2)
                    message = message[low : low + part // 2]
                held[way, piece] = lax.ppermute(message, "ind", left if way else right)
                found = (hop if way else size - hop, piece * part + low, held[way, piece])
                if hop == reach and piece == pieces - 1:
                    final.append(found)
                    continue
                eta = product([found], eta, last, small if len(etas) == 1 else light)
                last = eta[0]
                etas.append(last)
        if updated < pieces and hop < reach:
            outs = update(updated, outs, last)
            last = outs[0]
            updated += 1
    while updated < pieces:
        outs = update(updated, outs, last)
        last = outs[0]
        updated += 1

    half = people // 2
    eta_got = [lax.ppermute(eta[1][k : k + half], "ind", swap) for k in (0, half)]
    places = [(d, low, False) for d, low, _ in final] + [(d, low, True) for d, low, _ in final]
    args = (genotype, eta[0], *eta_got, labels, offset.reshape(1, cols))
    args += tuple(effect for _, _, effect in final)
    args += tuple(lax.ppermute(effect, "ind", swap) for _, _, effect in final)
    resid_new = pl.pallas_call(
        functools.partial(end_kernel, ring, places),
        out_shape=eta_shape,
        compiler_params=params,
        cost_estimate=light,
        name="new_residual",
    )(*args)
    return (outs[0], outs[1], resid_new)


def solution(mesh):
    split = P(("groups", "ind"), None)
    return jax.shard_map(
        functools.partial(on_device, ring_of(mesh.devices)),
        mesh=mesh,
        in_specs=(split, split, split, split, split, P(), P(), P()),
        out_specs=(split, split, split),
        check_vma=False,
    )
```

```python
import functools

import jax
import jax.numpy as jnp
from jax import lax
from jax.experimental import pallas as pl
from jax.experimental.pallas import tpu as pltpu
from jax.sharding import PartitionSpec as P

STEPS = 256.0
TOP = 32700.0
PAD = 16
LANES = 128
VMEM = 14 * 1024 * 1024


def ring_of(devices):
    chips = devices[0, ::2]
    where = [getattr(d, "coords", None) for d in chips]
    count = len(where)
    plain = list(range(count))
    if any(w is None for w in where):
        where = [(0, k % 2, k // 2) for k in plain]
    varying = [k for k in range(3) if len({w[k] for w in where}) > 1]
    if len(varying) != 2:
        return sorted(plain, key=lambda k: tuple(where[k]))
    short, long = sorted(varying, key=lambda k: len({w[k] for w in where}))
    low = min(w[short] for w in where)
    if len({w[short] for w in where}) != 2:
        return plain
    up = sorted((k for k in plain if where[k][short] == low), key=lambda k: where[k][long])
    down = sorted((k for k in plain if where[k][short] != low), key=lambda k: -where[k][long])
    return up + down


def owners_of(ring, distances):
    chip = lax.div(lax.axis_index("ind"), 2)
    spot = jnp.int32(0)
    for k, c in enumerate(ring):
        spot = jnp.where(chip == c, k, spot)
    found = []
    for d in distances:
        at = lax.rem(spot + d, len(ring))
        owner = jnp.int32(ring[0])
        for k, c in enumerate(ring):
            owner = jnp.where(at == k, c, owner)
        found.append(owner)
    return found


def pick_kernel(ring, wanted, block, genotype_ref, *refs):
    outs, sems = refs[-1 - len(wanted) : -1], refs[-1]
    core = lax.rem(lax.axis_index("ind"), 2)
    copies = []
    for out_ref, (distances, swapped, low, _) in zip(outs, wanted):
        parity = 1 - core if swapped else core
        width = out_ref.shape[2]
        for k, owner in enumerate(owners_of(ring, distances)):
            at = pl.multiple_of((2 * owner + parity) * block + low, LANES)
            copies.append(
                pltpu.make_async_copy(
                    genotype_ref.at[:, pl.ds(at, width)], out_ref.at[k], sems.at[len(copies)]
                )
            )
            copies[-1].start()
    for copy in copies:
        copy.wait()


def flip_kernel(before_ref, mine_ref, other_ref, out_ref):
    people = mine_ref.shape[0]
    out_ref[:, :people] = mine_ref[...].T
    out_ref[:, people:] = other_ref[...].T


def own_columns(ring, own_ref, d, low, high, swapped=False):
    (owner,) = owners_of(ring, [d])
    block = own_ref.shape[1] // (2 * len(ring))
    core = lax.rem(lax.axis_index("ind"), 2)
    at = (2 * owner + (1 - core if swapped else core)) * block + low
    return own_ref[:, pl.ds(pl.multiple_of(at, LANES), high - low)]


def local_sum(res_ref, own, other):
    people = own.shape[0]
    return jnp.dot(
        res_ref[:, :people], own, preferred_element_type=jnp.float32
    ) + jnp.dot(res_ref[:, people:], other, preferred_element_type=jnp.float32)


def decode(ref):
    rows = ref.shape[0] - PAD
    code = ref[rows:, :].astype(jnp.float32)[:1, :]
    return ref[:rows, :].astype(jnp.float32) * (jnp.exp2(code * (1.0 / STEPS)) * (1.0 / TOP))


def encode(ref, tiles):
    height = tiles[0].shape[0]
    top = functools.reduce(jnp.maximum, [jnp.abs(t) for t in tiles])
    top = jnp.maximum(jnp.max(top, axis=0, keepdims=True), 1e-30)
    code = jnp.ceil(jnp.log2(top) * STEPS)
    scale = TOP * jnp.exp2(code * (-1.0 / STEPS))
    for k, t in enumerate(tiles):
        ref[k * height : (k + 1) * height, :] = (
            jnp.round(t * scale).astype(jnp.int32).astype(jnp.int16)
        )
    ref[len(tiles) * height :, :] = (
        jnp.broadcast_to(code, (PAD, LANES)).astype(jnp.int32).astype(jnp.int16)
    )


def tiles_of(total):
    return [total[:, k : k + LANES] for k in range(0, total.shape[1], LANES)]


def far_kernel(before_ref, res_ref, own_ref, peer_ref, right_ref, left_ref):
    tiles = tiles_of(local_sum(res_ref, own_ref[0], peer_ref[0]))
    half = len(tiles) // 2
    encode(right_ref, tiles[:half])
    encode(left_ref, tiles[half:])


def hop_kernel(
    ring, at, low, high, way, before_ref, res_ref, own_ref, peer_ref, got_ref, out_ref
):
    own = own_columns(ring, own_ref, at[0], low, high)
    tiles = tiles_of(local_sum(res_ref, own, peer_ref[at[1], :, low:high]))
    got = decode(got_ref)
    height = tiles[0].shape[0]
    count = got.shape[0] // height
    first = 0 if way == 0 else len(tiles) - count
    for k in range(count):
        tiles[first + k] = tiles[first + k] + got[k * height : (k + 1) * height, :]
    encode(out_ref, tiles)


def near_kernel(ring, at, before_ref, res_ref, own_ref, peer_ref, out_ref):
    own = own_columns(ring, own_ref, at[0], 0, peer_ref.shape[2])
    out_ref[...] = local_sum(res_ref, own, peer_ref[at[1]])


def new_state(total, low, first, rows, refs):
    corr_ref, right_ref, left_ref, incl_ref, mean_ref, prior_ref, scale_ref = refs
    height = corr_ref.shape[0]
    right, left = decode(right_ref), decode(left_ref)
    scale = scale_ref[...]
    shrink = scale / (1.0 + scale)
    start = prior_ref[...] - 0.5 * jnp.log1p(scale)
    steep = 0.5 * total * shrink
    tiles = rows // LANES
    for k in range(tiles):
        corr = corr_ref[:, low + k * LANES : low + (k + 1) * LANES]
        for got, way in ((right, 0), (left, 1)):
            count = got.shape[0] // height
            skip = 0 if way == 0 else tiles - count
            if skip <= k < skip + count:
                corr = corr + got[(k - skip) * height : (k - skip + 1) * height, :]
        at = slice(first + k * LANES, first + (k + 1) * LANES)
        incl = incl_ref[at, :]
        stat = corr.T * (1.0 / total) + incl * mean_ref[at, :]
        mean_new = stat * shrink
        incl_new = 0.5 * incl + 0.5 * jax.nn.sigmoid(start + steep * stat * stat)
        yield slice(k * LANES, (k + 1) * LANES), incl_new, mean_new


def effect_kernel(total, low, before_ref, *refs):
    out_ref = refs[-1]
    for rows, incl_new, mean_new in new_state(total, low, low, out_ref.shape[0], refs[:7]):
        out_ref[rows, :] = (incl_new * mean_new).astype(jnp.bfloat16)


def update_kernel(total, low, before_ref, *refs):
    incl_new_ref, mean_new_ref, token_ref = refs[-3:]
    token_ref[...] = jnp.zeros_like(token_ref)
    rows_all = incl_new_ref.shape[0]
    for rows, incl_new, mean_new in new_state(total, low, 0, rows_all, refs[:7]):
        incl_new_ref[rows, :] = incl_new
        mean_new_ref[rows, :] = mean_new


def eta_kernel(ring, places, first, before_ref, *refs):
    out_ref, out_other_ref = refs[-2:]
    mine = other = None
    for k, (at, low) in enumerate(places):
        effect_ref, own_ref, peer_ref = refs[3 * k : 3 * k + 3]
        effect = effect_ref[...]
        high = low + effect.shape[0]
        own = own_columns(ring, own_ref, at[0], low, high)
        a = jnp.dot(own, effect, preferred_element_type=jnp.float32)
        b = jnp.dot(peer_ref[at[1], :, low - at[2] : high - at[2]], effect, preferred_element_type=jnp.float32)
        mine = a if mine is None else mine + a
        other = b if other is None else other + b
    if not first:
        mine = mine + refs[3 * len(places)][...]
        other = other + refs[3 * len(places) + 1][...]
    out_ref[...] = mine
    out_other_ref[...] = other


def columns_product(ring, places, genotype_ref, refs, eta):
    for effect_ref, (d, low, swapped) in zip(refs, places):
        own = own_columns(ring, genotype_ref, d, low, low + effect_ref.shape[0], swapped)
        eta = eta + jnp.dot(own, effect_ref[...], preferred_element_type=jnp.float32)
    return eta


def own_kernel(ring, places, genotype_ref, eta_ref, offset_ref, *refs):
    eta = eta_ref[...] + offset_ref[...]
    refs[-1][...] = columns_product(ring, places, genotype_ref, refs, eta)


def end_kernel(ring, places, genotype_ref, eta_ref, upper_ref, lower_ref, labels_ref, *refs):
    got = jnp.concatenate([upper_ref[...], lower_ref[...]], axis=0)
    eta = columns_product(ring, places, genotype_ref, refs, eta_ref[...] + got)
    refs[-1][...] = 4.0 * (labels_ref[...].astype(jnp.float32) - jax.nn.sigmoid(eta))


def on_device(ring, genotype, residual, labels, incl_old, mean_old, prior_logit, slab_scale, offset):
    n = lax.axis_size("ind")
    people, cols = residual.shape
    total = float(people * n)
    block = incl_old.shape[0]
    size = len(ring)
    reach = size // 2
    pieces = 2 if block % (4 * LANES) == 0 else 1
    part = block // pieces
    f32, bf16 = jnp.float32, jnp.bfloat16
    params = pltpu.CompilerParams(vmem_limit_bytes=VMEM)
    small = pl.CostEstimate(flops=1, bytes_accessed=1, transcendentals=0)
    longest = pl.CostEstimate(flops=25 * 10**9, bytes_accessed=10**6, transcendentals=0)
    heavy = pl.CostEstimate(flops=10**10, bytes_accessed=10**6, transcendentals=0)
    middle = pl.CostEstimate(flops=4 * 10**9, bytes_accessed=10**6, transcendentals=0)
    light = pl.CostEstimate(flops=2 * 10**9, bytes_accessed=10**6, transcendentals=0)

    swap = [(k, k ^ 1) for k in range(n)]
    right, left = [], []
    for k, chip in enumerate(ring):
        for c in range(2):
            right.append((2 * chip + c, 2 * ring[(k + 1) % size] + c))
            left.append((2 * chip + c, 2 * ring[(k - 1) % size] + c))

    anywhere = pl.BlockSpec(memory_space=pl.ANY)

    def after(before, args):
        return [anywhere] + [pl.BlockSpec()] * len(args)

    def pick(wanted, source, cost, *before):
        return pl.pallas_call(
            functools.partial(pick_kernel, ring, wanted, block),
            in_specs=[anywhere] * (1 + len(before)),
            out_specs=[anywhere] * len(wanted),
            out_shape=[
                jax.ShapeDtypeStruct((len(distances), people, width), bf16)
                for distances, _, _, width in wanted
            ],
            scratch_shapes=[pltpu.SemaphoreType.DMA((sum(len(w[0]) for w in wanted),))],
            compiler_params=params,
            cost_estimate=cost,
            name="pick_blocks",
        )(pltpu.with_memory_space_constraint(genotype, source), *before)

    order = [reach]
    for d in range(reach - 1, 0, -1):
        order += [d, size - d]
    order += [0]
    peer, own_far, peer_far = {}, {}, {}

    def swapped(distances, sent):
        got = lax.ppermute(sent, "ind", swap)
        peer.update({d: (got, k, 0) for k, d in enumerate(distances)})

    def far(piece):
        return [(order[:1], True, piece * part, part), (order[:1], False, piece * part, part)]

    def whole(distances):
        return [(distances, True, 0, block)] if distances else []

    later = [b for b in (order[3:5], order[5:]) if b]
    last, own_far[0] = pick(far(0), pltpu.HBM, small)
    peer_far[0] = lax.ppermute(last, "ind", swap)
    mine, _ = lax.optimization_barrier((residual, last))
    residual_other = lax.ppermute(mine, "ind", swap)
    wanted = (far(1) if pieces > 1 else []) + whole(order[1:3])
    if wanted:
        found = pick(wanted, pltpu.HBM, heavy, last)
        last = found[0]
        if pieces > 1:
            peer_far[1], own_far[1] = lax.ppermute(found[0], "ind", swap), found[1]
        if order[1:3]:
            swapped(order[1:3], found[-1])
    res = last = pl.pallas_call(
        flip_kernel,
        in_specs=after(last, (residual, residual_other)),
        out_shape=jax.ShapeDtypeStruct((cols, 2 * people), bf16),
        compiler_params=params,
        cost_estimate=small,
        name="flip",
    )(last, residual, residual_other)

    def shape_of(width):
        return jax.ShapeDtypeStruct((width // LANES * cols + PAD, LANES), jnp.int16)

    got = {}
    for d in range(reach, 0, -1):
        for piece in range(pieces):
            low, high = piece * part, (piece + 1) * part
            if d == reach > 1 and piece == pieces - 1:
                last, _ = lax.optimization_barrier((last, peer[d - 1][0]))
            if d == reach:
                args = (res, own_far[piece], peer_far[piece])
                sent = pl.pallas_call(
                    far_kernel,
                    in_specs=after(last, args),
                    out_shape=[shape_of(part // 2)] * 2,
                    compiler_params=params,
                    cost_estimate=small if piece else longest,
                    name="sum_far",
                )(last, *args)
                last = sent[0]
                got[0, piece] = lax.ppermute(sent[0], "ind", right)
                got[1, piece] = lax.ppermute(sent[1], "ind", left)
            else:
                if d == reach - 1 > 1 and piece == pieces - 1:
                    last, _ = lax.optimization_barrier((last, peer[d - 1][0]))
                for way in (1, 0):
                    w = size - d if way else d
                    args = (res, genotype, peer[w][0], got[way, piece])
                    last = pl.pallas_call(
                        functools.partial(
                            hop_kernel, ring, (w, peer[w][1]), low, high, way
                        ),
                        in_specs=after(last, args),
                        out_shape=shape_of(part),
                        compiler_params=params,
                        cost_estimate=heavy if d == reach - 1 else middle,
                        name="sum_hop",
                    )(last, *args)
                    got[way, piece] = lax.ppermute(last, "ind", left if way else right)
            if later and (d, piece) in ((reach, pieces - 1), (reach - 1, 0)):
                distances = later.pop(0)
                (last,) = pick(whole(distances), pltpu.VMEM, light, last)
                swapped(distances, last)

    near = last = pl.pallas_call(
        functools.partial(near_kernel, ring, (0, peer[0][1])),
        in_specs=after(last, (res, genotype, peer[0][0])),
        out_shape=jax.ShapeDtypeStruct((cols, block), f32),
        compiler_params=params,
        cost_estimate=light,
        name="sum_near",
    )(last, res, genotype, peer[0][0])

    prior = prior_logit.reshape(1, cols)
    scale = slab_scale.reshape(1, cols)

    def full(shape):
        return pl.BlockSpec(shape, lambda i: (0,) * len(shape))

    effects = []
    for piece in range(pieces):
        args = (near, got[0, piece], got[1, piece], incl_old, mean_old, prior, scale)
        last = pl.pallas_call(
            functools.partial(effect_kernel, total, piece * part),
            in_specs=after(last, args),
            out_shape=jax.ShapeDtypeStruct((part, cols), bf16),
            compiler_params=params,
            cost_estimate=light,
            name="effect",
        )(last, *args)
        effects.append(last)

    def update(piece, outs, before):
        rows = pl.BlockSpec((part, cols), lambda i, piece=piece: (piece, 0))
        return pl.pallas_call(
            functools.partial(update_kernel, total, piece * part),
            grid=(1,),
            in_specs=[anywhere, full((cols, block))]
            + [full(got[way, piece].shape) for way in range(2)]
            + [rows] * 2
            + [full((1, cols))] * 2
            + [anywhere] * len(outs),
            out_specs=[rows, rows, full((8, LANES))],
            out_shape=[jax.ShapeDtypeStruct((block, cols), f32)] * 2
            + [jax.ShapeDtypeStruct((8, LANES), f32)],
            input_output_aliases={8: 0, 9: 1} if outs else {},
            compiler_params=params,
            cost_estimate=small,
            name="update",
        )(before, near, got[0, piece], got[1, piece], incl_old, mean_old, prior, scale, *outs)

    eta_shape = jax.ShapeDtypeStruct((people, cols), f32)
    def product(found, eta, before, cost):
        args, places = list(eta), []
        for d, low, effect in reversed(found):
            piece = low // part
            there = (peer_far[piece], 0, piece * part) if d == reach else peer[d]
            args = [effect, genotype, there[0]] + args
            places = [((d, *there[1:]), low)] + places
        return pl.pallas_call(
            functools.partial(eta_kernel, ring, places, not eta),
            in_specs=after(before, args),
            out_shape=[eta_shape] * 2,
            compiler_params=params,
            cost_estimate=cost,
            name="add_eta",
        )(before, *args)

    eta = product([(0, piece * part, effects[piece]) for piece in range(pieces)], (), last, small)
    last = eta[0]
    held = {(way, piece): effects[piece] for way in range(2) for piece in range(pieces)}
    etas = [eta[0]]
    outs, updated, final = (), 0, []
    for hop in range(1, reach + 1):
        for piece in range(pieces):
            for way in (1, 0):
                message = held[way, piece]
                perm = left if way else right
                d, low = (hop if way else size - hop), piece * part
                if hop > 1:
                    message, _ = lax.optimization_barrier((message, etas[-2 * pieces - 1]))
                near_half = way * (part // 2)
                halved = message.shape[0] != part
                if hop == reach:
                    if not halved:
                        message = message[near_half : near_half + part // 2]
                    held[way, piece] = lax.ppermute(message, "ind", perm)
                    found = [(d, low + near_half, held[way, piece])]
                elif hop == reach - 1 and piece == pieces - 1:
                    far_half = part // 2 - near_half
                    first = message[near_half : near_half + part // 2]
                    first = held[way, piece] = lax.ppermute(first, "ind", perm)
                    message, _ = lax.optimization_barrier((message, etas[-2 * pieces]))
                    second = message[far_half : far_half + part // 2]
                    second = lax.ppermute(second, "ind", perm)
                    found = [(d, low + near_half, first), (d, low + far_half, second)]
                else:
                    held[way, piece] = lax.ppermute(message, "ind", perm)
                    found = [(d, low, held[way, piece])]
                if hop == reach and piece == pieces - 1:
                    final += found
                    continue
                eta = product(found, eta, last, small if len(etas) == 1 or (hop, piece) >= (reach - 1, pieces - 1) else light)
                last = eta[0]
                etas.append(last)
        if updated < pieces and hop < reach:
            *outs, last = update(updated, outs, last)
            updated += 1
    while updated < pieces:
        *outs, last = update(updated, outs, last)
        updated += 1

    half = people // 2
    eta_got = [lax.ppermute(eta[1][k : k + half], "ind", swap) for k in (0, half)]
    others = [lax.ppermute(effect, "ind", swap) for _, _, effect in final]
    mine = pl.pallas_call(
        functools.partial(own_kernel, ring, [(d, low, False) for d, low, _ in final]),
        out_shape=eta_shape,
        compiler_params=params,
        cost_estimate=heavy,
        name="own_last",
    )(genotype, eta[0], offset.reshape(1, cols), *[effect for _, _, effect in final])
    resid_new = pl.pallas_call(
        functools.partial(end_kernel, ring, [(d, low, True) for d, low, _ in final]),
        out_shape=eta_shape,
        compiler_params=params,
        cost_estimate=light,
        name="new_residual",
    )(genotype, mine, *eta_got, labels, *others)
    return (outs[0], outs[1], resid_new)


def solution(mesh):
    split = P(("groups", "ind"), None)
    return jax.shard_map(
        functools.partial(on_device, ring_of(mesh.devices)),
        mesh=mesh,
        in_specs=(split, split, split, split, split, P(), P(), P()),
        out_specs=(split, split, split),
        check_vma=False,
    )
```

```python
import functools

import jax
import jax.numpy as jnp
from jax import lax
from jax.experimental import pallas as pl
from jax.experimental.pallas import tpu as pltpu
from jax.sharding import PartitionSpec as P

STEPS = 256.0
TOP = 32700.0
PAD = 16
LANES = 128
VMEM = 14 * 1024 * 1024


def ring_of(devices):
    chips = devices[0, ::2]
    where = [getattr(d, "coords", None) for d in chips]
    count = len(where)
    plain = list(range(count))
    if any(w is None for w in where):
        where = [(0, k % 2, k // 2) for k in plain]
    varying = [k for k in range(3) if len({w[k] for w in where}) > 1]
    if len(varying) != 2:
        return sorted(plain, key=lambda k: tuple(where[k]))
    short, long = sorted(varying, key=lambda k: len({w[k] for w in where}))
    low = min(w[short] for w in where)
    if len({w[short] for w in where}) != 2:
        return plain
    up = sorted((k for k in plain if where[k][short] == low), key=lambda k: where[k][long])
    down = sorted((k for k in plain if where[k][short] != low), key=lambda k: -where[k][long])
    return up + down


def owners_of(ring, distances):
    chip = lax.div(lax.axis_index("ind"), 2)
    spot = jnp.int32(0)
    for k, c in enumerate(ring):
        spot = jnp.where(chip == c, k, spot)
    found = []
    for d in distances:
        at = lax.rem(spot + d, len(ring))
        owner = jnp.int32(ring[0])
        for k, c in enumerate(ring):
            owner = jnp.where(at == k, c, owner)
        found.append(owner)
    return found


def pick_kernel(ring, wanted, block, genotype_ref, *refs):
    outs, sems = refs[-1 - len(wanted) : -1], refs[-1]
    core = lax.rem(lax.axis_index("ind"), 2)
    copies = []
    for out_ref, (distances, swapped, low, _) in zip(outs, wanted):
        parity = 1 - core if swapped else core
        width = out_ref.shape[2]
        for k, owner in enumerate(owners_of(ring, distances)):
            at = pl.multiple_of((2 * owner + parity) * block + low, LANES)
            copies.append(
                pltpu.make_async_copy(
                    genotype_ref.at[:, pl.ds(at, width)], out_ref.at[k], sems.at[len(copies)]
                )
            )
            copies[-1].start()
    for copy in copies:
        copy.wait()


def flip_kernel(before_ref, mine_ref, other_ref, out_ref):
    people = mine_ref.shape[0]
    out_ref[:, :people] = mine_ref[...].T
    out_ref[:, people:] = other_ref[...].T


def own_columns(ring, own_ref, d, low, high, swapped=False):
    (owner,) = owners_of(ring, [d])
    block = own_ref.shape[1] // (2 * len(ring))
    core = lax.rem(lax.axis_index("ind"), 2)
    at = (2 * owner + (1 - core if swapped else core)) * block + low
    return own_ref[:, pl.ds(pl.multiple_of(at, LANES), high - low)]


def local_sum(res_ref, own, other):
    people = own.shape[0]
    return jnp.dot(
        res_ref[:, :people], own, preferred_element_type=jnp.float32
    ) + jnp.dot(res_ref[:, people:], other, preferred_element_type=jnp.float32)


def decode(ref):
    rows = ref.shape[0] - PAD
    code = ref[rows:, :].astype(jnp.float32)[:1, :]
    return ref[:rows, :].astype(jnp.float32) * (jnp.exp2(code * (1.0 / STEPS)) * (1.0 / TOP))


def encode(ref, tiles):
    height = tiles[0].shape[0]
    top = functools.reduce(jnp.maximum, [jnp.abs(t) for t in tiles])
    top = jnp.maximum(jnp.max(top, axis=0, keepdims=True), 1e-30)
    code = jnp.ceil(jnp.log2(top) * STEPS)
    scale = TOP * jnp.exp2(code * (-1.0 / STEPS))
    for k, t in enumerate(tiles):
        ref[k * height : (k + 1) * height, :] = (
            jnp.round(t * scale).astype(jnp.int32).astype(jnp.int16)
        )
    ref[len(tiles) * height :, :] = (
        jnp.broadcast_to(code, (PAD, LANES)).astype(jnp.int32).astype(jnp.int16)
    )


def tiles_of(total):
    return [total[:, k : k + LANES] for k in range(0, total.shape[1], LANES)]


def far_kernel(before_ref, res_ref, own_ref, peer_ref, right_ref, left_ref):
    tiles = tiles_of(local_sum(res_ref, own_ref[0], peer_ref[0]))
    half = len(tiles) // 2
    encode(right_ref, tiles[:half])
    encode(left_ref, tiles[half:])


def hop_kernel(
    ring, at, low, high, way, before_ref, res_ref, own_ref, peer_ref, got_ref, out_ref
):
    own = own_columns(ring, own_ref, at[0], low, high)
    tiles = tiles_of(local_sum(res_ref, own, peer_ref[at[1], :, low:high]))
    got = decode(got_ref)
    height = tiles[0].shape[0]
    count = got.shape[0] // height
    first = 0 if way == 0 else len(tiles) - count
    for k in range(count):
        tiles[first + k] = tiles[first + k] + got[k * height : (k + 1) * height, :]
    encode(out_ref, tiles)


def near_kernel(ring, at, before_ref, res_ref, own_ref, peer_ref, out_ref):
    own = own_columns(ring, own_ref, at[0], 0, peer_ref.shape[2])
    out_ref[...] = local_sum(res_ref, own, peer_ref[at[1]])


def new_state(total, low, first, rows, refs):
    corr_ref, right_ref, left_ref, incl_ref, mean_ref, prior_ref, scale_ref = refs
    height = corr_ref.shape[0]
    right, left = decode(right_ref), decode(left_ref)
    scale = scale_ref[...]
    shrink = scale / (1.0 + scale)
    start = prior_ref[...] - 0.5 * jnp.log1p(scale)
    steep = 0.5 * total * shrink
    tiles = rows // LANES
    for k in range(tiles):
        corr = corr_ref[:, low + k * LANES : low + (k + 1) * LANES]
        for got, way in ((right, 0), (left, 1)):
            count = got.shape[0] // height
            skip = 0 if way == 0 else tiles - count
            if skip <= k < skip + count:
                corr = corr + got[(k - skip) * height : (k - skip + 1) * height, :]
        at = slice(first + k * LANES, first + (k + 1) * LANES)
        incl = incl_ref[at, :]
        stat = corr.T * (1.0 / total) + incl * mean_ref[at, :]
        mean_new = stat * shrink
        incl_new = 0.5 * incl + 0.5 * jax.nn.sigmoid(start + steep * stat * stat)
        yield slice(k * LANES, (k + 1) * LANES), incl_new, mean_new


def effect_kernel(total, low, before_ref, *refs):
    out_ref = refs[-1]
    for rows, incl_new, mean_new in new_state(total, low, low, out_ref.shape[0], refs[:7]):
        out_ref[rows, :] = (incl_new * mean_new).astype(jnp.bfloat16)


def update_kernel(total, low, before_ref, *refs):
    incl_new_ref, mean_new_ref, token_ref = refs[-3:]
    token_ref[...] = jnp.zeros_like(token_ref)
    rows_all = incl_new_ref.shape[0]
    for rows, incl_new, mean_new in new_state(total, low, 0, rows_all, refs[:7]):
        incl_new_ref[rows, :] = incl_new
        mean_new_ref[rows, :] = mean_new


def eta_kernel(ring, places, first, before_ref, *refs):
    out_ref, out_other_ref = refs[-2:]
    mine = other = None
    for k, (at, low) in enumerate(places):
        effect_ref, own_ref, peer_ref = refs[3 * k : 3 * k + 3]
        effect = effect_ref[...]
        high = low + effect.shape[0]
        own = own_columns(ring, own_ref, at[0], low, high)
        a = jnp.dot(own, effect, preferred_element_type=jnp.float32)
        b = jnp.dot(peer_ref[at[1], :, low - at[2] : high - at[2]], effect, preferred_element_type=jnp.float32)
        mine = a if mine is None else mine + a
        other = b if other is None else other + b
    if not first:
        mine = mine + refs[3 * len(places)][...]
        other = other + refs[3 * len(places) + 1][...]
    out_ref[...] = mine
    out_other_ref[...] = other


def columns_product(ring, places, genotype_ref, refs, eta):
    for effect_ref, (d, low, swapped) in zip(refs, places):
        own = own_columns(ring, genotype_ref, d, low, low + effect_ref.shape[0], swapped)
        eta = eta + jnp.dot(own, effect_ref[...], preferred_element_type=jnp.float32)
    return eta


def own_kernel(ring, places, genotype_ref, eta_ref, offset_ref, *refs):
    eta = eta_ref[...] + offset_ref[...]
    refs[-1][...] = columns_product(ring, places, genotype_ref, refs, eta)


def end_kernel(ring, places, genotype_ref, eta_ref, upper_ref, lower_ref, labels_ref, *refs):
    got = jnp.concatenate([upper_ref[...], lower_ref[...]], axis=0)
    eta = columns_product(ring, places, genotype_ref, refs, eta_ref[...] + got)
    refs[-1][...] = 4.0 * (labels_ref[...].astype(jnp.float32) - jax.nn.sigmoid(eta))


def on_device(ring, genotype, residual, labels, incl_old, mean_old, prior_logit, slab_scale, offset):
    n = lax.axis_size("ind")
    people, cols = residual.shape
    total = float(people * n)
    block = incl_old.shape[0]
    size = len(ring)
    reach = size // 2
    pieces = 2 if block % (4 * LANES) == 0 else 1
    part = block // pieces
    f32, bf16 = jnp.float32, jnp.bfloat16
    params = pltpu.CompilerParams(vmem_limit_bytes=VMEM)
    small = pl.CostEstimate(flops=1, bytes_accessed=1, transcendentals=0)
    longest = pl.CostEstimate(flops=25 * 10**9, bytes_accessed=10**6, transcendentals=0)
    heavy = pl.CostEstimate(flops=10**10, bytes_accessed=10**6, transcendentals=0)
    middle = pl.CostEstimate(flops=4 * 10**9, bytes_accessed=10**6, transcendentals=0)
    light = pl.CostEstimate(flops=2 * 10**9, bytes_accessed=10**6, transcendentals=0)

    swap = [(k, k ^ 1) for k in range(n)]
    right, left = [], []
    for k, chip in enumerate(ring):
        for c in range(2):
            right.append((2 * chip + c, 2 * ring[(k + 1) % size] + c))
            left.append((2 * chip + c, 2 * ring[(k - 1) % size] + c))

    anywhere = pl.BlockSpec(memory_space=pl.ANY)

    def after(before, args):
        return [anywhere] + [pl.BlockSpec()] * len(args)

    def pick(wanted, source, cost, *before):
        return pl.pallas_call(
            functools.partial(pick_kernel, ring, wanted, block),
            in_specs=[anywhere] * (1 + len(before)),
            out_specs=[anywhere] * len(wanted),
            out_shape=[
                jax.ShapeDtypeStruct((len(distances), people, width), bf16)
                for distances, _, _, width in wanted
            ],
            scratch_shapes=[pltpu.SemaphoreType.DMA((sum(len(w[0]) for w in wanted),))],
            compiler_params=params,
            cost_estimate=cost,
            name="pick_blocks",
        )(pltpu.with_memory_space_constraint(genotype, source), *before)

    order = [reach]
    for d in range(reach - 1, 0, -1):
        order += [d, size - d]
    order += [0]
    peer, own_far, peer_far = {}, {}, {}

    def swapped(distances, sent):
        got = lax.ppermute(sent, "ind", swap)
        peer.update({d: (got, k, 0) for k, d in enumerate(distances)})

    def far(piece):
        return [(order[:1], True, piece * part, part), (order[:1], False, piece * part, part)]

    def whole(distances):
        return [(distances, True, 0, block)] if distances else []

    later = [b for b in (order[3:5], order[5:]) if b]
    last, own_far[0] = pick(far(0), pltpu.HBM, small)
    peer_far[0] = lax.ppermute(last, "ind", swap)
    mine, _ = lax.optimization_barrier((residual, last))
    residual_other = lax.ppermute(mine, "ind", swap)
    wanted = (far(1) if pieces > 1 else []) + whole(order[1:3])
    if wanted:
        found = pick(wanted, pltpu.HBM, heavy, last)
        last = found[0]
        if pieces > 1:
            peer_far[1], own_far[1] = lax.ppermute(found[0], "ind", swap), found[1]
        if order[1:3]:
            swapped(order[1:3], found[-1])
    res = last = pl.pallas_call(
        flip_kernel,
        in_specs=after(last, (residual, residual_other)),
        out_shape=jax.ShapeDtypeStruct((cols, 2 * people), bf16),
        compiler_params=params,
        cost_estimate=small,
        name="flip",
    )(last, residual, residual_other)

    def shape_of(width):
        return jax.ShapeDtypeStruct((width // LANES * cols + PAD, LANES), jnp.int16)

    got = {}
    for d in range(reach, 0, -1):
        for piece in range(pieces):
            low, high = piece * part, (piece + 1) * part
            if d == reach:
                args = (res, own_far[piece], peer_far[piece])
                sent = pl.pallas_call(
                    far_kernel,
                    in_specs=after(last, args),
                    out_shape=[shape_of(part // 2)] * 2,
                    compiler_params=params,
                    cost_estimate=small if piece else longest,
                    name="sum_far",
                )(last, *args)
                last = sent[0]
                got[0, piece] = lax.ppermute(sent[0], "ind", right)
                got[1, piece] = lax.ppermute(sent[1], "ind", left)
            else:
                if d == reach - 1 > 1 and piece == pieces - 1:
                    last, _ = lax.optimization_barrier((last, peer[d - 1][0]))
                for way in (1, 0):
                    w = size - d if way else d
                    args = (res, genotype, peer[w][0], got[way, piece])
                    last = pl.pallas_call(
                        functools.partial(
                            hop_kernel, ring, (w, peer[w][1]), low, high, way
                        ),
                        in_specs=after(last, args),
                        out_shape=shape_of(part),
                        compiler_params=params,
                        cost_estimate=heavy if d == reach - 1 else middle,
                        name="sum_hop",
                    )(last, *args)
                    got[way, piece] = lax.ppermute(last, "ind", left if way else right)
            if later and (d, piece) in ((reach, pieces - 1), (reach - 1, 0)):
                if d == reach > 1:
                    last, _ = lax.optimization_barrier((last, peer[d - 1][0]))
                distances = later.pop(0)
                (last,) = pick(whole(distances), pltpu.VMEM, light, last)
                swapped(distances, last)

    near = last = pl.pallas_call(
        functools.partial(near_kernel, ring, (0, peer[0][1])),
        in_specs=after(last, (res, genotype, peer[0][0])),
        out_shape=jax.ShapeDtypeStruct((cols, block), f32),
        compiler_params=params,
        cost_estimate=light,
        name="sum_near",
    )(last, res, genotype, peer[0][0])

    prior = prior_logit.reshape(1, cols)
    scale = slab_scale.reshape(1, cols)

    def full(shape):
        return pl.BlockSpec(shape, lambda i: (0,) * len(shape))

    effects = []
    for piece in range(pieces):
        args = (near, got[0, piece], got[1, piece], incl_old, mean_old, prior, scale)
        last = pl.pallas_call(
            functools.partial(effect_kernel, total, piece * part),
            in_specs=after(last, args),
            out_shape=jax.ShapeDtypeStruct((part, cols), bf16),
            compiler_params=params,
            cost_estimate=light,
            name="effect",
        )(last, *args)
        effects.append(last)

    def update(piece, outs, before):
        rows = pl.BlockSpec((part, cols), lambda i, piece=piece: (piece, 0))
        return pl.pallas_call(
            functools.partial(update_kernel, total, piece * part),
            grid=(1,),
            in_specs=[anywhere, full((cols, block))]
            + [full(got[way, piece].shape) for way in range(2)]
            + [rows] * 2
            + [full((1, cols))] * 2
            + [anywhere] * len(outs),
            out_specs=[rows, rows, full((8, LANES))],
            out_shape=[jax.ShapeDtypeStruct((block, cols), f32)] * 2
            + [jax.ShapeDtypeStruct((8, LANES), f32)],
            input_output_aliases={8: 0, 9: 1} if outs else {},
            compiler_params=params,
            cost_estimate=small,
            name="update",
        )(before, near, got[0, piece], got[1, piece], incl_old, mean_old, prior, scale, *outs)

    eta_shape = jax.ShapeDtypeStruct((people, cols), f32)
    def product(found, eta, before, cost):
        args, places = list(eta), []
        for d, low, effect in reversed(found):
            piece = low // part
            there = (peer_far[piece], 0, piece * part) if d == reach else peer[d]
            args = [effect, genotype, there[0]] + args
            places = [((d, *there[1:]), low)] + places
        return pl.pallas_call(
            functools.partial(eta_kernel, ring, places, not eta),
            in_specs=after(before, args),
            out_shape=[eta_shape] * 2,
            compiler_params=params,
            cost_estimate=cost,
            name="add_eta",
        )(before, *args)

    eta = product([(0, piece * part, effects[piece]) for piece in range(pieces)], (), last, small)
    last = eta[0]
    held = {(way, piece): effects[piece] for way in range(2) for piece in range(pieces)}
    etas = [eta[0]]
    outs, updated, final = (), 0, []
    for hop in range(1, reach + 1):
        for piece in range(pieces):
            for way in (1, 0):
                message = held[way, piece]
                perm = left if way else right
                d, low = (hop if way else size - hop), piece * part
                if hop > 1:
                    message, _ = lax.optimization_barrier((message, etas[-2 * pieces - 1]))
                near_half = way * (part // 2)
                halved = message.shape[0] != part
                if hop == reach:
                    if not halved:
                        message = message[near_half : near_half + part // 2]
                    held[way, piece] = lax.ppermute(message, "ind", perm)
                    found = [(d, low + near_half, held[way, piece])]
                elif hop == reach - 1 and piece == pieces - 1:
                    far_half = part // 2 - near_half
                    first = message[near_half : near_half + part // 2]
                    first = held[way, piece] = lax.ppermute(first, "ind", perm)
                    message, _ = lax.optimization_barrier((message, etas[-2 * pieces]))
                    second = message[far_half : far_half + part // 2]
                    second = lax.ppermute(second, "ind", perm)
                    found = [(d, low + near_half, first), (d, low + far_half, second)]
                else:
                    held[way, piece] = lax.ppermute(message, "ind", perm)
                    found = [(d, low, held[way, piece])]
                if hop == reach and piece == pieces - 1:
                    final += found
                    continue
                eta = product(found, eta, last, small if len(etas) == 1 or (hop, piece) >= (reach - 1, pieces - 1) else light)
                last = eta[0]
                etas.append(last)
        if updated < pieces and hop < reach:
            *outs, last = update(updated, outs, last)
            updated += 1
    while updated < pieces:
        *outs, last = update(updated, outs, last)
        updated += 1

    half = people // 2
    eta_got = [lax.ppermute(eta[1][k : k + half], "ind", swap) for k in (0, half)]
    others = [lax.ppermute(effect, "ind", swap) for _, _, effect in final]
    mine = pl.pallas_call(
        functools.partial(own_kernel, ring, [(d, low, False) for d, low, _ in final]),
        out_shape=eta_shape,
        compiler_params=params,
        cost_estimate=heavy,
        name="own_last",
    )(genotype, eta[0], offset.reshape(1, cols), *[effect for _, _, effect in final])
    resid_new = pl.pallas_call(
        functools.partial(end_kernel, ring, [(d, low, True) for d, low, _ in final]),
        out_shape=eta_shape,
        compiler_params=params,
        cost_estimate=light,
        name="new_residual",
    )(genotype, mine, *eta_got, labels, *others)
    return (outs[0], outs[1], resid_new)


def solution(mesh):
    split = P(("groups", "ind"), None)
    return jax.shard_map(
        functools.partial(on_device, ring_of(mesh.devices)),
        mesh=mesh,
        in_specs=(split, split, split, split, split, P(), P(), P()),
        out_specs=(split, split, split),
        check_vma=False,
    )
```

```python
import functools

import jax
import jax.numpy as jnp
from jax import lax
from jax.experimental import pallas as pl
from jax.experimental.pallas import tpu as pltpu
from jax.sharding import PartitionSpec as P

STEPS = 256.0
TOP = 32700.0
PAD = 16
LANES = 128
VMEM = 14 * 1024 * 1024


def ring_of(devices):
    chips = devices[0, ::2]
    where = [getattr(d, "coords", None) for d in chips]
    count = len(where)
    plain = list(range(count))
    if any(w is None for w in where):
        where = [(0, k % 2, k // 2) for k in plain]
    varying = [k for k in range(3) if len({w[k] for w in where}) > 1]
    if len(varying) != 2:
        return sorted(plain, key=lambda k: tuple(where[k]))
    short, long = sorted(varying, key=lambda k: len({w[k] for w in where}))
    low = min(w[short] for w in where)
    if len({w[short] for w in where}) != 2:
        return plain
    up = sorted((k for k in plain if where[k][short] == low), key=lambda k: where[k][long])
    down = sorted((k for k in plain if where[k][short] != low), key=lambda k: -where[k][long])
    return up + down


def owners_of(ring, distances):
    chip = lax.div(lax.axis_index("ind"), 2)
    spot = jnp.int32(0)
    for k, c in enumerate(ring):
        spot = jnp.where(chip == c, k, spot)
    found = []
    for d in distances:
        at = lax.rem(spot + d, len(ring))
        owner = jnp.int32(ring[0])
        for k, c in enumerate(ring):
            owner = jnp.where(at == k, c, owner)
        found.append(owner)
    return found


def pick_kernel(ring, wanted, block, genotype_ref, *refs):
    outs, sems = refs[-1 - len(wanted) : -1], refs[-1]
    core = lax.rem(lax.axis_index("ind"), 2)
    copies = []
    for out_ref, (distances, swapped, low, _) in zip(outs, wanted):
        parity = 1 - core if swapped else core
        width = out_ref.shape[2]
        for k, owner in enumerate(owners_of(ring, distances)):
            at = pl.multiple_of((2 * owner + parity) * block + low, LANES)
            copies.append(
                pltpu.make_async_copy(
                    genotype_ref.at[:, pl.ds(at, width)], out_ref.at[k], sems.at[len(copies)]
                )
            )
            copies[-1].start()
    for copy in copies:
        copy.wait()


def flip_kernel(before_ref, mine_ref, other_ref, out_ref):
    people = mine_ref.shape[0]
    out_ref[:, :people] = mine_ref[...].T
    out_ref[:, people:] = other_ref[...].T


def own_columns(ring, own_ref, d, low, high, swapped=False):
    (owner,) = owners_of(ring, [d])
    block = own_ref.shape[1] // (2 * len(ring))
    core = lax.rem(lax.axis_index("ind"), 2)
    at = (2 * owner + (1 - core if swapped else core)) * block + low
    return own_ref[:, pl.ds(pl.multiple_of(at, LANES), high - low)]


def local_sum(res_ref, own, other):
    people = own.shape[0]
    return jnp.dot(
        res_ref[:, :people], own, preferred_element_type=jnp.float32
    ) + jnp.dot(res_ref[:, people:], other, preferred_element_type=jnp.float32)


def decode(ref):
    rows = ref.shape[0] - PAD
    code = ref[rows:, :].astype(jnp.float32)[:1, :]
    return ref[:rows, :].astype(jnp.float32) * (jnp.exp2(code * (1.0 / STEPS)) * (1.0 / TOP))


def encode(ref, tiles):
    height = tiles[0].shape[0]
    top = functools.reduce(jnp.maximum, [jnp.abs(t) for t in tiles])
    top = jnp.maximum(jnp.max(top, axis=0, keepdims=True), 1e-30)
    code = jnp.ceil(jnp.log2(top) * STEPS)
    scale = TOP * jnp.exp2(code * (-1.0 / STEPS))
    for k, t in enumerate(tiles):
        ref[k * height : (k + 1) * height, :] = (
            jnp.round(t * scale).astype(jnp.int32).astype(jnp.int16)
        )
    ref[len(tiles) * height :, :] = (
        jnp.broadcast_to(code, (PAD, LANES)).astype(jnp.int32).astype(jnp.int16)
    )


def tiles_of(total):
    return [total[:, k : k + LANES] for k in range(0, total.shape[1], LANES)]


def far_kernel(before_ref, res_ref, own_ref, peer_ref, right_ref, left_ref):
    tiles = tiles_of(local_sum(res_ref, own_ref[0], peer_ref[0]))
    half = len(tiles) // 2
    encode(right_ref, tiles[:half])
    encode(left_ref, tiles[half:])


def hop_kernel(ring, at, low, high, way, before_ref, res_ref, own_ref, peer_ref, got_ref, out_ref):
    own = own_columns(ring, own_ref, at[0], low, high)
    add_and_send(local_sum(res_ref, own, peer_ref[at[1], :, low:high]), way, got_ref, out_ref)


def add_kernel(way, before_ref, local_ref, got_ref, out_ref):
    add_and_send(local_ref[...], way, got_ref, out_ref)


def add_and_send(local, way, got_ref, out_ref):
    tiles = tiles_of(local)
    got = decode(got_ref)
    height = tiles[0].shape[0]
    count = got.shape[0] // height
    first = 0 if way == 0 else len(tiles) - count
    for k in range(count):
        tiles[first + k] = tiles[first + k] + got[k * height : (k + 1) * height, :]
    encode(out_ref, tiles)


def local_kernel(ring, at, low, high, before_ref, res_ref, own_ref, peer_ref, out_ref):
    own = own_columns(ring, own_ref, at[0], low, high)
    out_ref[...] = local_sum(res_ref, own, peer_ref[at[1], :, low:high])


def new_state(total, low, first, rows, refs):
    corr_ref, right_ref, left_ref, incl_ref, mean_ref, prior_ref, scale_ref = refs
    height = corr_ref.shape[0]
    right, left = decode(right_ref), decode(left_ref)
    scale = scale_ref[...]
    shrink = scale / (1.0 + scale)
    start = prior_ref[...] - 0.5 * jnp.log1p(scale)
    steep = 0.5 * total * shrink
    tiles = rows // LANES
    for k in range(tiles):
        corr = corr_ref[:, low + k * LANES : low + (k + 1) * LANES]
        for got, way in ((right, 0), (left, 1)):
            count = got.shape[0] // height
            skip = 0 if way == 0 else tiles - count
            if skip <= k < skip + count:
                corr = corr + got[(k - skip) * height : (k - skip + 1) * height, :]
        at = slice(first + k * LANES, first + (k + 1) * LANES)
        incl = incl_ref[at, :]
        stat = corr.T * (1.0 / total) + incl * mean_ref[at, :]
        mean_new = stat * shrink
        incl_new = 0.5 * incl + 0.5 * jax.nn.sigmoid(start + steep * stat * stat)
        yield slice(k * LANES, (k + 1) * LANES), incl_new, mean_new


def effect_kernel(total, low, before_ref, *refs):
    out_ref = refs[-1]
    for rows, incl_new, mean_new in new_state(total, low, low, out_ref.shape[0], refs[:7]):
        out_ref[rows, :] = (incl_new * mean_new).astype(jnp.bfloat16)


def update_kernel(total, low, before_ref, *refs):
    incl_new_ref, mean_new_ref, token_ref = refs[-3:]
    token_ref[...] = jnp.zeros_like(token_ref)
    rows_all = incl_new_ref.shape[0]
    for rows, incl_new, mean_new in new_state(total, low, 0, rows_all, refs[:7]):
        incl_new_ref[rows, :] = incl_new
        mean_new_ref[rows, :] = mean_new


def eta_kernel(ring, places, first, before_ref, *refs):
    out_ref, out_other_ref = refs[-2:]
    mine = other = None
    for k, (at, low) in enumerate(places):
        effect_ref, own_ref, peer_ref = refs[3 * k : 3 * k + 3]
        effect = effect_ref[...]
        high = low + effect.shape[0]
        own = own_columns(ring, own_ref, at[0], low, high)
        a = jnp.dot(own, effect, preferred_element_type=jnp.float32)
        b = jnp.dot(peer_ref[at[1], :, low - at[2] : high - at[2]], effect, preferred_element_type=jnp.float32)
        mine = a if mine is None else mine + a
        other = b if other is None else other + b
    if not first:
        mine = mine + refs[3 * len(places)][...]
        other = other + refs[3 * len(places) + 1][...]
    out_ref[...] = mine
    out_other_ref[...] = other


def columns_product(ring, places, genotype_ref, refs, eta):
    for effect_ref, (d, low, swapped) in zip(refs, places):
        own = own_columns(ring, genotype_ref, d, low, low + effect_ref.shape[0], swapped)
        eta = eta + jnp.dot(own, effect_ref[...], preferred_element_type=jnp.float32)
    return eta


def own_kernel(ring, places, genotype_ref, eta_ref, offset_ref, *refs):
    eta = eta_ref[...] + offset_ref[...]
    refs[-1][...] = columns_product(ring, places, genotype_ref, refs, eta)


def other_kernel(ring, places, genotype_ref, eta_ref, upper_ref, lower_ref, *refs):
    got = jnp.concatenate([upper_ref[...], lower_ref[...]], axis=0)
    refs[-1][...] = columns_product(ring, places, genotype_ref, refs, eta_ref[...] + got)


def end_kernel(ring, places, genotype_ref, eta_ref, labels_ref, *refs):
    eta = columns_product(ring, places, genotype_ref, refs, eta_ref[...])
    refs[-1][...] = 4.0 * (labels_ref[...].astype(jnp.float32) - jax.nn.sigmoid(eta))


def on_device(ring, genotype, residual, labels, incl_old, mean_old, prior_logit, slab_scale, offset):
    n = lax.axis_size("ind")
    people, cols = residual.shape
    total = float(people * n)
    block = incl_old.shape[0]
    size = len(ring)
    reach = size // 2
    pieces = 2 if block % (4 * LANES) == 0 else 1
    part = block // pieces
    f32, bf16 = jnp.float32, jnp.bfloat16
    params = pltpu.CompilerParams(vmem_limit_bytes=VMEM)
    small = pl.CostEstimate(flops=1, bytes_accessed=1, transcendentals=0)
    longest = pl.CostEstimate(flops=25 * 10**9, bytes_accessed=10**6, transcendentals=0)
    heavy = pl.CostEstimate(flops=10**10, bytes_accessed=10**6, transcendentals=0)
    middle = pl.CostEstimate(flops=4 * 10**9, bytes_accessed=10**6, transcendentals=0)
    light = pl.CostEstimate(flops=2 * 10**9, bytes_accessed=10**6, transcendentals=0)

    swap = [(k, k ^ 1) for k in range(n)]
    right, left = [], []
    for k, chip in enumerate(ring):
        for c in range(2):
            right.append((2 * chip + c, 2 * ring[(k + 1) % size] + c))
            left.append((2 * chip + c, 2 * ring[(k - 1) % size] + c))

    anywhere = pl.BlockSpec(memory_space=pl.ANY)

    def after(before, args):
        return [anywhere] + [pl.BlockSpec()] * len(args)

    def pick(wanted, source, cost, *before):
        return pl.pallas_call(
            functools.partial(pick_kernel, ring, wanted, block),
            in_specs=[anywhere] * (1 + len(before)),
            out_specs=[anywhere] * len(wanted),
            out_shape=[
                jax.ShapeDtypeStruct((len(distances), people, width), bf16)
                for distances, _, _, width in wanted
            ],
            scratch_shapes=[pltpu.SemaphoreType.DMA((sum(len(w[0]) for w in wanted),))],
            compiler_params=params,
            cost_estimate=cost,
            name="pick_blocks",
        )(pltpu.with_memory_space_constraint(genotype, source), *before)

    order = [reach]
    for d in range(reach - 1, 0, -1):
        order += [d, size - d]
    order += [0]
    peer, own_far, peer_far = {}, {}, {}

    def swapped(distances, sent):
        got = lax.ppermute(sent, "ind", swap)
        peer.update({d: (got, k, 0) for k, d in enumerate(distances)})

    def far(piece):
        return [(order[:1], True, piece * part, part), (order[:1], False, piece * part, part)]

    def whole(distances):
        return [(distances, True, 0, block)] if distances else []

    later = [b for b in (order[3:5], order[5:]) if b]
    last, own_far[0] = pick(far(0), pltpu.HBM, small)
    peer_far[0] = lax.ppermute(last, "ind", swap)
    mine, _ = lax.optimization_barrier((residual, last))
    residual_other = lax.ppermute(mine, "ind", swap)
    wanted = (far(1) if pieces > 1 else []) + whole(order[1:3])
    if wanted:
        found = pick(wanted, pltpu.HBM, heavy, last)
        last = found[0]
        if pieces > 1:
            peer_far[1], own_far[1] = lax.ppermute(found[0], "ind", swap), found[1]
        if order[1:3]:
            swapped(order[1:3], found[-1])
    res = last = pl.pallas_call(
        flip_kernel,
        in_specs=after(last, (residual, residual_other)),
        out_shape=jax.ShapeDtypeStruct((cols, 2 * people), bf16),
        compiler_params=params,
        cost_estimate=small,
        name="flip",
    )(last, residual, residual_other)

    def shape_of(width):
        return jax.ShapeDtypeStruct((width // LANES * cols + PAD, LANES), jnp.int16)

    def local(d, low, high, before, cost):
        args = (res, genotype, peer[d][0])
        return pl.pallas_call(
            functools.partial(local_kernel, ring, (d, peer[d][1]), low, high),
            in_specs=after(before, args),
            out_shape=jax.ShapeDtypeStruct((cols, high - low), f32),
            compiler_params=params,
            cost_estimate=cost,
            name="sum_local",
        )(before, *args)

    got = {}
    for d in range(reach, 0, -1):
        for piece in range(pieces):
            low, high = piece * part, (piece + 1) * part
            if d == reach:
                args = (res, own_far[piece], peer_far[piece])
                sent = pl.pallas_call(
                    far_kernel,
                    in_specs=after(last, args),
                    out_shape=[shape_of(part // 2)] * 2,
                    compiler_params=params,
                    cost_estimate=small if piece else longest,
                    name="sum_far",
                )(last, *args)
                last = sent[0]
                got[0, piece] = lax.ppermute(sent[0], "ind", right)
                got[1, piece] = lax.ppermute(sent[1], "ind", left)
            else:
                if d == reach - 1 > 1 and piece == pieces - 1:
                    last, _ = lax.optimization_barrier((last, peer[d - 1][0]))
                ahead = {}
                if d == reach - 1 and piece == 0:
                    for way in (1, 0):
                        w = size - d if way else d
                        ahead[way] = last = local(w, low, high, last, light)
                for way in (1, 0):
                    w = size - d if way else d
                    if ahead:
                        kernel = functools.partial(add_kernel, way)
                        args = (ahead[way], got[way, piece])
                    else:
                        kernel = functools.partial(
                            hop_kernel, ring, (w, peer[w][1]), low, high, way
                        )
                        args = (res, genotype, peer[w][0], got[way, piece])
                    last = pl.pallas_call(
                        kernel,
                        in_specs=after(last, args),
                        out_shape=shape_of(part),
                        compiler_params=params,
                        cost_estimate=heavy if d == reach - 1 else middle,
                        name="sum_hop",
                    )(last, *args)
                    got[way, piece] = lax.ppermute(last, "ind", left if way else right)
            if later and (d, piece) in ((reach, pieces - 1), (reach - 1, 0)):
                if d == reach > 1:
                    last, _ = lax.optimization_barrier((last, peer[d - 1][0]))
                distances = later.pop(0)
                (last,) = pick(whole(distances), pltpu.VMEM, light, last)
                swapped(distances, last)

    near = last = local(0, 0, block, last, light)

    prior = prior_logit.reshape(1, cols)
    scale = slab_scale.reshape(1, cols)

    def full(shape):
        return pl.BlockSpec(shape, lambda i: (0,) * len(shape))

    effects = []
    for piece in range(pieces):
        args = (near, got[0, piece], got[1, piece], incl_old, mean_old, prior, scale)
        last = pl.pallas_call(
            functools.partial(effect_kernel, total, piece * part),
            in_specs=after(last, args),
            out_shape=jax.ShapeDtypeStruct((part, cols), bf16),
            compiler_params=params,
            cost_estimate=light,
            name="effect",
        )(last, *args)
        effects.append(last)

    def update(piece, outs, before):
        rows = pl.BlockSpec((part, cols), lambda i, piece=piece: (piece, 0))
        return pl.pallas_call(
            functools.partial(update_kernel, total, piece * part),
            grid=(1,),
            in_specs=[anywhere, full((cols, block))]
            + [full(got[way, piece].shape) for way in range(2)]
            + [rows] * 2
            + [full((1, cols))] * 2
            + [anywhere] * len(outs),
            out_specs=[rows, rows, full((8, LANES))],
            out_shape=[jax.ShapeDtypeStruct((block, cols), f32)] * 2
            + [jax.ShapeDtypeStruct((8, LANES), f32)],
            input_output_aliases={8: 0, 9: 1} if outs else {},
            compiler_params=params,
            cost_estimate=small,
            name="update",
        )(before, near, got[0, piece], got[1, piece], incl_old, mean_old, prior, scale, *outs)

    eta_shape = jax.ShapeDtypeStruct((people, cols), f32)
    def product(found, eta, before, cost):
        args, places = list(eta), []
        for d, low, effect in reversed(found):
            piece = low // part
            there = (peer_far[piece], 0, piece * part) if d == reach else peer[d]
            args = [effect, genotype, there[0]] + args
            places = [((d, *there[1:]), low)] + places
        return pl.pallas_call(
            functools.partial(eta_kernel, ring, places, not eta),
            in_specs=after(before, args),
            out_shape=[eta_shape] * 2,
            compiler_params=params,
            cost_estimate=cost,
            name="add_eta",
        )(before, *args)

    eta = product([(0, piece * part, effects[piece]) for piece in range(pieces)], (), last, small)
    last = eta[0]
    held = {(way, piece): effects[piece] for way in range(2) for piece in range(pieces)}
    etas = [eta[0]]
    outs, updated, final = (), 0, []
    for hop in range(1, reach + 1):
        for piece in range(pieces):
            for way in (1, 0):
                message = held[way, piece]
                perm = left if way else right
                d, low = (hop if way else size - hop), piece * part
                if hop > 1:
                    message, _ = lax.optimization_barrier((message, etas[-2 * pieces - 1]))
                near_half = way * (part // 2)
                halved = message.shape[0] != part
                if hop == reach:
                    if not halved:
                        message = message[near_half : near_half + part // 2]
                    held[way, piece] = lax.ppermute(message, "ind", perm)
                    found = [(d, low + near_half, held[way, piece])]
                elif hop == reach - 1 and piece == pieces - 1:
                    far_half = part // 2 - near_half
                    first = message[near_half : near_half + part // 2]
                    first = held[way, piece] = lax.ppermute(first, "ind", perm)
                    message, _ = lax.optimization_barrier((message, etas[-2 * pieces]))
                    second = message[far_half : far_half + part // 2]
                    second = lax.ppermute(second, "ind", perm)
                    found = [(d, low + near_half, first), (d, low + far_half, second)]
                else:
                    held[way, piece] = lax.ppermute(message, "ind", perm)
                    found = [(d, low, held[way, piece])]
                if hop == reach and piece == pieces - 1:
                    final += found
                    continue
                eta = product(found, eta, last, small if len(etas) == 1 or (hop, piece) >= (reach - 1, pieces - 1) else light)
                last = eta[0]
                etas.append(last)
        if updated < pieces and hop < reach:
            *outs, last = update(updated, outs, last)
            updated += 1
    while updated < pieces:
        *outs, last = update(updated, outs, last)
        updated += 1

    half = people // 2
    eta_got = [lax.ppermute(eta[1][k : k + half], "ind", swap) for k in (0, half)]
    others = [lax.ppermute(effect, "ind", swap) for _, _, effect in final]
    mine = pl.pallas_call(
        functools.partial(own_kernel, ring, [(d, low, False) for d, low, _ in final]),
        out_shape=eta_shape,
        compiler_params=params,
        cost_estimate=heavy,
        name="own_last",
    )(genotype, eta[0], offset.reshape(1, cols), *[effect for _, _, effect in final])
    there = [(d, low, True) for d, low, _ in final]
    mine = pl.pallas_call(
        functools.partial(other_kernel, ring, there[:1]),
        out_shape=eta_shape,
        compiler_params=params,
        cost_estimate=heavy,
        name="other_last",
    )(genotype, mine, *eta_got, others[0])
    resid_new = pl.pallas_call(
        functools.partial(end_kernel, ring, there[1:]),
        out_shape=eta_shape,
        compiler_params=params,
        cost_estimate=light,
        name="new_residual",
    )(genotype, mine, labels, *others[1:])
    return (outs[0], outs[1], resid_new)


def solution(mesh):
    split = P(("groups", "ind"), None)
    return jax.shard_map(
        functools.partial(on_device, ring_of(mesh.devices)),
        mesh=mesh,
        in_specs=(split, split, split, split, split, P(), P(), P()),
        out_specs=(split, split, split),
        check_vma=False,
    )
```

```python
import functools

import jax
import jax.numpy as jnp
from jax import lax
from jax.experimental import pallas as pl
from jax.experimental.pallas import tpu as pltpu
from jax.sharding import PartitionSpec as P

STEPS = 256.0
TOP = 32700.0
PAD = 16
LANES = 128
VMEM = 14 * 1024 * 1024


def ring_of(devices):
    chips = devices[0, ::2]
    where = [getattr(d, "coords", None) for d in chips]
    count = len(where)
    plain = list(range(count))
    if any(w is None for w in where):
        where = [(0, k % 2, k // 2) for k in plain]
    varying = [k for k in range(3) if len({w[k] for w in where}) > 1]
    if len(varying) != 2:
        return sorted(plain, key=lambda k: tuple(where[k]))
    short, long = sorted(varying, key=lambda k: len({w[k] for w in where}))
    low = min(w[short] for w in where)
    if len({w[short] for w in where}) != 2:
        return plain
    up = sorted((k for k in plain if where[k][short] == low), key=lambda k: where[k][long])
    down = sorted((k for k in plain if where[k][short] != low), key=lambda k: -where[k][long])
    return up + down


def owners_of(ring, distances):
    chip = lax.div(lax.axis_index("ind"), 2)
    spot = jnp.int32(0)
    for k, c in enumerate(ring):
        spot = jnp.where(chip == c, k, spot)
    found = []
    for d in distances:
        at = lax.rem(spot + d, len(ring))
        owner = jnp.int32(ring[0])
        for k, c in enumerate(ring):
            owner = jnp.where(at == k, c, owner)
        found.append(owner)
    return found


def pick_kernel(ring, wanted, block, genotype_ref, *refs):
    outs, sems = refs[-1 - len(wanted) : -1], refs[-1]
    core = lax.rem(lax.axis_index("ind"), 2)
    copies = []
    for out_ref, (distances, swapped, low, _) in zip(outs, wanted):
        parity = 1 - core if swapped else core
        width = out_ref.shape[2]
        for k, owner in enumerate(owners_of(ring, distances)):
            at = pl.multiple_of((2 * owner + parity) * block + low, LANES)
            copies.append(
                pltpu.make_async_copy(
                    genotype_ref.at[:, pl.ds(at, width)], out_ref.at[k], sems.at[len(copies)]
                )
            )
            copies[-1].start()
    for copy in copies:
        copy.wait()


def flip_kernel(before_ref, mine_ref, other_ref, out_ref):
    people = mine_ref.shape[0]
    out_ref[:, :people] = mine_ref[...].T
    out_ref[:, people:] = other_ref[...].T


def own_columns(ring, own_ref, d, low, high, swapped=False):
    (owner,) = owners_of(ring, [d])
    block = own_ref.shape[1] // (2 * len(ring))
    core = lax.rem(lax.axis_index("ind"), 2)
    at = (2 * owner + (1 - core if swapped else core)) * block + low
    return own_ref[:, pl.ds(pl.multiple_of(at, LANES), high - low)]


def local_sum(res_ref, own, other):
    people = own.shape[0]
    return jnp.dot(
        res_ref[:, :people], own, preferred_element_type=jnp.float32
    ) + jnp.dot(res_ref[:, people:], other, preferred_element_type=jnp.float32)


def decode(ref):
    rows = ref.shape[0] - PAD
    code = ref[rows:, :].astype(jnp.float32)[:1, :]
    return ref[:rows, :].astype(jnp.float32) * (jnp.exp2(code * (1.0 / STEPS)) * (1.0 / TOP))


def encode(ref, tiles):
    height = tiles[0].shape[0]
    top = functools.reduce(jnp.maximum, [jnp.abs(t) for t in tiles])
    top = jnp.maximum(jnp.max(top, axis=0, keepdims=True), 1e-30)
    code = jnp.ceil(jnp.log2(top) * STEPS)
    scale = TOP * jnp.exp2(code * (-1.0 / STEPS))
    for k, t in enumerate(tiles):
        ref[k * height : (k + 1) * height, :] = (
            jnp.round(t * scale).astype(jnp.int32).astype(jnp.int16)
        )
    ref[len(tiles) * height :, :] = (
        jnp.broadcast_to(code, (PAD, LANES)).astype(jnp.int32).astype(jnp.int16)
    )


def tiles_of(total):
    return [total[:, k : k + LANES] for k in range(0, total.shape[1], LANES)]


def far_kernel(before_ref, res_ref, own_ref, peer_ref, right_ref, left_ref):
    tiles = tiles_of(local_sum(res_ref, own_ref[0], peer_ref[0]))
    half = len(tiles) // 2
    encode(right_ref, tiles[:half])
    encode(left_ref, tiles[half:])


def hop_kernel(
    ring, at, low, high, way, before_ref, res_ref, own_ref, peer_ref, got_ref, out_ref
):
    own = own_columns(ring, own_ref, at[0], low, high)
    tiles = tiles_of(local_sum(res_ref, own, peer_ref[at[1], :, low:high]))
    got = decode(got_ref)
    height = tiles[0].shape[0]
    count = got.shape[0] // height
    first = 0 if way == 0 else len(tiles) - count
    for k in range(count):
        tiles[first + k] = tiles[first + k] + got[k * height : (k + 1) * height, :]
    encode(out_ref, tiles)


def near_kernel(ring, at, before_ref, res_ref, own_ref, peer_ref, out_ref):
    own = own_columns(ring, own_ref, at[0], 0, peer_ref.shape[2])
    out_ref[...] = local_sum(res_ref, own, peer_ref[at[1]])


def new_state(total, low, first, rows, refs):
    corr_ref, right_ref, left_ref, incl_ref, mean_ref, prior_ref, scale_ref = refs
    height = corr_ref.shape[0]
    right, left = decode(right_ref), decode(left_ref)
    scale = scale_ref[...]
    shrink = scale / (1.0 + scale)
    start = prior_ref[...] - 0.5 * jnp.log1p(scale)
    steep = 0.5 * total * shrink
    tiles = rows // LANES
    for k in range(tiles):
        corr = corr_ref[:, low + k * LANES : low + (k + 1) * LANES]
        for got, way in ((right, 0), (left, 1)):
            count = got.shape[0] // height
            skip = 0 if way == 0 else tiles - count
            if skip <= k < skip + count:
                corr = corr + got[(k - skip) * height : (k - skip + 1) * height, :]
        at = slice(first + k * LANES, first + (k + 1) * LANES)
        incl = incl_ref[at, :]
        stat = corr.T * (1.0 / total) + incl * mean_ref[at, :]
        mean_new = stat * shrink
        incl_new = 0.5 * incl + 0.5 * jax.nn.sigmoid(start + steep * stat * stat)
        yield slice(k * LANES, (k + 1) * LANES), incl_new, mean_new


def effect_kernel(total, low, before_ref, *refs):
    out_ref = refs[-1]
    for rows, incl_new, mean_new in new_state(total, low, low, out_ref.shape[0], refs[:7]):
        out_ref[rows, :] = (incl_new * mean_new).astype(jnp.bfloat16)


def update_kernel(total, low, before_ref, *refs):
    incl_new_ref, mean_new_ref, token_ref = refs[-3:]
    token_ref[...] = jnp.zeros_like(token_ref)
    rows_all = incl_new_ref.shape[0]
    for rows, incl_new, mean_new in new_state(total, low, 0, rows_all, refs[:7]):
        incl_new_ref[rows, :] = incl_new
        mean_new_ref[rows, :] = mean_new


def eta_kernel(ring, places, first, before_ref, *refs):
    out_ref, out_other_ref = refs[-2:]
    mine = other = None
    for k, (at, low) in enumerate(places):
        effect_ref, own_ref, peer_ref = refs[3 * k : 3 * k + 3]
        effect = effect_ref[...]
        high = low + effect.shape[0]
        own = own_columns(ring, own_ref, at[0], low, high)
        a = jnp.dot(own, effect, preferred_element_type=jnp.float32)
        b = jnp.dot(peer_ref[at[1], :, low - at[2] : high - at[2]], effect, preferred_element_type=jnp.float32)
        mine = a if mine is None else mine + a
        other = b if other is None else other + b
    if not first:
        mine = mine + refs[3 * len(places)][...]
        other = other + refs[3 * len(places) + 1][...]
    out_ref[...] = mine
    out_other_ref[...] = other


def columns_product(ring, places, genotype_ref, refs, eta):
    for effect_ref, (d, low, swapped) in zip(refs, places):
        own = own_columns(ring, genotype_ref, d, low, low + effect_ref.shape[0], swapped)
        eta = eta + jnp.dot(own, effect_ref[...], preferred_element_type=jnp.float32)
    return eta


def own_kernel(ring, places, genotype_ref, eta_ref, offset_ref, *refs):
    eta = eta_ref[...] + offset_ref[...]
    refs[-1][...] = columns_product(ring, places, genotype_ref, refs, eta)


def other_kernel(ring, places, genotype_ref, eta_ref, upper_ref, lower_ref, *refs):
    got = jnp.concatenate([upper_ref[...], lower_ref[...]], axis=0)
    refs[-1][...] = columns_product(ring, places, genotype_ref, refs, eta_ref[...] + got)


def end_kernel(ring, places, genotype_ref, eta_ref, labels_ref, *refs):
    eta = columns_product(ring, places, genotype_ref, refs, eta_ref[...])
    refs[-1][...] = 4.0 * (labels_ref[...].astype(jnp.float32) - jax.nn.sigmoid(eta))


def on_device(ring, genotype, residual, labels, incl_old, mean_old, prior_logit, slab_scale, offset):
    n = lax.axis_size("ind")
    people, cols = residual.shape
    total = float(people * n)
    block = incl_old.shape[0]
    size = len(ring)
    reach = size // 2
    pieces = 2 if block % (4 * LANES) == 0 else 1
    part = block // pieces
    f32, bf16 = jnp.float32, jnp.bfloat16
    params = pltpu.CompilerParams(vmem_limit_bytes=VMEM)
    small = pl.CostEstimate(flops=1, bytes_accessed=1, transcendentals=0)
    longest = pl.CostEstimate(flops=25 * 10**9, bytes_accessed=10**6, transcendentals=0)
    heavy = pl.CostEstimate(flops=10**10, bytes_accessed=10**6, transcendentals=0)
    middle = pl.CostEstimate(flops=4 * 10**9, bytes_accessed=10**6, transcendentals=0)
    light = pl.CostEstimate(flops=2 * 10**9, bytes_accessed=10**6, transcendentals=0)

    swap = [(k, k ^ 1) for k in range(n)]
    right, left = [], []
    for k, chip in enumerate(ring):
        for c in range(2):
            right.append((2 * chip + c, 2 * ring[(k + 1) % size] + c))
            left.append((2 * chip + c, 2 * ring[(k - 1) % size] + c))

    anywhere = pl.BlockSpec(memory_space=pl.ANY)

    def after(before, args):
        return [anywhere] + [pl.BlockSpec()] * len(args)

    def pick(wanted, source, cost, *before):
        return pl.pallas_call(
            functools.partial(pick_kernel, ring, wanted, block),
            in_specs=[anywhere] * (1 + len(before)),
            out_specs=[anywhere] * len(wanted),
            out_shape=[
                jax.ShapeDtypeStruct((len(distances), people, width), bf16)
                for distances, _, _, width in wanted
            ],
            scratch_shapes=[pltpu.SemaphoreType.DMA((sum(len(w[0]) for w in wanted),))],
            compiler_params=params,
            cost_estimate=cost,
            name="pick_blocks",
        )(pltpu.with_memory_space_constraint(genotype, source), *before)

    order = [reach]
    for d in range(reach - 1, 0, -1):
        order += [d, size - d]
    order += [0]
    peer, own_far, peer_far = {}, {}, {}

    def swapped(distances, sent):
        got = lax.ppermute(sent, "ind", swap)
        peer.update({d: (got, k, 0) for k, d in enumerate(distances)})

    def far(piece):
        return [(order[:1], True, piece * part, part), (order[:1], False, piece * part, part)]

    def whole(distances):
        return [(distances, True, 0, block)] if distances else []

    later = [b for b in (order[3:5], order[5:]) if b]
    wanted = [w for piece in range(pieces) for w in far(piece)] + whole(order[1:3])
    found = pick(wanted, pltpu.HBM, small)
    last = found[0]
    for piece in range(pieces):
        peer_far[piece] = lax.ppermute(found[2 * piece], "ind", swap)
        own_far[piece] = found[2 * piece + 1]
        if piece == 0:
            mine, _ = lax.optimization_barrier((residual, last))
            residual_other = lax.ppermute(mine, "ind", swap)
    if order[1:3]:
        swapped(order[1:3], found[-1])
    res = last = pl.pallas_call(
        flip_kernel,
        in_specs=after(last, (residual, residual_other)),
        out_shape=jax.ShapeDtypeStruct((cols, 2 * people), bf16),
        compiler_params=params,
        cost_estimate=small,
        name="flip",
    )(last, residual, residual_other)

    def shape_of(width):
        return jax.ShapeDtypeStruct((width // LANES * cols + PAD, LANES), jnp.int16)

    got = {}
    for d in range(reach, 0, -1):
        for piece in range(pieces):
            low, high = piece * part, (piece + 1) * part
            if d == reach:
                args = (res, own_far[piece], peer_far[piece])
                sent = pl.pallas_call(
                    far_kernel,
                    in_specs=after(last, args),
                    out_shape=[shape_of(part // 2)] * 2,
                    compiler_params=params,
                    cost_estimate=small if piece else longest,
                    name="sum_far",
                )(last, *args)
                last = sent[0]
                got[0, piece] = lax.ppermute(sent[0], "ind", right)
                got[1, piece] = lax.ppermute(sent[1], "ind", left)
            else:
                if d == reach - 1 > 1 and piece == pieces - 1:
                    last, _ = lax.optimization_barrier((last, peer[d - 1][0]))
                for way in (1, 0):
                    w = size - d if way else d
                    args = (res, genotype, peer[w][0], got[way, piece])
                    last = pl.pallas_call(
                        functools.partial(
                            hop_kernel, ring, (w, peer[w][1]), low, high, way
                        ),
                        in_specs=after(last, args),
                        out_shape=shape_of(part),
                        compiler_params=params,
                        cost_estimate=heavy if d == reach - 1 else middle,
                        name="sum_hop",
                    )(last, *args)
                    got[way, piece] = lax.ppermute(last, "ind", left if way else right)
            if later and (d, piece) in ((reach, pieces - 1), (reach - 1, 0)):
                if d == reach > 1:
                    last, _ = lax.optimization_barrier((last, peer[d - 1][0]))
                distances = later.pop(0)
                (last,) = pick(whole(distances), pltpu.VMEM, small, last)
                swapped(distances, last)

    near = last = pl.pallas_call(
        functools.partial(near_kernel, ring, (0, peer[0][1])),
        in_specs=after(last, (res, genotype, peer[0][0])),
        out_shape=jax.ShapeDtypeStruct((cols, block), f32),
        compiler_params=params,
        cost_estimate=light,
        name="sum_near",
    )(last, res, genotype, peer[0][0])

    prior = prior_logit.reshape(1, cols)
    scale = slab_scale.reshape(1, cols)

    def full(shape):
        return pl.BlockSpec(shape, lambda i: (0,) * len(shape))

    effects = []
    for piece in range(pieces):
        args = (near, got[0, piece], got[1, piece], incl_old, mean_old, prior, scale)
        last = pl.pallas_call(
            functools.partial(effect_kernel, total, piece * part),
            in_specs=after(last, args),
            out_shape=jax.ShapeDtypeStruct((part, cols), bf16),
            compiler_params=params,
            cost_estimate=light,
            name="effect",
        )(last, *args)
        effects.append(last)

    def update(piece, outs, before):
        rows = pl.BlockSpec((part, cols), lambda i, piece=piece: (piece, 0))
        return pl.pallas_call(
            functools.partial(update_kernel, total, piece * part),
            grid=(1,),
            in_specs=[anywhere, full((cols, block))]
            + [full(got[way, piece].shape) for way in range(2)]
            + [rows] * 2
            + [full((1, cols))] * 2
            + [anywhere] * len(outs),
            out_specs=[rows, rows, full((8, LANES))],
            out_shape=[jax.ShapeDtypeStruct((block, cols), f32)] * 2
            + [jax.ShapeDtypeStruct((8, LANES), f32)],
            input_output_aliases={8: 0, 9: 1} if outs else {},
            compiler_params=params,
            cost_estimate=small,
            name="update",
        )(before, near, got[0, piece], got[1, piece], incl_old, mean_old, prior, scale, *outs)

    eta_shape = jax.ShapeDtypeStruct((people, cols), f32)
    def product(found, eta, before, cost):
        args, places = list(eta), []
        for d, low, effect in reversed(found):
            piece = low // part
            there = (peer_far[piece], 0, piece * part) if d == reach else peer[d]
            args = [effect, genotype, there[0]] + args
            places = [((d, *there[1:]), low)] + places
        return pl.pallas_call(
            functools.partial(eta_kernel, ring, places, not eta),
            in_specs=after(before, args),
            out_shape=[eta_shape] * 2,
            compiler_params=params,
            cost_estimate=cost,
            name="add_eta",
        )(before, *args)

    eta = product([(0, piece * part, effects[piece]) for piece in range(pieces)], (), last, small)
    last = eta[0]
    held = {(way, piece): effects[piece] for way in range(2) for piece in range(pieces)}
    etas = [eta[0]]
    outs, updated, final = (), 0, []
    for hop in range(1, reach + 1):
        for piece in range(pieces):
            for way in (1, 0):
                message = held[way, piece]
                perm = left if way else right
                d, low = (hop if way else size - hop), piece * part
                if hop > 1:
                    message, _ = lax.optimization_barrier((message, etas[-2 * pieces - 1]))
                near_half = way * (part // 2)
                halved = message.shape[0] != part
                if hop == reach:
                    if not halved:
                        message = message[near_half : near_half + part // 2]
                    held[way, piece] = lax.ppermute(message, "ind", perm)
                    found = [(d, low + near_half, held[way, piece])]
                elif hop == reach - 1 and piece == pieces - 1:
                    far_half = part // 2 - near_half
                    first = message[near_half : near_half + part // 2]
                    first = held[way, piece] = lax.ppermute(first, "ind", perm)
                    message, _ = lax.optimization_barrier((message, etas[-2 * pieces]))
                    second = message[far_half : far_half + part // 2]
                    second = lax.ppermute(second, "ind", perm)
                    found = [(d, low + near_half, first), (d, low + far_half, second)]
                else:
                    held[way, piece] = lax.ppermute(message, "ind", perm)
                    found = [(d, low, held[way, piece])]
                if hop == reach and piece == pieces - 1:
                    final += found
                    continue
                eta = product(found, eta, last, small if len(etas) == 1 or (hop, piece) >= (reach - 1, pieces - 1) else light)
                last = eta[0]
                etas.append(last)
        if updated < pieces and hop < reach:
            *outs, last = update(updated, outs, last)
            updated += 1
    while updated < pieces:
        *outs, last = update(updated, outs, last)
        updated += 1

    half = people // 2
    eta_got = [lax.ppermute(eta[1][k : k + half], "ind", swap) for k in (0, half)]
    others = [lax.ppermute(effect, "ind", swap) for _, _, effect in final]
    mine = pl.pallas_call(
        functools.partial(own_kernel, ring, [(d, low, False) for d, low, _ in final]),
        out_shape=eta_shape,
        compiler_params=params,
        cost_estimate=heavy,
        name="own_last",
    )(genotype, eta[0], offset.reshape(1, cols), *[effect for _, _, effect in final])
    there = [(d, low, True) for d, low, _ in final]
    mine = pl.pallas_call(
        functools.partial(other_kernel, ring, there[:1]),
        out_shape=eta_shape,
        compiler_params=params,
        cost_estimate=heavy,
        name="other_last",
    )(genotype, mine, *eta_got, others[0])
    resid_new = pl.pallas_call(
        functools.partial(end_kernel, ring, there[1:]),
        out_shape=eta_shape,
        compiler_params=params,
        cost_estimate=light,
        name="new_residual",
    )(genotype, mine, labels, *others[1:])
    return (outs[0], outs[1], resid_new)


def solution(mesh):
    split = P(("groups", "ind"), None)
    return jax.shard_map(
        functools.partial(on_device, ring_of(mesh.devices)),
        mesh=mesh,
        in_specs=(split, split, split, split, split, P(), P(), P()),
        out_specs=(split, split, split),
        check_vma=False,
    )
```

```python
import functools

import jax
import jax.numpy as jnp
from jax import lax
from jax.experimental import pallas as pl
from jax.experimental.pallas import tpu as pltpu
from jax.sharding import PartitionSpec as P

STEPS = 256.0
TOP = 32700.0
PAD = 16
LANES = 128
VMEM = 14 * 1024 * 1024


def ring_of(devices):
    chips = devices[0, ::2]
    where = [getattr(d, "coords", None) for d in chips]
    count = len(where)
    plain = list(range(count))
    if any(w is None for w in where):
        where = [(0, k % 2, k // 2) for k in plain]
    varying = [k for k in range(3) if len({w[k] for w in where}) > 1]
    if len(varying) != 2:
        return sorted(plain, key=lambda k: tuple(where[k]))
    short, long = sorted(varying, key=lambda k: len({w[k] for w in where}))
    low = min(w[short] for w in where)
    if len({w[short] for w in where}) != 2:
        return plain
    up = sorted((k for k in plain if where[k][short] == low), key=lambda k: where[k][long])
    down = sorted((k for k in plain if where[k][short] != low), key=lambda k: -where[k][long])
    return up + down


def owners_of(ring, distances):
    chip = lax.div(lax.axis_index("ind"), 2)
    spot = jnp.int32(0)
    for k, c in enumerate(ring):
        spot = jnp.where(chip == c, k, spot)
    found = []
    for d in distances:
        at = lax.rem(spot + d, len(ring))
        owner = jnp.int32(ring[0])
        for k, c in enumerate(ring):
            owner = jnp.where(at == k, c, owner)
        found.append(owner)
    return found


def pick_kernel(ring, wanted, block, genotype_ref, *refs):
    outs, sems = refs[-1 - len(wanted) : -1], refs[-1]
    core = lax.rem(lax.axis_index("ind"), 2)
    copies = []
    for out_ref, (distances, swapped, low, _) in zip(outs, wanted):
        parity = 1 - core if swapped else core
        width = out_ref.shape[2]
        for k, owner in enumerate(owners_of(ring, distances)):
            at = pl.multiple_of((2 * owner + parity) * block + low, LANES)
            copies.append(
                pltpu.make_async_copy(
                    genotype_ref.at[:, pl.ds(at, width)], out_ref.at[k], sems.at[len(copies)]
                )
            )
            copies[-1].start()
    for copy in copies:
        copy.wait()


def flip_kernel(before_ref, mine_ref, other_ref, out_ref):
    people = mine_ref.shape[0]
    out_ref[:, :people] = mine_ref[...].T
    out_ref[:, people:] = other_ref[...].T


def own_columns(ring, own_ref, d, low, high, swapped=False):
    (owner,) = owners_of(ring, [d])
    block = own_ref.shape[1] // (2 * len(ring))
    core = lax.rem(lax.axis_index("ind"), 2)
    at = (2 * owner + (1 - core if swapped else core)) * block + low
    return own_ref[:, pl.ds(pl.multiple_of(at, LANES), high - low)]


def local_sum(res_ref, own, other):
    people = own.shape[0]
    return jnp.dot(
        res_ref[:, :people], own, preferred_element_type=jnp.float32
    ) + jnp.dot(res_ref[:, people:], other, preferred_element_type=jnp.float32)


def decode(ref):
    rows = ref.shape[0] - PAD
    code = ref[rows:, :].astype(jnp.float32)[:1, :]
    return ref[:rows, :].astype(jnp.float32) * (jnp.exp2(code * (1.0 / STEPS)) * (1.0 / TOP))


def encode(ref, tiles):
    height = tiles[0].shape[0]
    top = functools.reduce(jnp.maximum, [jnp.abs(t) for t in tiles])
    top = jnp.maximum(jnp.max(top, axis=0, keepdims=True), 1e-30)
    code = jnp.ceil(jnp.log2(top) * STEPS)
    scale = TOP * jnp.exp2(code * (-1.0 / STEPS))
    for k, t in enumerate(tiles):
        ref[k * height : (k + 1) * height, :] = (
            jnp.round(t * scale).astype(jnp.int32).astype(jnp.int16)
        )
    ref[len(tiles) * height :, :] = (
        jnp.broadcast_to(code, (PAD, LANES)).astype(jnp.int32).astype(jnp.int16)
    )


def tiles_of(total):
    return [total[:, k : k + LANES] for k in range(0, total.shape[1], LANES)]


def far_kernel(before_ref, res_ref, own_ref, peer_ref, right_ref, left_ref):
    tiles = tiles_of(local_sum(res_ref, own_ref[0], peer_ref[0]))
    half = len(tiles) // 2
    encode(right_ref, tiles[:half])
    encode(left_ref, tiles[half:])


def hop_kernel(
    ring, at, low, high, way, before_ref, res_ref, own_ref, peer_ref, got_ref, out_ref
):
    own = own_columns(ring, own_ref, at[0], low, high)
    tiles = tiles_of(local_sum(res_ref, own, peer_ref[at[1], :, low:high]))
    got = decode(got_ref)
    height = tiles[0].shape[0]
    count = got.shape[0] // height
    first = 0 if way == 0 else len(tiles) - count
    for k in range(count):
        tiles[first + k] = tiles[first + k] + got[k * height : (k + 1) * height, :]
    encode(out_ref, tiles)


def near_kernel(ring, at, before_ref, res_ref, own_ref, peer_ref, out_ref):
    own = own_columns(ring, own_ref, at[0], 0, peer_ref.shape[2])
    out_ref[...] = local_sum(res_ref, own, peer_ref[at[1]])


def new_state(total, low, first, rows, refs):
    corr_ref, right_ref, left_ref, incl_ref, mean_ref, prior_ref, scale_ref = refs
    height = corr_ref.shape[0]
    right, left = decode(right_ref), decode(left_ref)
    scale = scale_ref[...]
    shrink = scale / (1.0 + scale)
    start = prior_ref[...] - 0.5 * jnp.log1p(scale)
    steep = 0.5 * total * shrink
    tiles = rows // LANES
    for k in range(tiles):
        corr = corr_ref[:, low + k * LANES : low + (k + 1) * LANES]
        for got, way in ((right, 0), (left, 1)):
            count = got.shape[0] // height
            skip = 0 if way == 0 else tiles - count
            if skip <= k < skip + count:
                corr = corr + got[(k - skip) * height : (k - skip + 1) * height, :]
        at = slice(first + k * LANES, first + (k + 1) * LANES)
        incl = incl_ref[at, :]
        stat = corr.T * (1.0 / total) + incl * mean_ref[at, :]
        mean_new = stat * shrink
        incl_new = 0.5 * incl + 0.5 * jax.nn.sigmoid(start + steep * stat * stat)
        yield slice(k * LANES, (k + 1) * LANES), incl_new, mean_new


def effect_kernel(total, low, before_ref, *refs):
    out_ref = refs[-1]
    for rows, incl_new, mean_new in new_state(total, low, low, out_ref.shape[0], refs[:7]):
        out_ref[rows, :] = (incl_new * mean_new).astype(jnp.bfloat16)


def update_kernel(total, low, before_ref, *refs):
    incl_new_ref, mean_new_ref, token_ref = refs[-3:]
    token_ref[...] = jnp.zeros_like(token_ref)
    rows_all = incl_new_ref.shape[0]
    for rows, incl_new, mean_new in new_state(total, low, 0, rows_all, refs[:7]):
        incl_new_ref[rows, :] = incl_new
        mean_new_ref[rows, :] = mean_new


def eta_kernel(ring, places, first, before_ref, *refs):
    out_ref, out_other_ref = refs[-2:]
    mine = other = None
    for k, (at, low) in enumerate(places):
        effect_ref, own_ref, peer_ref = refs[3 * k : 3 * k + 3]
        effect = effect_ref[...]
        high = low + effect.shape[0]
        own = own_columns(ring, own_ref, at[0], low, high)
        a = jnp.dot(own, effect, preferred_element_type=jnp.float32)
        b = jnp.dot(peer_ref[at[1], :, low - at[2] : high - at[2]], effect, preferred_element_type=jnp.float32)
        mine = a if mine is None else mine + a
        other = b if other is None else other + b
    if not first:
        mine = mine + refs[3 * len(places)][...]
        other = other + refs[3 * len(places) + 1][...]
    out_ref[...] = mine
    out_other_ref[...] = other


def columns_product(ring, places, genotype_ref, refs, eta):
    for effect_ref, (d, low, swapped) in zip(refs, places):
        own = own_columns(ring, genotype_ref, d, low, low + effect_ref.shape[0], swapped)
        eta = eta + jnp.dot(own, effect_ref[...], preferred_element_type=jnp.float32)
    return eta


def own_kernel(ring, places, genotype_ref, eta_ref, offset_ref, *refs):
    eta = eta_ref[...] + offset_ref[...]
    refs[-1][...] = columns_product(ring, places, genotype_ref, refs, eta)


def other_kernel(ring, places, genotype_ref, eta_ref, upper_ref, lower_ref, *refs):
    got = jnp.concatenate([upper_ref[...], lower_ref[...]], axis=0)
    refs[-1][...] = columns_product(ring, places, genotype_ref, refs, eta_ref[...] + got)


def end_kernel(ring, places, genotype_ref, eta_ref, labels_ref, *refs):
    eta = columns_product(ring, places, genotype_ref, refs, eta_ref[...])
    refs[-1][...] = 4.0 * (labels_ref[...].astype(jnp.float32) - jax.nn.sigmoid(eta))


def on_device(ring, genotype, residual, labels, incl_old, mean_old, prior_logit, slab_scale, offset):
    n = lax.axis_size("ind")
    people, cols = residual.shape
    total = float(people * n)
    block = incl_old.shape[0]
    size = len(ring)
    reach = size // 2
    pieces = 2 if block % (4 * LANES) == 0 else 1
    part = block // pieces
    f32, bf16 = jnp.float32, jnp.bfloat16
    params = pltpu.CompilerParams(vmem_limit_bytes=VMEM)
    small = pl.CostEstimate(flops=1, bytes_accessed=1, transcendentals=0)
    longest = pl.CostEstimate(flops=25 * 10**9, bytes_accessed=10**6, transcendentals=0)
    heavy = pl.CostEstimate(flops=10**10, bytes_accessed=10**6, transcendentals=0)
    middle = pl.CostEstimate(flops=4 * 10**9, bytes_accessed=10**6, transcendentals=0)
    light = pl.CostEstimate(flops=2 * 10**9, bytes_accessed=10**6, transcendentals=0)

    swap = [(k, k ^ 1) for k in range(n)]
    right, left = [], []
    for k, chip in enumerate(ring):
        for c in range(2):
            right.append((2 * chip + c, 2 * ring[(k + 1) % size] + c))
            left.append((2 * chip + c, 2 * ring[(k - 1) % size] + c))

    anywhere = pl.BlockSpec(memory_space=pl.ANY)

    def after(before, args):
        return [anywhere] + [pl.BlockSpec()] * len(args)

    def pick(wanted, source, cost, *before):
        return pl.pallas_call(
            functools.partial(pick_kernel, ring, wanted, block),
            in_specs=[anywhere] * (1 + len(before)),
            out_specs=[anywhere] * len(wanted),
            out_shape=[
                jax.ShapeDtypeStruct((len(distances), people, width), bf16)
                for distances, _, _, width in wanted
            ],
            scratch_shapes=[pltpu.SemaphoreType.DMA((sum(len(w[0]) for w in wanted),))],
            compiler_params=params,
            cost_estimate=cost,
            name="pick_blocks",
        )(pltpu.with_memory_space_constraint(genotype, source), *before)

    order = [reach]
    for d in range(reach - 1, 0, -1):
        order += [d, size - d]
    order += [0]
    peer, own_far, peer_far = {}, {}, {}

    def swapped(distances, sent):
        got = lax.ppermute(sent, "ind", swap)
        peer.update({d: (got, k, 0) for k, d in enumerate(distances)})

    def far(piece):
        return [(order[:1], True, piece * part, part), (order[:1], False, piece * part, part)]

    def whole(distances):
        return [(distances, True, 0, block)] if distances else []

    later = [b for b in (order[3:5], order[5:]) if b]
    last, own_far[0] = pick(far(0), pltpu.HBM, small)
    peer_far[0] = lax.ppermute(last, "ind", swap)
    mine, _ = lax.optimization_barrier((residual, last))
    residual_other = lax.ppermute(mine, "ind", swap)
    wanted = (far(1) if pieces > 1 else []) + whole(order[1:3])
    if wanted:
        found = pick(wanted, pltpu.HBM, heavy, last)
        last = found[0]
        if pieces > 1:
            peer_far[1], own_far[1] = lax.ppermute(found[0], "ind", swap), found[1]
        if order[1:3]:
            swapped(order[1:3], found[-1])
    res = last = pl.pallas_call(
        flip_kernel,
        in_specs=after(last, (residual, residual_other)),
        out_shape=jax.ShapeDtypeStruct((cols, 2 * people), bf16),
        compiler_params=params,
        cost_estimate=small,
        name="flip",
    )(last, residual, residual_other)

    def shape_of(width):
        return jax.ShapeDtypeStruct((width // LANES * cols + PAD, LANES), jnp.int16)

    got = {}
    for d in range(reach, 0, -1):
        for piece in range(pieces):
            low, high = piece * part, (piece + 1) * part
            if d == reach:
                args = (res, own_far[piece], peer_far[piece])
                sent = pl.pallas_call(
                    far_kernel,
                    in_specs=after(last, args),
                    out_shape=[shape_of(part // 2)] * 2,
                    compiler_params=params,
                    cost_estimate=small if piece else longest,
                    name="sum_far",
                )(last, *args)
                last = sent[0]
                got[0, piece] = lax.ppermute(sent[0], "ind", right)
                got[1, piece] = lax.ppermute(sent[1], "ind", left)
            else:
                if d == reach - 1 > 1 and piece == pieces - 1:
                    last, _ = lax.optimization_barrier((last, peer[d - 1][0]))
                for way in (0, 1):
                    w = size - d if way else d
                    args = (res, genotype, peer[w][0], got[way, piece])
                    last = pl.pallas_call(
                        functools.partial(
                            hop_kernel, ring, (w, peer[w][1]), low, high, way
                        ),
                        in_specs=after(last, args),
                        out_shape=shape_of(part),
                        compiler_params=params,
                        cost_estimate=heavy if d == reach - 1 else middle,
                        name="sum_hop",
                    )(last, *args)
                    got[way, piece] = lax.ppermute(last, "ind", left if way else right)
            if later and (d, piece) in ((reach, pieces - 1), (reach - 1, 0)):
                if d == reach > 1:
                    last, _ = lax.optimization_barrier((last, peer[d - 1][0]))
                distances = later.pop(0)
                (last,) = pick(whole(distances), pltpu.VMEM, small, last)
                swapped(distances, last)

    near = last = pl.pallas_call(
        functools.partial(near_kernel, ring, (0, peer[0][1])),
        in_specs=after(last, (res, genotype, peer[0][0])),
        out_shape=jax.ShapeDtypeStruct((cols, block), f32),
        compiler_params=params,
        cost_estimate=light,
        name="sum_near",
    )(last, res, genotype, peer[0][0])

    prior = prior_logit.reshape(1, cols)
    scale = slab_scale.reshape(1, cols)

    def full(shape):
        return pl.BlockSpec(shape, lambda i: (0,) * len(shape))

    effects = []
    for piece in range(pieces):
        args = (near, got[0, piece], got[1, piece], incl_old, mean_old, prior, scale)
        last = pl.pallas_call(
            functools.partial(effect_kernel, total, piece * part),
            in_specs=after(last, args),
            out_shape=jax.ShapeDtypeStruct((part, cols), bf16),
            compiler_params=params,
            cost_estimate=light,
            name="effect",
        )(last, *args)
        effects.append(last)

    def update(piece, outs, before):
        rows = pl.BlockSpec((part, cols), lambda i, piece=piece: (piece, 0))
        return pl.pallas_call(
            functools.partial(update_kernel, total, piece * part),
            grid=(1,),
            in_specs=[anywhere, full((cols, block))]
            + [full(got[way, piece].shape) for way in range(2)]
            + [rows] * 2
            + [full((1, cols))] * 2
            + [anywhere] * len(outs),
            out_specs=[rows, rows, full((8, LANES))],
            out_shape=[jax.ShapeDtypeStruct((block, cols), f32)] * 2
            + [jax.ShapeDtypeStruct((8, LANES), f32)],
            input_output_aliases={8: 0, 9: 1} if outs else {},
            compiler_params=params,
            cost_estimate=small,
            name="update",
        )(before, near, got[0, piece], got[1, piece], incl_old, mean_old, prior, scale, *outs)

    eta_shape = jax.ShapeDtypeStruct((people, cols), f32)
    def product(found, eta, before, cost):
        args, places = list(eta), []
        for d, low, effect in reversed(found):
            piece = low // part
            there = (peer_far[piece], 0, piece * part) if d == reach else peer[d]
            args = [effect, genotype, there[0]] + args
            places = [((d, *there[1:]), low)] + places
        return pl.pallas_call(
            functools.partial(eta_kernel, ring, places, not eta),
            in_specs=after(before, args),
            out_shape=[eta_shape] * 2,
            compiler_params=params,
            cost_estimate=cost,
            name="add_eta",
        )(before, *args)

    eta = product([(0, piece * part, effects[piece]) for piece in range(pieces)], (), last, small)
    last = eta[0]
    held = {(way, piece): effects[piece] for way in range(2) for piece in range(pieces)}
    etas = [eta[0]]
    outs, updated, final = (), 0, []
    for hop in range(1, reach + 1):
        for piece in range(pieces):
            for way in (0, 1):
                message = held[way, piece]
                perm = left if way else right
                d, low = (hop if way else size - hop), piece * part
                if hop > 1:
                    message, _ = lax.optimization_barrier((message, etas[-2 * pieces - 1]))
                near_half = way * (part // 2)
                halved = message.shape[0] != part
                if hop == reach:
                    if not halved:
                        message = message[near_half : near_half + part // 2]
                    held[way, piece] = lax.ppermute(message, "ind", perm)
                    found = [(d, low + near_half, held[way, piece])]
                elif hop == reach - 1 and piece == pieces - 1:
                    far_half = part // 2 - near_half
                    first = message[near_half : near_half + part // 2]
                    first = held[way, piece] = lax.ppermute(first, "ind", perm)
                    message, _ = lax.optimization_barrier((message, etas[-2 * pieces]))
                    second = message[far_half : far_half + part // 2]
                    second = lax.ppermute(second, "ind", perm)
                    found = [(d, low + near_half, first), (d, low + far_half, second)]
                else:
                    held[way, piece] = lax.ppermute(message, "ind", perm)
                    found = [(d, low, held[way, piece])]
                if hop == reach and piece == pieces - 1:
                    final += found
                    continue
                eta = product(found, eta, last, small if len(etas) == 1 or (hop, piece) >= (reach - 1, pieces - 1) else light)
                last = eta[0]
                etas.append(last)
        if updated < pieces and hop < reach:
            *outs, last = update(updated, outs, last)
            updated += 1
    while updated < pieces:
        *outs, last = update(updated, outs, last)
        updated += 1

    half = people // 2
    eta_got = [lax.ppermute(eta[1][k : k + half], "ind", swap) for k in (0, half)]
    others = [lax.ppermute(effect, "ind", swap) for _, _, effect in final]
    mine = pl.pallas_call(
        functools.partial(own_kernel, ring, [(d, low, False) for d, low, _ in final]),
        out_shape=eta_shape,
        compiler_params=params,
        cost_estimate=heavy,
        name="own_last",
    )(genotype, eta[0], offset.reshape(1, cols), *[effect for _, _, effect in final])
    there = [(d, low, True) for d, low, _ in final]
    mine = pl.pallas_call(
        functools.partial(other_kernel, ring, there[:1]),
        out_shape=eta_shape,
        compiler_params=params,
        cost_estimate=heavy,
        name="other_last",
    )(genotype, mine, *eta_got, others[0])
    resid_new = pl.pallas_call(
        functools.partial(end_kernel, ring, there[1:]),
        out_shape=eta_shape,
        compiler_params=params,
        cost_estimate=light,
        name="new_residual",
    )(genotype, mine, labels, *others[1:])
    return (outs[0], outs[1], resid_new)


def solution(mesh):
    split = P(("groups", "ind"), None)
    return jax.shard_map(
        functools.partial(on_device, ring_of(mesh.devices)),
        mesh=mesh,
        in_specs=(split, split, split, split, split, P(), P(), P()),
        out_specs=(split, split, split),
        check_vma=False,
    )
```

```python
import functools

import jax
import jax.numpy as jnp
from jax import lax
from jax.experimental import pallas as pl
from jax.experimental.pallas import tpu as pltpu
from jax.sharding import PartitionSpec as P

STEPS = 256.0
TOP = 32700.0
PAD = 16
LANES = 128
VMEM = 14 * 1024 * 1024


def ring_of(devices):
    chips = devices[0, ::2]
    where = [getattr(d, "coords", None) for d in chips]
    count = len(where)
    plain = list(range(count))
    if any(w is None for w in where):
        where = [(0, k % 2, k // 2) for k in plain]
    varying = [k for k in range(3) if len({w[k] for w in where}) > 1]
    if len(varying) != 2:
        return sorted(plain, key=lambda k: tuple(where[k]))
    short, long = sorted(varying, key=lambda k: len({w[k] for w in where}))
    low = min(w[short] for w in where)
    if len({w[short] for w in where}) != 2:
        return plain
    up = sorted((k for k in plain if where[k][short] == low), key=lambda k: where[k][long])
    down = sorted((k for k in plain if where[k][short] != low), key=lambda k: -where[k][long])
    return up + down


def owners_of(ring, distances):
    chip = lax.div(lax.axis_index("ind"), 2)
    spot = jnp.int32(0)
    for k, c in enumerate(ring):
        spot = jnp.where(chip == c, k, spot)
    found = []
    for d in distances:
        at = lax.rem(spot + d, len(ring))
        owner = jnp.int32(ring[0])
        for k, c in enumerate(ring):
            owner = jnp.where(at == k, c, owner)
        found.append(owner)
    return found


def pick_kernel(ring, wanted, block, genotype_ref, *refs):
    outs, sems = refs[-1 - len(wanted) : -1], refs[-1]
    core = lax.rem(lax.axis_index("ind"), 2)
    copies = []
    for out_ref, (distances, swapped, low, _) in zip(outs, wanted):
        parity = 1 - core if swapped else core
        width = out_ref.shape[2]
        for k, owner in enumerate(owners_of(ring, distances)):
            at = pl.multiple_of((2 * owner + parity) * block + low, LANES)
            copies.append(
                pltpu.make_async_copy(
                    genotype_ref.at[:, pl.ds(at, width)], out_ref.at[k], sems.at[len(copies)]
                )
            )
            copies[-1].start()
    for copy in copies:
        copy.wait()


def flip_kernel(before_ref, mine_ref, other_ref, out_ref):
    people = mine_ref.shape[0]
    out_ref[:, :people] = mine_ref[...].T
    out_ref[:, people:] = other_ref[...].T


def own_columns(ring, own_ref, d, low, high, swapped=False):
    (owner,) = owners_of(ring, [d])
    block = own_ref.shape[1] // (2 * len(ring))
    core = lax.rem(lax.axis_index("ind"), 2)
    at = (2 * owner + (1 - core if swapped else core)) * block + low
    return own_ref[:, pl.ds(pl.multiple_of(at, LANES), high - low)]


def local_sum(res_ref, own, other):
    people = own.shape[0]
    return jnp.dot(
        res_ref[:, :people], own, preferred_element_type=jnp.float32
    ) + jnp.dot(res_ref[:, people:], other, preferred_element_type=jnp.float32)


def decode(ref):
    rows = ref.shape[0] - PAD
    code = ref[rows:, :].astype(jnp.float32)[:1, :]
    return ref[:rows, :].astype(jnp.float32) * (jnp.exp2(code * (1.0 / STEPS)) * (1.0 / TOP))


def encode(ref, tiles):
    height = tiles[0].shape[0]
    top = functools.reduce(jnp.maximum, [jnp.abs(t) for t in tiles])
    top = jnp.maximum(jnp.max(top, axis=0, keepdims=True), 1e-30)
    code = jnp.ceil(jnp.log2(top) * STEPS)
    scale = TOP * jnp.exp2(code * (-1.0 / STEPS))
    for k, t in enumerate(tiles):
        ref[k * height : (k + 1) * height, :] = (
            jnp.round(t * scale).astype(jnp.int32).astype(jnp.int16)
        )
    ref[len(tiles) * height :, :] = (
        jnp.broadcast_to(code, (PAD, LANES)).astype(jnp.int32).astype(jnp.int16)
    )


def tiles_of(total):
    return [total[:, k : k + LANES] for k in range(0, total.shape[1], LANES)]


def far_kernel(before_ref, res_ref, own_ref, peer_ref, right_ref, left_ref):
    tiles = tiles_of(local_sum(res_ref, own_ref[0], peer_ref[0]))
    half = len(tiles) // 2
    encode(right_ref, tiles[:half])
    encode(left_ref, tiles[half:])


def hop_kernel(
    ring, at, low, high, way, before_ref, res_ref, own_ref, peer_ref, got_ref, out_ref
):
    own = own_columns(ring, own_ref, at[0], low, high)
    tiles = tiles_of(local_sum(res_ref, own, peer_ref[at[1], :, low:high]))
    got = decode(got_ref)
    height = tiles[0].shape[0]
    count = got.shape[0] // height
    first = 0 if way == 0 else len(tiles) - count
    for k in range(count):
        tiles[first + k] = tiles[first + k] + got[k * height : (k + 1) * height, :]
    encode(out_ref, tiles)


def near_kernel(ring, at, before_ref, res_ref, own_ref, peer_ref, out_ref):
    own = own_columns(ring, own_ref, at[0], 0, peer_ref.shape[2])
    out_ref[...] = local_sum(res_ref, own, peer_ref[at[1]])


def new_state(total, low, first, rows, refs):
    corr_ref, right_ref, left_ref, incl_ref, mean_ref, prior_ref, scale_ref = refs
    height = corr_ref.shape[0]
    right, left = decode(right_ref), decode(left_ref)
    scale = scale_ref[...]
    shrink = scale / (1.0 + scale)
    start = prior_ref[...] - 0.5 * jnp.log1p(scale)
    steep = 0.5 * total * shrink
    tiles = rows // LANES
    for k in range(tiles):
        corr = corr_ref[:, low + k * LANES : low + (k + 1) * LANES]
        for got, way in ((right, 0), (left, 1)):
            count = got.shape[0] // height
            skip = 0 if way == 0 else tiles - count
            if skip <= k < skip + count:
                corr = corr + got[(k - skip) * height : (k - skip + 1) * height, :]
        at = slice(first + k * LANES, first + (k + 1) * LANES)
        incl = incl_ref[at, :]
        stat = corr.T * (1.0 / total) + incl * mean_ref[at, :]
        mean_new = stat * shrink
        incl_new = 0.5 * incl + 0.5 * jax.nn.sigmoid(start + steep * stat * stat)
        yield slice(k * LANES, (k + 1) * LANES), incl_new, mean_new


def effect_kernel(total, low, before_ref, *refs):
    out_ref = refs[-1]
    for rows, incl_new, mean_new in new_state(total, low, low, out_ref.shape[0], refs[:7]):
        out_ref[rows, :] = (incl_new * mean_new).astype(jnp.bfloat16)


def update_kernel(total, low, before_ref, *refs):
    incl_new_ref, mean_new_ref, token_ref = refs[-3:]
    token_ref[...] = jnp.zeros_like(token_ref)
    rows_all = incl_new_ref.shape[0]
    for rows, incl_new, mean_new in new_state(total, low, 0, rows_all, refs[:7]):
        incl_new_ref[rows, :] = incl_new
        mean_new_ref[rows, :] = mean_new


def eta_kernel(ring, places, first, before_ref, *refs):
    out_ref, out_other_ref = refs[-2:]
    mine = other = None
    for k, (at, low) in enumerate(places):
        effect_ref, own_ref, peer_ref = refs[3 * k : 3 * k + 3]
        effect = effect_ref[...]
        high = low + effect.shape[0]
        own = own_columns(ring, own_ref, at[0], low, high)
        a = jnp.dot(own, effect, preferred_element_type=jnp.float32)
        b = jnp.dot(peer_ref[at[1], :, low - at[2] : high - at[2]], effect, preferred_element_type=jnp.float32)
        mine = a if mine is None else mine + a
        other = b if other is None else other + b
    if not first:
        mine = mine + refs[3 * len(places)][...]
        other = other + refs[3 * len(places) + 1][...]
    out_ref[...] = mine
    out_other_ref[...] = other


def columns_product(ring, places, genotype_ref, refs, eta):
    for effect_ref, (d, low, swapped) in zip(refs, places):
        own = own_columns(ring, genotype_ref, d, low, low + effect_ref.shape[0], swapped)
        eta = eta + jnp.dot(own, effect_ref[...], preferred_element_type=jnp.float32)
    return eta


def own_kernel(ring, places, genotype_ref, eta_ref, offset_ref, *refs):
    eta = eta_ref[...] + offset_ref[...]
    refs[-1][...] = columns_product(ring, places, genotype_ref, refs, eta)


def other_kernel(ring, places, genotype_ref, eta_ref, upper_ref, lower_ref, *refs):
    got = jnp.concatenate([upper_ref[...], lower_ref[...]], axis=0)
    refs[-1][...] = columns_product(ring, places, genotype_ref, refs, eta_ref[...] + got)


def end_kernel(ring, places, genotype_ref, eta_ref, labels_ref, *refs):
    eta = columns_product(ring, places, genotype_ref, refs, eta_ref[...])
    refs[-1][...] = 4.0 * (labels_ref[...].astype(jnp.float32) - jax.nn.sigmoid(eta))


def on_device(ring, genotype, residual, labels, incl_old, mean_old, prior_logit, slab_scale, offset):
    n = lax.axis_size("ind")
    people, cols = residual.shape
    total = float(people * n)
    block = incl_old.shape[0]
    size = len(ring)
    reach = size // 2
    pieces = 2 if block % (4 * LANES) == 0 else 1
    part = block // pieces
    f32, bf16 = jnp.float32, jnp.bfloat16
    params = pltpu.CompilerParams(vmem_limit_bytes=VMEM)
    small = pl.CostEstimate(flops=1, bytes_accessed=1, transcendentals=0)
    longest = pl.CostEstimate(flops=25 * 10**9, bytes_accessed=10**6, transcendentals=0)
    heavy = pl.CostEstimate(flops=10**10, bytes_accessed=10**6, transcendentals=0)
    middle = pl.CostEstimate(flops=4 * 10**9, bytes_accessed=10**6, transcendentals=0)
    light = pl.CostEstimate(flops=2 * 10**9, bytes_accessed=10**6, transcendentals=0)

    swap = [(k, k ^ 1) for k in range(n)]
    right, left = [], []
    for k, chip in enumerate(ring):
        for c in range(2):
            right.append((2 * chip + c, 2 * ring[(k + 1) % size] + c))
            left.append((2 * chip + c, 2 * ring[(k - 1) % size] + c))

    anywhere = pl.BlockSpec(memory_space=pl.ANY)

    def after(before, args):
        return [anywhere] + [pl.BlockSpec()] * len(args)

    def pick(wanted, source, cost, *before):
        return pl.pallas_call(
            functools.partial(pick_kernel, ring, wanted, block),
            in_specs=[anywhere] * (1 + len(before)),
            out_specs=[anywhere] * len(wanted),
            out_shape=[
                jax.ShapeDtypeStruct((len(distances), people, width), bf16)
                for distances, _, _, width in wanted
            ],
            scratch_shapes=[pltpu.SemaphoreType.DMA((sum(len(w[0]) for w in wanted),))],
            compiler_params=params,
            cost_estimate=cost,
            name="pick_blocks",
        )(pltpu.with_memory_space_constraint(genotype, source), *before)

    order = [reach]
    for d in range(reach - 1, 0, -1):
        order += [d, size - d]
    order += [0]
    peer, own_far, peer_far = {}, {}, {}

    def swapped(distances, sent):
        got = lax.ppermute(sent, "ind", swap)
        peer.update({d: (got, k, 0) for k, d in enumerate(distances)})

    def far(piece):
        return [(order[:1], True, piece * part, part), (order[:1], False, piece * part, part)]

    def whole(distances):
        return [(distances, True, 0, block)] if distances else []

    later = [b for b in (order[3:5], order[5:]) if b]
    last, own_far[0] = pick(far(0), pltpu.HBM, small)
    peer_far[0] = lax.ppermute(last, "ind", swap)
    mine, _ = lax.optimization_barrier((residual, last))
    residual_other = lax.ppermute(mine, "ind", swap)
    wanted = (far(1) if pieces > 1 else []) + whole(order[1:3])
    if wanted:
        found = pick(wanted, pltpu.HBM, heavy, last)
        last = found[0]
        if pieces > 1:
            peer_far[1], own_far[1] = lax.ppermute(found[0], "ind", swap), found[1]
        if order[1:3]:
            swapped(order[1:3], found[-1])
    res = last = pl.pallas_call(
        flip_kernel,
        in_specs=after(last, (residual, residual_other)),
        out_shape=jax.ShapeDtypeStruct((cols, 2 * people), bf16),
        compiler_params=params,
        cost_estimate=small,
        name="flip",
    )(last, residual, residual_other)

    def shape_of(width):
        return jax.ShapeDtypeStruct((width // LANES * cols + PAD, LANES), jnp.int16)

    got = {}
    for d in range(reach, 0, -1):
        for piece in range(pieces):
            low, high = piece * part, (piece + 1) * part
            if d == reach:
                args = (res, own_far[piece], peer_far[piece])
                sent = pl.pallas_call(
                    far_kernel,
                    in_specs=after(last, args),
                    out_shape=[shape_of(part // 2)] * 2,
                    compiler_params=params,
                    cost_estimate=small if piece else longest,
                    name="sum_far",
                )(last, *args)
                last = sent[0]
                got[0, piece] = lax.ppermute(sent[0], "ind", right)
                got[1, piece] = lax.ppermute(sent[1], "ind", left)
            else:
                if d == reach - 1 > 1 and piece == pieces - 1:
                    last, _ = lax.optimization_barrier((last, peer[d - 1][0]))
                for way in (0, 1):
                    w = size - d if way else d
                    args = (res, genotype, peer[w][0], got[way, piece])
                    last = pl.pallas_call(
                        functools.partial(
                            hop_kernel, ring, (w, peer[w][1]), low, high, way
                        ),
                        in_specs=after(last, args),
                        out_shape=shape_of(part),
                        compiler_params=params,
                        cost_estimate=heavy if d == reach - 1 else middle,
                        name="sum_hop",
                    )(last, *args)
                    got[way, piece] = lax.ppermute(last, "ind", left if way else right)
            if later and (d, piece) in ((reach, pieces - 1), (reach - 1, 0)):
                if d == reach > 1:
                    last, _ = lax.optimization_barrier((last, peer[d - 1][0]))
                distances = later.pop(0)
                (last,) = pick(whole(distances), pltpu.VMEM, small, last)
                swapped(distances, last)

    near = last = pl.pallas_call(
        functools.partial(near_kernel, ring, (0, peer[0][1])),
        in_specs=after(last, (res, genotype, peer[0][0])),
        out_shape=jax.ShapeDtypeStruct((cols, block), f32),
        compiler_params=params,
        cost_estimate=light,
        name="sum_near",
    )(last, res, genotype, peer[0][0])

    prior = prior_logit.reshape(1, cols)
    scale = slab_scale.reshape(1, cols)

    def full(shape):
        return pl.BlockSpec(shape, lambda i: (0,) * len(shape))

    effects = []
    for piece in range(pieces):
        args = (near, got[0, piece], got[1, piece], incl_old, mean_old, prior, scale)
        last = pl.pallas_call(
            functools.partial(effect_kernel, total, piece * part),
            in_specs=after(last, args),
            out_shape=jax.ShapeDtypeStruct((part, cols), bf16),
            compiler_params=params,
            cost_estimate=light,
            name="effect",
        )(last, *args)
        effects.append(last)

    def update(piece, outs, before):
        rows = pl.BlockSpec((part, cols), lambda i, piece=piece: (piece, 0))
        return pl.pallas_call(
            functools.partial(update_kernel, total, piece * part),
            grid=(1,),
            in_specs=[anywhere, full((cols, block))]
            + [full(got[way, piece].shape) for way in range(2)]
            + [rows] * 2
            + [full((1, cols))] * 2
            + [anywhere] * len(outs),
            out_specs=[rows, rows, full((8, LANES))],
            out_shape=[jax.ShapeDtypeStruct((block, cols), f32)] * 2
            + [jax.ShapeDtypeStruct((8, LANES), f32)],
            input_output_aliases={8: 0, 9: 1} if outs else {},
            compiler_params=params,
            cost_estimate=small,
            name="update",
        )(before, near, got[0, piece], got[1, piece], incl_old, mean_old, prior, scale, *outs)

    eta_shape = jax.ShapeDtypeStruct((people, cols), f32)
    def product(found, eta, before, cost):
        args, places = list(eta), []
        for d, low, effect in reversed(found):
            piece = low // part
            there = (peer_far[piece], 0, piece * part) if d == reach else peer[d]
            args = [effect, genotype, there[0]] + args
            places = [((d, *there[1:]), low)] + places
        return pl.pallas_call(
            functools.partial(eta_kernel, ring, places, not eta),
            in_specs=after(before, args),
            out_shape=[eta_shape] * 2,
            compiler_params=params,
            cost_estimate=cost,
            name="add_eta",
        )(before, *args)

    eta = product([(0, piece * part, effects[piece]) for piece in range(pieces)], (), last, small)
    last = eta[0]
    held = {(way, piece): effects[piece] for way in range(2) for piece in range(pieces)}
    etas = [eta[0]]
    outs, updated, final = (), 0, []
    for hop in range(1, reach + 1):
        for piece in range(pieces):
            for way in (0, 1):
                message = held[way, piece]
                perm = left if way else right
                d, low = (hop if way else size - hop), piece * part
                if hop > 1:
                    message, _ = lax.optimization_barrier((message, etas[-2 * pieces - 1]))
                near_half = way * (part // 2)
                halved = message.shape[0] != part
                if hop == reach:
                    if not halved:
                        message = message[near_half : near_half + part // 2]
                    held[way, piece] = lax.ppermute(message, "ind", perm)
                    found = [(d, low + near_half, held[way, piece])]
                elif hop == reach - 1 and piece == pieces - 1:
                    far_half = part // 2 - near_half
                    first = message[near_half : near_half + part // 2]
                    first = held[way, piece] = lax.ppermute(first, "ind", perm)
                    message, _ = lax.optimization_barrier((message, etas[-2 * pieces]))
                    second = message[far_half : far_half + part // 2]
                    second = lax.ppermute(second, "ind", perm)
                    found = [(d, low + near_half, first), (d, low + far_half, second)]
                else:
                    held[way, piece] = lax.ppermute(message, "ind", perm)
                    found = [(d, low, held[way, piece])]
                if hop == reach and piece == pieces - 1:
                    final += found
                    continue
                eta = product(found, eta, last, small if len(etas) == 1 or (hop, piece) >= (reach - 1, pieces - 1) else light)
                last = eta[0]
                etas.append(last)
            if updated < pieces and hop < reach and piece == (pieces - 1 if hop == 1 else 0):
                *outs, last = update(updated, outs, last)
                updated += 1
    while updated < pieces:
        *outs, last = update(updated, outs, last)
        updated += 1

    half = people // 2
    eta_got = [lax.ppermute(eta[1][k : k + half], "ind", swap) for k in (0, half)]
    others = [lax.ppermute(effect, "ind", swap) for _, _, effect in final]
    mine = pl.pallas_call(
        functools.partial(own_kernel, ring, [(d, low, False) for d, low, _ in final]),
        out_shape=eta_shape,
        compiler_params=params,
        cost_estimate=heavy,
        name="own_last",
    )(genotype, eta[0], offset.reshape(1, cols), *[effect for _, _, effect in final])
    there = [(d, low, True) for d, low, _ in final]
    mine = pl.pallas_call(
        functools.partial(other_kernel, ring, there[:1]),
        out_shape=eta_shape,
        compiler_params=params,
        cost_estimate=heavy,
        name="other_last",
    )(genotype, mine, *eta_got, others[0])
    resid_new = pl.pallas_call(
        functools.partial(end_kernel, ring, there[1:]),
        out_shape=eta_shape,
        compiler_params=params,
        cost_estimate=light,
        name="new_residual",
    )(genotype, mine, labels, *others[1:])
    return (outs[0], outs[1], resid_new)


def solution(mesh):
    split = P(("groups", "ind"), None)
    return jax.shard_map(
        functools.partial(on_device, ring_of(mesh.devices)),
        mesh=mesh,
        in_specs=(split, split, split, split, split, P(), P(), P()),
        out_specs=(split, split, split),
        check_vma=False,
    )
```

```python
import functools

import jax
import jax.numpy as jnp
from jax import lax
from jax.experimental import pallas as pl
from jax.experimental.pallas import tpu as pltpu
from jax.sharding import PartitionSpec as P

STEPS = 256.0
TOP = 32700.0
PAD = 16
LANES = 128
VMEM = 14 * 1024 * 1024


def ring_of(devices):
    chips = devices[0, ::2]
    where = [getattr(d, "coords", None) for d in chips]
    count = len(where)
    plain = list(range(count))
    if any(w is None for w in where):
        where = [(0, k % 2, k // 2) for k in plain]
    varying = [k for k in range(3) if len({w[k] for w in where}) > 1]
    if len(varying) != 2:
        return sorted(plain, key=lambda k: tuple(where[k]))
    short, long = sorted(varying, key=lambda k: len({w[k] for w in where}))
    low = min(w[short] for w in where)
    if len({w[short] for w in where}) != 2:
        return plain
    up = sorted((k for k in plain if where[k][short] == low), key=lambda k: where[k][long])
    down = sorted((k for k in plain if where[k][short] != low), key=lambda k: -where[k][long])
    return up + down


def owners_of(ring, distances):
    chip = lax.div(lax.axis_index("ind"), 2)
    spot = jnp.int32(0)
    for k, c in enumerate(ring):
        spot = jnp.where(chip == c, k, spot)
    found = []
    for d in distances:
        at = lax.rem(spot + d, len(ring))
        owner = jnp.int32(ring[0])
        for k, c in enumerate(ring):
            owner = jnp.where(at == k, c, owner)
        found.append(owner)
    return found


def pick_kernel(ring, wanted, block, genotype_ref, *refs):
    outs, sems = refs[-1 - len(wanted) : -1], refs[-1]
    core = lax.rem(lax.axis_index("ind"), 2)
    copies = []
    for out_ref, (distances, swapped, low, _) in zip(outs, wanted):
        parity = 1 - core if swapped else core
        width = out_ref.shape[2]
        for k, owner in enumerate(owners_of(ring, distances)):
            at = pl.multiple_of((2 * owner + parity) * block + low, LANES)
            copies.append(
                pltpu.make_async_copy(
                    genotype_ref.at[:, pl.ds(at, width)], out_ref.at[k], sems.at[len(copies)]
                )
            )
            copies[-1].start()
    for copy in copies:
        copy.wait()


def flip_kernel(before_ref, mine_ref, other_ref, out_ref):
    people = mine_ref.shape[0]
    out_ref[:, :people] = mine_ref[...].T
    out_ref[:, people:] = other_ref[...].T


def own_columns(ring, own_ref, d, low, high, swapped=False):
    (owner,) = owners_of(ring, [d])
    block = own_ref.shape[1] // (2 * len(ring))
    core = lax.rem(lax.axis_index("ind"), 2)
    at = (2 * owner + (1 - core if swapped else core)) * block + low
    return own_ref[:, pl.ds(pl.multiple_of(at, LANES), high - low)]


def local_sum(res_ref, own, other):
    people = own.shape[0]
    return jnp.dot(
        res_ref[:, :people], own, preferred_element_type=jnp.float32
    ) + jnp.dot(res_ref[:, people:], other, preferred_element_type=jnp.float32)


def decode(ref):
    rows = ref.shape[0] - PAD
    code = ref[rows:, :].astype(jnp.float32)[:1, :]
    return ref[:rows, :].astype(jnp.float32) * (jnp.exp2(code * (1.0 / STEPS)) * (1.0 / TOP))


def encode(ref, tiles):
    height = tiles[0].shape[0]
    top = functools.reduce(jnp.maximum, [jnp.abs(t) for t in tiles])
    top = jnp.maximum(jnp.max(top, axis=0, keepdims=True), 1e-30)
    code = jnp.ceil(jnp.log2(top) * STEPS)
    scale = TOP * jnp.exp2(code * (-1.0 / STEPS))
    for k, t in enumerate(tiles):
        ref[k * height : (k + 1) * height, :] = (
            jnp.round(t * scale).astype(jnp.int32).astype(jnp.int16)
        )
    ref[len(tiles) * height :, :] = (
        jnp.broadcast_to(code, (PAD, LANES)).astype(jnp.int32).astype(jnp.int16)
    )


def tiles_of(total):
    return [total[:, k : k + LANES] for k in range(0, total.shape[1], LANES)]


def far_kernel(before_ref, res_ref, own_ref, peer_ref, right_ref, left_ref):
    tiles = tiles_of(local_sum(res_ref, own_ref[0], peer_ref[0]))
    half = len(tiles) // 2
    encode(right_ref, tiles[:half])
    encode(left_ref, tiles[half:])


def hop_kernel(
    ring, at, low, high, way, before_ref, res_ref, own_ref, peer_ref, got_ref, out_ref
):
    own = own_columns(ring, own_ref, at[0], low, high)
    tiles = tiles_of(local_sum(res_ref, own, peer_ref[at[1], :, low:high]))
    got = decode(got_ref)
    height = tiles[0].shape[0]
    count = got.shape[0] // height
    first = 0 if way == 0 else len(tiles) - count
    for k in range(count):
        tiles[first + k] = tiles[first + k] + got[k * height : (k + 1) * height, :]
    encode(out_ref, tiles)


def near_kernel(ring, at, before_ref, res_ref, own_ref, peer_ref, out_ref):
    own = own_columns(ring, own_ref, at[0], 0, peer_ref.shape[2])
    out_ref[...] = local_sum(res_ref, own, peer_ref[at[1]])


def new_state(total, low, first, rows, refs):
    corr_ref, right_ref, left_ref, incl_ref, mean_ref, prior_ref, scale_ref = refs
    height = corr_ref.shape[0]
    right, left = decode(right_ref), decode(left_ref)
    scale = scale_ref[...]
    shrink = scale / (1.0 + scale)
    start = prior_ref[...] - 0.5 * jnp.log1p(scale)
    steep = 0.5 * total * shrink
    tiles = rows // LANES
    for k in range(tiles):
        corr = corr_ref[:, low + k * LANES : low + (k + 1) * LANES]
        for got, way in ((right, 0), (left, 1)):
            count = got.shape[0] // height
            skip = 0 if way == 0 else tiles - count
            if skip <= k < skip + count:
                corr = corr + got[(k - skip) * height : (k - skip + 1) * height, :]
        at = slice(first + k * LANES, first + (k + 1) * LANES)
        incl = incl_ref[at, :]
        stat = corr.T * (1.0 / total) + incl * mean_ref[at, :]
        mean_new = stat * shrink
        incl_new = 0.5 * incl + 0.5 * jax.nn.sigmoid(start + steep * stat * stat)
        yield slice(k * LANES, (k + 1) * LANES), incl_new, mean_new


def effect_kernel(total, low, before_ref, *refs):
    out_ref = refs[-1]
    for rows, incl_new, mean_new in new_state(total, low, low, out_ref.shape[0], refs[:7]):
        out_ref[rows, :] = (incl_new * mean_new).astype(jnp.bfloat16)


def update_kernel(total, low, before_ref, *refs):
    incl_new_ref, mean_new_ref, token_ref = refs[-3:]
    token_ref[...] = jnp.zeros_like(token_ref)
    rows_all = incl_new_ref.shape[0]
    for rows, incl_new, mean_new in new_state(total, low, 0, rows_all, refs[:7]):
        incl_new_ref[rows, :] = incl_new
        mean_new_ref[rows, :] = mean_new


def eta_kernel(ring, places, first, before_ref, *refs):
    out_ref, out_other_ref = refs[-2:]
    mine = other = None
    for k, (at, low) in enumerate(places):
        effect_ref, own_ref, peer_ref = refs[3 * k : 3 * k + 3]
        effect = effect_ref[...]
        high = low + effect.shape[0]
        own = own_columns(ring, own_ref, at[0], low, high)
        a = jnp.dot(own, effect, preferred_element_type=jnp.float32)
        b = jnp.dot(peer_ref[at[1], :, low - at[2] : high - at[2]], effect, preferred_element_type=jnp.float32)
        mine = a if mine is None else mine + a
        other = b if other is None else other + b
    if not first:
        mine = mine + refs[3 * len(places)][...]
        other = other + refs[3 * len(places) + 1][...]
    out_ref[...] = mine
    out_other_ref[...] = other


def columns_product(ring, places, genotype_ref, refs, eta):
    for effect_ref, (d, low, swapped) in zip(refs, places):
        own = own_columns(ring, genotype_ref, d, low, low + effect_ref.shape[0], swapped)
        eta = eta + jnp.dot(own, effect_ref[...], preferred_element_type=jnp.float32)
    return eta


def own_kernel(ring, places, genotype_ref, eta_ref, offset_ref, *refs):
    eta = eta_ref[...] + offset_ref[...]
    refs[-1][...] = columns_product(ring, places, genotype_ref, refs, eta)


def other_kernel(ring, places, genotype_ref, eta_ref, upper_ref, lower_ref, *refs):
    got = jnp.concatenate([upper_ref[...], lower_ref[...]], axis=0)
    refs[-1][...] = columns_product(ring, places, genotype_ref, refs, eta_ref[...] + got)


def end_kernel(ring, places, genotype_ref, eta_ref, labels_ref, *refs):
    eta = columns_product(ring, places, genotype_ref, refs, eta_ref[...])
    refs[-1][...] = 4.0 * (labels_ref[...].astype(jnp.float32) - jax.nn.sigmoid(eta))


def on_device(ring, genotype, residual, labels, incl_old, mean_old, prior_logit, slab_scale, offset):
    n = lax.axis_size("ind")
    people, cols = residual.shape
    total = float(people * n)
    block = incl_old.shape[0]
    size = len(ring)
    reach = size // 2
    pieces = 2 if block % (4 * LANES) == 0 else 1
    part = block // pieces
    f32, bf16 = jnp.float32, jnp.bfloat16
    params = pltpu.CompilerParams(vmem_limit_bytes=VMEM)
    small = pl.CostEstimate(flops=1, bytes_accessed=1, transcendentals=0)
    longest = pl.CostEstimate(flops=25 * 10**9, bytes_accessed=10**6, transcendentals=0)
    heavy = pl.CostEstimate(flops=10**10, bytes_accessed=10**6, transcendentals=0)
    middle = pl.CostEstimate(flops=4 * 10**9, bytes_accessed=10**6, transcendentals=0)
    light = pl.CostEstimate(flops=2 * 10**9, bytes_accessed=10**6, transcendentals=0)

    swap = [(k, k ^ 1) for k in range(n)]
    right, left = [], []
    for k, chip in enumerate(ring):
        for c in range(2):
            right.append((2 * chip + c, 2 * ring[(k + 1) % size] + c))
            left.append((2 * chip + c, 2 * ring[(k - 1) % size] + c))

    anywhere = pl.BlockSpec(memory_space=pl.ANY)

    def after(before, args):
        return [anywhere] + [pl.BlockSpec()] * len(args)

    def pick(wanted, source, cost, *before):
        return pl.pallas_call(
            functools.partial(pick_kernel, ring, wanted, block),
            in_specs=[anywhere] * (1 + len(before)),
            out_specs=[anywhere] * len(wanted),
            out_shape=[
                jax.ShapeDtypeStruct((len(distances), people, width), bf16)
                for distances, _, _, width in wanted
            ],
            scratch_shapes=[pltpu.SemaphoreType.DMA((sum(len(w[0]) for w in wanted),))],
            compiler_params=params,
            cost_estimate=cost,
            name="pick_blocks",
        )(pltpu.with_memory_space_constraint(genotype, source), *before)

    order = [reach]
    for d in range(reach - 1, 0, -1):
        order += [d, size - d]
    order += [0]
    peer, own_far, peer_far = {}, {}, {}

    def swapped(distances, sent):
        got = lax.ppermute(sent, "ind", swap)
        peer.update({d: (got, k, 0) for k, d in enumerate(distances)})

    def far(piece):
        return [(order[:1], True, piece * part, part), (order[:1], False, piece * part, part)]

    def whole(distances):
        return [(distances, True, 0, block)] if distances else []

    later = [b for b in (order[3:5], order[5:]) if b]
    last, own_far[0] = pick(far(0), pltpu.HBM, small)
    peer_far[0] = lax.ppermute(last, "ind", swap)
    mine, _ = lax.optimization_barrier((residual, last))
    residual_other = lax.ppermute(mine, "ind", swap)
    wanted = (far(1) if pieces > 1 else []) + whole(order[1:3])
    if wanted:
        found = pick(wanted, pltpu.HBM, heavy, last)
        last = found[0]
        if pieces > 1:
            peer_far[1], own_far[1] = lax.ppermute(found[0], "ind", swap), found[1]
        if order[1:3]:
            swapped(order[1:3], found[-1])
    res = last = pl.pallas_call(
        flip_kernel,
        in_specs=after(last, (residual, residual_other)),
        out_shape=jax.ShapeDtypeStruct((cols, 2 * people), bf16),
        compiler_params=params,
        cost_estimate=small,
        name="flip",
    )(last, residual, residual_other)

    def shape_of(width):
        return jax.ShapeDtypeStruct((width // LANES * cols + PAD, LANES), jnp.int16)

    got = {}
    for d in range(reach, 0, -1):
        for piece in range(pieces):
            low, high = piece * part, (piece + 1) * part
            if d == reach:
                args = (res, own_far[piece], peer_far[piece])
                sent = pl.pallas_call(
                    far_kernel,
                    in_specs=after(last, args),
                    out_shape=[shape_of(part // 2)] * 2,
                    compiler_params=params,
                    cost_estimate=small if piece else longest,
                    name="sum_far",
                )(last, *args)
                last = sent[0]
                got[0, piece] = lax.ppermute(sent[0], "ind", right)
                got[1, piece] = lax.ppermute(sent[1], "ind", left)
            else:
                if d == reach - 1 > 1 and piece == pieces - 1:
                    last, _ = lax.optimization_barrier((last, peer[d - 1][0]))
                for way in (1, 0):
                    w = size - d if way else d
                    args = (res, genotype, peer[w][0], got[way, piece])
                    last = pl.pallas_call(
                        functools.partial(
                            hop_kernel, ring, (w, peer[w][1]), low, high, way
                        ),
                        in_specs=after(last, args),
                        out_shape=shape_of(part),
                        compiler_params=params,
                        cost_estimate=heavy if d == reach - 1 else middle,
                        name="sum_hop",
                    )(last, *args)
                    got[way, piece] = lax.ppermute(last, "ind", left if way else right)
            if later and (d, piece) in ((reach, pieces - 1), (reach - 1, 0)):
                if d == reach > 1:
                    last, _ = lax.optimization_barrier((last, peer[d - 1][0]))
                distances = later.pop(0)
                (last,) = pick(whole(distances), pltpu.VMEM, light, last)
                swapped(distances, last)

    near = last = pl.pallas_call(
        functools.partial(near_kernel, ring, (0, peer[0][1])),
        in_specs=after(last, (res, genotype, peer[0][0])),
        out_shape=jax.ShapeDtypeStruct((cols, block), f32),
        compiler_params=params,
        cost_estimate=light,
        name="sum_near",
    )(last, res, genotype, peer[0][0])

    prior = prior_logit.reshape(1, cols)
    scale = slab_scale.reshape(1, cols)

    def full(shape):
        return pl.BlockSpec(shape, lambda i: (0,) * len(shape))

    effects = []
    for piece in range(pieces):
        args = (near, got[0, piece], got[1, piece], incl_old, mean_old, prior, scale)
        last = pl.pallas_call(
            functools.partial(effect_kernel, total, piece * part),
            in_specs=after(last, args),
            out_shape=jax.ShapeDtypeStruct((part, cols), bf16),
            compiler_params=params,
            cost_estimate=light,
            name="effect",
        )(last, *args)
        effects.append(last)

    def update(piece, outs, before):
        rows = pl.BlockSpec((part, cols), lambda i, piece=piece: (piece, 0))
        return pl.pallas_call(
            functools.partial(update_kernel, total, piece * part),
            grid=(1,),
            in_specs=[anywhere, full((cols, block))]
            + [full(got[way, piece].shape) for way in range(2)]
            + [rows] * 2
            + [full((1, cols))] * 2
            + [anywhere] * len(outs),
            out_specs=[rows, rows, full((8, LANES))],
            out_shape=[jax.ShapeDtypeStruct((block, cols), f32)] * 2
            + [jax.ShapeDtypeStruct((8, LANES), f32)],
            input_output_aliases={8: 0, 9: 1} if outs else {},
            compiler_params=params,
            cost_estimate=small,
            name="update",
        )(before, near, got[0, piece], got[1, piece], incl_old, mean_old, prior, scale, *outs)

    eta_shape = jax.ShapeDtypeStruct((people, cols), f32)
    def product(found, eta, before, cost):
        args, places = list(eta), []
        for d, low, effect in reversed(found):
            piece = low // part
            there = (peer_far[piece], 0, piece * part) if d == reach else peer[d]
            args = [effect, genotype, there[0]] + args
            places = [((d, *there[1:]), low)] + places
        return pl.pallas_call(
            functools.partial(eta_kernel, ring, places, not eta),
            in_specs=after(before, args),
            out_shape=[eta_shape] * 2,
            compiler_params=params,
            cost_estimate=cost,
            name="add_eta",
        )(before, *args)

    eta = product([(0, piece * part, effects[piece]) for piece in range(pieces)], (), last, small)
    last = eta[0]
    held = {(way, piece): effects[piece] for way in range(2) for piece in range(pieces)}
    etas = [eta[0]]
    outs, updated, final = (), 0, []
    for hop in range(1, reach + 1):
        for piece in range(pieces):
            for way in (1, 0):
                message = held[way, piece]
                perm = left if way else right
                d, low = (hop if way else size - hop), piece * part
                if hop > 1:
                    message, _ = lax.optimization_barrier((message, etas[-2 * pieces - 1]))
                near_half = way * (part // 2)
                halved = message.shape[0] != part
                if hop == reach:
                    if not halved:
                        message = message[near_half : near_half + part // 2]
                    held[way, piece] = lax.ppermute(message, "ind", perm)
                    found = [(d, low + near_half, held[way, piece])]
                elif hop == reach - 1 and piece == pieces - 1:
                    far_half = part // 2 - near_half
                    first = message[near_half : near_half + part // 2]
                    first = held[way, piece] = lax.ppermute(first, "ind", perm)
                    message, _ = lax.optimization_barrier((message, etas[-2 * pieces]))
                    second = message[far_half : far_half + part // 2]
                    second = lax.ppermute(second, "ind", perm)
                    found = [(d, low + near_half, first), (d, low + far_half, second)]
                else:
                    held[way, piece] = lax.ppermute(message, "ind", perm)
                    found = [(d, low, held[way, piece])]
                if hop == reach and piece == pieces - 1:
                    final += found
                    continue
                eta = product(found, eta, last, small if len(etas) == 1 or (hop, piece) >= (reach - 1, pieces - 1) else light)
                last = eta[0]
                etas.append(last)
        if updated < pieces and hop < reach:
            *outs, last = update(updated, outs, last)
            updated += 1
    while updated < pieces:
        *outs, last = update(updated, outs, last)
        updated += 1

    half = people // 2
    eta_got = [lax.ppermute(eta[1][k : k + half], "ind", swap) for k in (0, half)]
    others = [lax.ppermute(effect, "ind", swap) for _, _, effect in final]
    mine = pl.pallas_call(
        functools.partial(own_kernel, ring, [(d, low, False) for d, low, _ in final]),
        out_shape=eta_shape,
        compiler_params=params,
        cost_estimate=heavy,
        name="own_last",
    )(genotype, eta[0], offset.reshape(1, cols), *[effect for _, _, effect in final])
    there = [(d, low, True) for d, low, _ in final]
    mine = pl.pallas_call(
        functools.partial(other_kernel, ring, there[:1]),
        out_shape=eta_shape,
        compiler_params=params,
        cost_estimate=heavy,
        name="other_last",
    )(genotype, mine, *eta_got, others[0])
    resid_new = pl.pallas_call(
        functools.partial(end_kernel, ring, there[1:]),
        out_shape=eta_shape,
        compiler_params=params,
        cost_estimate=light,
        name="new_residual",
    )(genotype, mine, labels, *others[1:])
    return (outs[0], outs[1], resid_new)


def solution(mesh):
    split = P(("groups", "ind"), None)
    return jax.shard_map(
        functools.partial(on_device, ring_of(mesh.devices)),
        mesh=mesh,
        in_specs=(split, split, split, split, split, P(), P(), P()),
        out_specs=(split, split, split),
        check_vma=False,
    )
```
